128 devices in a mesh: dp: 2 (over y_lo), space: 16 (over x, y_hi, core), chan: 4 (over z).
Axes of the slice: x: 4, y: 4 (y_hi: 2, y_lo: 2; y = y_hi * 2 + y_lo), z: 4, core: 2. Of those that a mesh axis runs over, the one named last changes fastest.
Arguments:
- samples: bfloat16 [2, 64, 64, 32, 256], P('dp', None, 'space', 'chan'), may hold values from -6 to 6
- early_filters: bfloat16 [27, 128, 64], replicated, may hold values from -0.15625 to 0.15625
- deep_filters: bfloat16 [27, 256, 128], P(None, 'chan'), may hold values from -0.109375 to 0.109375
- deep_cotangent: bfloat16 [2, 256, 32, 16, 128], P('dp', 'chan', 'space'), may hold values from -0.09375 to 0.09375
Outputs:
- deep_act: bfloat16 [2, 256, 32, 16, 128], P('dp', 'chan', 'space')
- deep_grad: float32 [27, 256, 128], P(None, 'chan')
- early_grad: float32 [27, 128, 64], replicated
The draws below stay inside these ranges and needn't reach their ends.
All inputs are finite; a program needn't handle non-finite values.
Results may differ from the reference program's by a relative error of at most 0.0053.
Values may be sent and summed in bfloat16 or wider, within the bound.
A program may use at most 256 MiB of HBM per device.

```python
from functools import partial
import jax
import jax.numpy as jnp
from jax import lax

C1 = 64
C2 = 128
C3 = 256
NZ = 256
SAMPLES = 2
NX = 64
NY = 32


def levels(key, shape, shards, smallest, largest):
    factor_of, own = 1.0, jax.random.fold_in(key, 6)
    for axis_at, shards_of in shards:
        draws = jnp.exp(jax.random.uniform(jax.random.fold_in(own, axis_at), (shards_of,), jnp.float32, smallest / len(shards), largest / len(shards)))
        factor_of = factor_of * jnp.repeat(draws, shape[axis_at] // shards_of).reshape([-1 if axis == axis_at else 1 for axis in range(len(shape))])
    return factor_of


def gaussian(key, extent, width, bound, split=(), held_as=jnp.bfloat16):
    drawn = jax.random.normal(key, extent, jnp.float32) * width
    if len(split) > 0:
        drawn = levels(key, extent, split, -0.22, 0.18) * drawn
    return jnp.clip(drawn, min=-bound, max=bound).astype(held_as)


def setup_inputs(seed: int = 0) -> dict:
    splits = jax.random.split(jax.random.key(seed), 5)
    samples = gaussian(splits[0], (SAMPLES, C1, NX, NY, NZ), 1.0, 6.0, ((0, 2), (2, 16), (3, 4)))
    early_filters = gaussian(splits[1], (27, C2, C1), (27 * C1) ** -0.5, 0.15625)
    deep_filters = gaussian(splits[2], (27, C3, C2), (27 * C2) ** -0.5, 0.109375, ((1, 4),))
    deep_cotangent = gaussian(splits[3], (SAMPLES, C3, NX // 2, NY // 2, NZ // 2), 0.015625, 0.09375, ((0, 2), (1, 4), (2, 16)))
    return {"samples": samples, "early_filters": early_filters, "deep_filters": deep_filters, "deep_cotangent": deep_cotangent}


def convolve(field, filters):
    kernel = filters.reshape(3, 3, 3, filters.shape[1], filters.shape[2]).transpose(3, 4, 0, 1, 2)
    return lax.conv_general_dilated(field, kernel, (1, 1, 1), ((1, 1), (1, 1), (1, 1)), dimension_numbers=('NCDHW', 'OIDHW', 'NCDHW'), precision=lax.Precision.HIGHEST)

def slope(values):
    gate = jax.nn.sigmoid(values)
    return gate * (1.0 + values * (1.0 - gate))

def reference(samples, early_filters, deep_filters, deep_cotangent):
    wide_samples = samples.astype(jnp.float32)
    early_wide = early_filters.astype(jnp.float32)
    deep_wide = deep_filters.astype(jnp.float32)
    pre_early, early_vjp = jax.vjp(partial(convolve, wide_samples), early_wide)
    active = jax.nn.silu(pre_early)
    shape_in = active.shape
    blocks = active.reshape(shape_in[0], shape_in[1], shape_in[2] // 2, 2, shape_in[3] // 2, 2, shape_in[4] // 2, 2)
    pooled = (lax.optimization_barrier(jnp.sum(blocks, axis=(3, 5, 7))) * 0.125).astype(jnp.bfloat16)
    pre_deep, deep_vjp = jax.vjp(convolve, pooled.astype(jnp.float32), deep_wide)
    deep_act = jax.nn.silu(pre_deep).astype(jnp.bfloat16)
    deep_in = (deep_cotangent.astype(jnp.float32) * slope(pre_deep)).astype(jnp.bfloat16)
    pooled_grad, deep_grad = deep_vjp(deep_in.astype(jnp.float32))
    small = pooled_grad.shape
    spread = jnp.broadcast_to(pooled_grad.reshape(small[0], small[1], small[2], 1, small[3], 1, small[4], 1), (small[0], small[1], small[2], 2, small[3], 2, small[4], 2)).reshape(shape_in) * 0.125
    early_in = (spread * slope(pre_early)).astype(jnp.bfloat16)
    early_grad = early_vjp(early_in.astype(jnp.float32))[0]
    return (deep_act, deep_grad, early_grad)
```

```python
import jax
import jax.numpy as jnp
from jax import lax
from jax.experimental import pallas as pl
from jax.experimental.pallas import tpu as pltpu
from jax.sharding import PartitionSpec as P

BF16 = jnp.bfloat16
F32 = jnp.float32
MESH = pl.DeviceIdType.MESH

SIDES = [(dx, dy) for dx in (-1, 0, 1) for dy in (-1, 0, 1) if (dx, dy) != (0, 0)]


def dot(a, b):
    return lax.dot_general(a, b, (((1,), (0,)), ((), ())), preferred_element_type=F32)


def dot_nt(a, b):
    return lax.dot_general(a, b, (((1,), (1,)), ((), ())), preferred_element_type=F32)


def selector(rows, cols, hit):
    row = lax.broadcasted_iota(jnp.int32, (rows, cols), 0)
    col = lax.broadcasted_iota(jnp.int32, (rows, cols), 1)
    return jnp.where(hit(row, col), 1.0, 0.0).astype(BF16)


def sigmoid(u):
    return 0.5 + 0.5 * jnp.tanh(0.5 * u)


def sent_and_landed(side, length):
    if side == 0:
        return (1, length), (1, length)
    if side == 1:
        return (length, 1), (0, 1)
    return (1, 1), (length + 1, 1)


def build_early_weights(ef, w9):
    places = [selector(64, 256, lambda r, c, s=s: c == r + 64 * s) for s in range(4)]

    def body(ae, carry):
        for p in range(2):
            w9[ae, p * 128 : (p + 1) * 128, :] = sum(dot(ef[3 * ae + f], places[f + p]) for f in range(3)).astype(BF16)
        return carry

    lax.fori_loop(0, 9, body, 0)


def place_taps(block, spread, taps_in, x, first_y, count):
    wide = dot(block, spread[...]).astype(BF16)
    for y in range(count):
        for s in range(4):
            taps_in[x, s * 64 : (s + 1) * 64, pl.ds((first_y + y) * 128, 128)] = wide[
                y * 64 : (y + 1) * 64, s * 128 : (s + 1) * 128
            ]


def early_forward(taps_in, w9, slopes, pooled):
    def body(i, carry):
        X, Y = i // 4, i % 4
        total = None
        for dx in range(2):
            x = 2 * X + dx
            pre = None
            for a in range(3):
                for e in range(3):
                    lanes = pl.ds(pl.multiple_of((2 * Y + e) * 128, 128), 256)
                    term = dot(w9[3 * a + e], taps_in[x + a, :, lanes])
                    pre = term if pre is None else pre + term
            s = sigmoid(pre)
            slopes[x, :, pl.ds(pl.multiple_of(Y * 256, 256), 256)] = s * (1.0 + pre * (1.0 - s))
            act = pre * s
            act = act[:128] + act[128:]
            act = act[:, :128] + act[:, 128:]
            total = act if total is None else total + act
        pooled[X + 1, 128:256, pl.ds(pl.multiple_of((Y + 1) * 128, 128), 128)] = (total * 0.125).astype(BF16)
        return carry

    lax.fori_loop(0, 8, body, 0)


def shift_pooled(pooled):
    shifts = selector(128, 256, lambda r, c: r == jnp.where(c < 128, c - 1, c - 127))

    def body(i, carry):
        x = i // 6
        lanes = pl.ds(pl.multiple_of((i % 6) * 128, 128), 128)
        both = dot(pooled[x, 128:256, lanes], shifts).astype(BF16)
        pooled[x, 0:128, lanes] = both[:, :128]
        pooled[x, 256:384, lanes] = both[:, 128:]
        return carry

    lax.fori_loop(0, 24, body, 0)


def transpose_deep_weights(wd, wdt):
    eye = selector(128, 128, lambda r, c: r == c)

    def body(ae, carry):
        for f in range(3):
            wdt[ae, f * 128 : (f + 1) * 128, :] = dot_nt(eye, wd[ae, :, f * 128 : (f + 1) * 128]).astype(BF16)
        return carry

    lax.fori_loop(0, 9, body, 0)


def deep_forward(pooled, wd, ct, act_out, deep_in):
    def body(i, carry):
        X, h = i // 2, i % 2
        pre = None
        for a in range(3):
            for e in range(3):
                lanes = pl.ds(pl.multiple_of(h * 256 + e * 128, 128), 256)
                term = dot(wd[3 * a + e], pooled[X + a, :, lanes])
                pre = term if pre is None else pre + term
        s = sigmoid(pre)
        own = pl.ds(pl.multiple_of(h * 256, 256), 256)
        act_out[X, :, own] = (pre * s).astype(BF16)
        slope = s * (1.0 + pre * (1.0 - s))
        lanes = pl.ds(pl.multiple_of(h * 256 + 128, 128), 256)
        deep_in[X + 1, :, lanes] = (ct[X, :, own].astype(F32) * slope).astype(BF16)
        return carry

    lax.fori_loop(0, 4, body, 0)


def deep_gradient(deep_in, pooled, out):
    def body(i, carry):
        a, e = i // 3, i % 3
        lanes = pl.ds(pl.multiple_of(e * 128, 128), 512)
        total = None
        for X in range(2):
            term = dot_nt(deep_in[X + 1, :, 128:640], pooled[X + a, :, lanes])
            total = term if total is None else total + term
        out[i] = total.astype(BF16)
        return carry

    lax.fori_loop(0, 9, body, 0)


def early_cotangent(deep_in, wdt, slopes, early_in):
    column = lax.broadcasted_iota(jnp.int32, (128, 128), 1)

    def body(i, carry):
        X, h = i // 2, i % 2
        total = None
        for a in range(3):
            for e in range(3):
                lanes = pl.ds(pl.multiple_of(h * 256 + (2 - e) * 128, 128), 256)
                term = dot(wdt[3 * a + e], deep_in[X + 2 - a, :, lanes])
                total = term if total is None else total + term
        for k in range(2):
            part = total[:, k * 128 : (k + 1) * 128]
            grad = part[128:256]
            grad += jnp.where(column < 127, pltpu.roll(part[0:128], 127, 1), 0.0)
            grad += jnp.where(column > 0, pltpu.roll(part[256:384], 1, 1), 0.0)
            grad *= 0.125
            for dx in range(2):
                for dy in range(2):
                    lanes = pl.ds(pl.multiple_of((4 * h + 2 * k + dy) * 128, 128), 128)
                    for p in range(2):
                        rows = slice(p * 128, (p + 1) * 128)
                        early_in[2 * X + dx, rows, lanes] = (grad * slopes[2 * X + dx, rows, lanes]).astype(BF16)
        return carry

    lax.fori_loop(0, 4, body, 0)


def early_gradient(early_in, taps_in, out):
    def body(i, carry):
        a, e = i // 3, i % 3
        lanes = pl.ds(pl.multiple_of(e * 128, 128), 1024)
        total = None
        for x in range(4):
            term = dot_nt(early_in[x], taps_in[x + a, :, lanes])
            total = term if total is None else total + term
        out[i] = (total[:128] + pltpu.roll(total[128:], 192, 1)).astype(BF16)
        return carry

    lax.fori_loop(0, 9, body, 0)


def kernel(
    samples, ef, wd_own, ct_own,
    act_out, dg_out, eg_out,
    sample_ext, taps_in, w9, spread, slopes, pooled, wd, wdt, ct, act, deep_in, early_in,
    dg, dg_a, dg_s, dg_b, dg_full, eg, eg_a, eg_s, eg_b, eg_full,
    halo_send, halo_recv, chan_send, chan_recv, a_send, a_recv, b_send, b_recv,
):
    dp, space, chan = lax.axis_index("dp"), lax.axis_index("space"), lax.axis_index("chan")
    core, chip_row = space % 2, space // 2
    rank_a = chan * 2 + core
    rank_b = chip_row * 2 + dp

    def side_device(dx, dy):
        return {"dp": dp, "space": (space + dx + 16) % 16, "chan": (chan + dy + 4) % 4}

    def chan_device(j):
        return {"dp": dp, "space": space, "chan": (chan + j) % 4}

    def a_device(j):
        r = (rank_a + j) % 8
        return {"dp": dp, "space": chip_row * 2 + r % 2, "chan": r // 2}

    def b_device(j):
        r = (rank_b + j) % 16
        return {"dp": r % 2, "space": (r // 2) * 2 + core, "chan": chan}

    barrier = pltpu.get_barrier_semaphore()
    peers = [side_device(dx, dy) for dx, dy in SIDES]
    peers += [a_device(j) for j in range(1, 8)] + [b_device(j) for j in range(1, 16)]
    for peer in peers:
        pl.semaphore_signal(barrier, inc=1, device_id=peer, device_id_type=MESH)

    build_early_weights(ef, w9)
    spread[...] = selector(256, 512, lambda r, c: r == 2 * (c % 128) + c // 128 - 1)

    pl.semaphore_wait(barrier, len(peers))

    sends = []

    def remote(src, dst, send_sem, recv_sem, device):
        copy = pltpu.make_async_remote_copy(
            src_ref=src, dst_ref=dst, send_sem=send_sem, recv_sem=recv_sem, device_id=device, device_id_type=MESH
        )
        copy.start()
        sends.append(copy)
        return copy

    def halo(n, view):
        copies = []
        for k, (dx, dy) in enumerate(SIDES):
            src, dst = view(dx, dy)
            copies.append(remote(src, dst, halo_send.at[n, k], halo_recv.at[n, k], side_device(dx, dy)))
        return copies

    def sample_view(dx, dy):
        (sx, nx), (tx, _) = sent_and_landed(dx, 4)
        (sy, ny), (ty, _) = sent_and_landed(dy, 8)
        src = samples.at[pl.ds(sx - 1, nx), pl.ds(sy - 1, ny)]
        return src, sample_ext.at[pl.ds(tx, nx), pl.ds(ty, ny)]

    def field_view(ref, first, rows):
        def view(dx, dy):
            (sx, nx), (tx, _) = sent_and_landed(dx, 2)
            (sy, ny), (ty, _) = sent_and_landed(dy, 4)
            block = pl.ds(first, rows)
            src = ref.at[pl.ds(sx, nx), block, pl.ds(sy * 128, ny * 128)]
            return src, ref.at[pl.ds(tx, nx), block, pl.ds(ty * 128, ny * 128)]

        return view

    def clear_outside(ref, rows, lanes):
        last, width = ref.shape[0] - 1, ref.shape[2]

        def clear(x, span):
            ref[x, rows, span] = jnp.zeros((rows.stop - rows.start, span.stop - span.start), BF16)

        @pl.when(space == 0)
        def _():
            clear(0, slice(0, width))

        @pl.when(space == 15)
        def _():
            clear(last, slice(0, width))

        @pl.when(chan == 0)
        def _():
            for x in range(last + 1):
                clear(x, slice(0, lanes))

        @pl.when(chan == 3)
        def _():
            for x in range(last + 1):
                clear(x, slice(width - lanes, width))

    sample_halo = halo(0, sample_view)
    wd_copies, ct_copies = [], []
    mine = pl.ds(pl.multiple_of(chan * 64, 64), 64)
    for j in (1, 2, 3):
        wd_copies.append(remote(wd_own, wd.at[:, mine, :], chan_send.at[0, j], chan_recv.at[0, j], chan_device(j)))
    for j in (1, 2, 3):
        theirs = pl.ds(pl.multiple_of((chan + j) % 4 * 512, 512), 512)
        ct_copies.append(
            remote(ct_own.at[:, :, theirs], ct.at[:, mine, :], chan_send.at[1, j], chan_recv.at[1, j], chan_device(j))
        )
    wd[:, mine, :] = wd_own[...]
    ct[:, mine, :] = ct_own[:, :, pl.ds(pl.multiple_of(chan * 512, 512), 512)]

    for x in range(4):
        place_taps(samples[x].reshape(512, 256), spread, taps_in, x + 1, 1, 8)
    for copy in sample_halo:
        copy.wait_recv()
    for x in (0, 5):
        place_taps(sample_ext[x].reshape(640, 256), spread, taps_in, x, 0, 10)
    for y in (0, 9):
        for x in range(1, 5):
            place_taps(sample_ext[x, y], spread, taps_in, x, y, 1)
    clear_outside(taps_in, slice(0, 256), 128)

    early_forward(taps_in, w9, slopes, pooled)
    pooled_halo = halo(1, field_view(pooled, 128, 128))
    for copy in wd_copies + ct_copies:
        copy.wait_recv()
    transpose_deep_weights(wd, wdt)
    for copy in pooled_halo:
        copy.wait_recv()
    clear_outside(pooled, slice(128, 256), 128)
    shift_pooled(pooled)

    deep_forward(pooled, wd, ct, act, deep_in)
    deep_halo = halo(2, field_view(deep_in, 0, 256))
    act_copies = []
    here = pl.ds(pl.multiple_of(chan * 512, 512), 512)
    for j in (1, 2, 3):
        theirs = pl.ds(pl.multiple_of((chan + j) % 4 * 64, 64), 64)
        act_copies.append(
            remote(act.at[:, theirs, :], act_out.at[:, :, here], chan_send.at[2, j], chan_recv.at[2, j], chan_device(j))
        )
    act_out[:, :, here] = act[:, mine, :]

    deep_gradient(deep_in, pooled, dg)

    def reduce_a(n, src, dst, rows):
        copies = []
        for j in range(1, 8):
            theirs = pl.ds(pl.multiple_of((rank_a + j) % 8 * rows, rows), rows)
            copies.append(remote(src.at[:, theirs, :], dst.at[j], a_send.at[n, j], a_recv.at[n, j], a_device(j)))
        return copies

    def sum_a(src, dst, out, rows):
        own = pl.ds(pl.multiple_of(rank_a * rows, rows), rows)

        def body(ae, carry):
            total = src[ae, own, :].astype(F32)
            for j in range(1, 8):
                total += dst[j, ae].astype(F32)
            out[ae] = total.astype(BF16)
            return carry

        lax.fori_loop(0, 9, body, 0)

    conditional = []

    def remote_if(pred, src, dst, send_sem, recv_sem, device):
        copy = pltpu.make_async_remote_copy(
            src_ref=src, dst_ref=dst, send_sem=send_sem, recv_sem=recv_sem, device_id=device, device_id_type=MESH
        )

        @pl.when(pred)
        def _():
            copy.start()

        conditional.append((pred, copy))

    def reduce_b(n, src, dst):
        for j in range(1, 16):
            r = (rank_b + j) % 16
            row = jnp.minimum(r, 8)
            remote_if(r < 9, src.at[row], dst.at[j], b_send.at[n, j], b_recv.at[n, j], b_device(j))

    def sum_and_spread_b(n, src, dst, full, rows, first):
        own = pl.ds(first, rows)

        @pl.when(rank_b < 9)
        def _():
            total = src[rank_b].astype(F32)
            for j in range(1, 16):
                pltpu.make_async_remote_copy(
                    src_ref=src.at[0], dst_ref=dst.at[j], send_sem=b_send.at[n, j], recv_sem=b_recv.at[n, j],
                    device_id=b_device(j), device_id_type=MESH,
                ).wait_recv()
            for j in range(1, 16):
                total += dst[j].astype(F32)
            full[rank_b, own, :] = total.astype(BF16)

        block = full.at[jnp.minimum(rank_b, 8), own, :]
        for j in range(1, 16):
            remote_if(rank_b < 9, block, block, b_send.at[n + 2, j], b_recv.at[n + 2, j], b_device(j))

    def landed_b(n, full, rows, first):
        for j in range(1, 16):
            r = (rank_b - j + 16) % 16
            block = full.at[jnp.minimum(r, 8), pl.ds(first, rows), :]

            @pl.when(r < 9)
            def _():
                pltpu.make_async_remote_copy(
                    src_ref=block, dst_ref=block, send_sem=b_send.at[n + 2, j], recv_sem=b_recv.at[n + 2, j],
                    device_id=b_device(j), device_id_type=MESH,
                ).wait_recv()

    for copy in deep_halo:
        copy.wait_recv()
    dg_copies = reduce_a(0, dg, dg_a, 32)
    clear_outside(deep_in, slice(0, 256), 128)
    early_cotangent(deep_in, wdt, slopes, early_in)
    early_gradient(early_in, taps_in, eg)
    eg_copies = reduce_a(1, eg, eg_a, 16)

    for copy in dg_copies:
        copy.wait_recv()
    sum_a(dg, dg_a, dg_s, 32)
    reduce_b(0, dg_s, dg_b)
    for copy in eg_copies:
        copy.wait_recv()
    sum_a(eg, eg_a, eg_s, 16)
    reduce_b(1, eg_s, eg_b)
    dg_first = pl.multiple_of(core * 32, 32)
    eg_first = pl.multiple_of(rank_a * 16, 16)
    sum_and_spread_b(0, dg_s, dg_b, dg_full, 32, dg_first)
    sum_and_spread_b(1, eg_s, eg_b, eg_full, 16, eg_first)
    landed_b(0, dg_full, 32, dg_first)
    half = dg_full.at[:, pl.ds(dg_first, 32), :]
    sibling = {"dp": dp, "space": chip_row * 2 + 1 - core, "chan": chan}
    dg_pair = remote(half, half, a_send.at[2, 0], a_recv.at[2, 0], sibling)
    landed_b(1, eg_full, 16, eg_first)
    eg_last = []
    block = eg_full.at[:, pl.ds(eg_first, 16), :]
    for j in range(1, 8):
        eg_last.append(remote(block, block, a_send.at[2, j], a_recv.at[2, j], a_device(j)))

    other = dg_full.at[:, pl.ds(pl.multiple_of(32 - core * 32, 32), 32), :]
    pltpu.make_async_remote_copy(
        src_ref=half, dst_ref=other, send_sem=a_send.at[2, 0], recv_sem=a_recv.at[2, 0], device_id=sibling,
        device_id_type=MESH,
    ).wait_recv()
    for ae in range(9):
        for f in range(3):
            dg_out[3 * ae + f] = dg_full[ae, :, f * 128 : (f + 1) * 128].astype(F32)
    for j in range(1, 8):
        r = (rank_a - j + 8) % 8
        theirs = eg_full.at[:, pl.ds(pl.multiple_of(r * 16, 16), 16), :]
        pltpu.make_async_remote_copy(
            src_ref=block, dst_ref=theirs, send_sem=a_send.at[2, j], recv_sem=a_recv.at[2, j], device_id=a_device(j),
            device_id_type=MESH,
        ).wait_recv()
    for ae in range(9):
        for f in range(3):
            eg_out[3 * ae + f] = eg_full[ae, :, f * 64 : (f + 1) * 64].astype(F32)

    for copy in act_copies:
        copy.wait_recv()
    for copy in sends:
        copy.wait_send()
    for pred, copy in conditional:

        @pl.when(pred)
        def _():
            copy.wait_send()


def on_device(samples, early_filters, deep_filters, deep_cotangent):
    samples = samples[0].transpose(1, 2, 0, 3)
    deep_filters = deep_filters.reshape(9, 3, 64, 128).transpose(0, 2, 1, 3).reshape(9, 64, 384)
    deep_cotangent = deep_cotangent[0].transpose(1, 0, 2, 3).reshape(2, 64, 2048)
    act, deep_grad, early_grad = pl.pallas_call(
        kernel,
        out_shape=(
            jax.ShapeDtypeStruct((2, 64, 2048), BF16),
            jax.ShapeDtypeStruct((27, 64, 128), F32),
            jax.ShapeDtypeStruct((27, 128, 64), F32),
        ),
        in_specs=[pl.BlockSpec(memory_space=pltpu.VMEM)] * 4,
        out_specs=[pl.BlockSpec(memory_space=pltpu.VMEM)] * 3,
        scratch_shapes=[
            pltpu.VMEM((6, 10, 64, 256), BF16),
            pltpu.VMEM((6, 256, 1280), BF16),
            pltpu.VMEM((9, 256, 256), BF16),
            pltpu.VMEM((256, 512), BF16),
            pltpu.VMEM((4, 256, 1024), F32),
            pltpu.VMEM((4, 384, 768), BF16),
            pltpu.VMEM((9, 256, 384), BF16),
            pltpu.VMEM((9, 384, 256), BF16),
            pltpu.VMEM((2, 256, 512), BF16),
            pltpu.VMEM((2, 256, 512), BF16),
            pltpu.VMEM((4, 256, 768), BF16),
            pltpu.VMEM((4, 256, 1024), BF16),
            pltpu.VMEM((9, 256, 384), BF16),
            pltpu.VMEM((8, 9, 32, 384), BF16),
            pltpu.VMEM((9, 32, 384), BF16),
            pltpu.VMEM((16, 32, 384), BF16),
            pltpu.VMEM((9, 64, 384), BF16),
            pltpu.VMEM((9, 128, 256), BF16),
            pltpu.VMEM((8, 9, 16, 256), BF16),
            pltpu.VMEM((9, 16, 256), BF16),
            pltpu.VMEM((16, 16, 256), BF16),
            pltpu.VMEM((9, 128, 256), BF16),
            pltpu.SemaphoreType.DMA((3, 8)),
            pltpu.SemaphoreType.DMA((3, 8)),
            pltpu.SemaphoreType.DMA((3, 4)),
            pltpu.SemaphoreType.DMA((3, 4)),
            pltpu.SemaphoreType.DMA((3, 8)),
            pltpu.SemaphoreType.DMA((3, 8)),
            pltpu.SemaphoreType.DMA((4, 16)),
            pltpu.SemaphoreType.DMA((4, 16)),
        ],
        compiler_params=pltpu.CompilerParams(
            collective_id=0, has_side_effects=True, vmem_limit_bytes=56 * 1024 * 1024
        ),
        name="conv_step",
    )(samples, early_filters, deep_filters, deep_cotangent)
    act = act.reshape(2, 64, 16, 128).transpose(1, 0, 2, 3)[None]
    return act, deep_grad, early_grad


def solution(mesh):
    placed = (
        P("dp", None, "space", "chan", None),
        P(),
        P(None, "chan", None),
        P("dp", "chan", "space", None, None),
    )
    return jax.shard_map(
        on_device,
        mesh=mesh,
        in_specs=placed,
        out_specs=(P("dp", "chan", "space", None, None), P(None, "chan", None), P()),
        check_vma=False,
    )
```

```python
import jax
import jax.numpy as jnp
from jax import lax
from jax.experimental import pallas as pl
from jax.experimental.pallas import tpu as pltpu
from jax.sharding import PartitionSpec as P

BF16 = jnp.bfloat16
F32 = jnp.float32
MESH = pl.DeviceIdType.MESH

SIDES = [(dx, dy) for dx in (-1, 0, 1) for dy in (-1, 0, 1) if (dx, dy) != (0, 0)]


def dot(a, b):
    return lax.dot_general(a, b, (((1,), (0,)), ((), ())), preferred_element_type=F32)


def dot_nt(a, b):
    return lax.dot_general(a, b, (((1,), (1,)), ((), ())), preferred_element_type=F32)


def selector(rows, cols, hit):
    row = lax.broadcasted_iota(jnp.int32, (rows, cols), 0)
    col = lax.broadcasted_iota(jnp.int32, (rows, cols), 1)
    return jnp.where(hit(row, col), 1.0, 0.0).astype(BF16)


def sigmoid(u):
    return 0.5 + 0.5 * jnp.tanh(0.5 * u)


def sent_and_landed(side, length):
    if side == 0:
        return (1, length), (1, length)
    if side == 1:
        return (length, 1), (0, 1)
    return (1, 1), (length + 1, 1)


def build_early_weights(ef, w9):
    eye = selector(128, 128, lambda r, c: r == c)
    none = jnp.zeros((64, 128), BF16)

    def body(ae, carry):
        taps = [ef[3 * ae + f] for f in range(3)]
        for p in range(2):
            slots = [none] + taps if p else taps + [none]
            w9[ae, p * 128 : (p + 1) * 128, :] = dot_nt(eye, jnp.concatenate(slots, axis=0)).astype(BF16)
        return carry

    lax.fori_loop(0, 9, body, 0)


def place_taps(block, spread, taps_in, x, first_y, count):
    wide = dot(block, spread[...]).astype(BF16)
    for y in range(count):
        for s in range(4):
            taps_in[x, s * 64 : (s + 1) * 64, pl.ds((first_y + y) * 128, 128)] = wide[
                y * 64 : (y + 1) * 64, s * 128 : (s + 1) * 128
            ]


def early_terms(taps_in, w9, x, Y, shifts):
    total = None
    for a in shifts:
        for e in range(3):
            lanes = pl.ds(pl.multiple_of((2 * Y + e) * 128, 128), 256)
            term = dot(w9[3 * a + e], taps_in[x + a, :, lanes])
            total = term if total is None else total + term
    return total


def early_activation(pre, slopes, x, Y):
    s = sigmoid(pre)
    slopes[x, :, pl.ds(pl.multiple_of(Y * 256, 256), 256)] = s * (1.0 + pre * (1.0 - s))
    act = pre * s
    act = act[:128] + act[128:]
    return act[:, :128] + act[:, 128:]


def early_inner(taps_in, w9, slopes, pool_sum):
    def body(Y, carry):
        own = pl.ds(pl.multiple_of(Y * 256, 256), 256)
        for x, shifts in ((0, (1, 2)), (3, (0, 1))):
            slopes[x, :, own] = early_terms(taps_in, w9, x, Y, shifts)
        for X, x in enumerate((1, 2)):
            pre = early_terms(taps_in, w9, x, Y, (0, 1, 2))
            pool_sum[X, :, pl.ds(pl.multiple_of(Y * 128, 128), 128)] = early_activation(pre, slopes, x, Y)
        return carry

    lax.fori_loop(0, 4, body, 0)


def early_outer(taps_in, w9, slopes, pool_sum, pooled):
    for Y in range(4):
        for X, x, a in ((0, 0, 0), (1, 3, 2)):
            pre = slopes[x, :, Y * 256 : (Y + 1) * 256] + early_terms(taps_in, w9, x, Y, (a,))
            total = pool_sum[X, :, Y * 128 : (Y + 1) * 128] + early_activation(pre, slopes, x, Y)
            pooled[X + 1, 128:256, (Y + 1) * 128 : (Y + 2) * 128] = (total * 0.125).astype(BF16)


def shift_pooled(pooled, xs, first, count):
    shifts = selector(128, 256, lambda r, c: r == jnp.where(c < 128, c - 1, c - 127))
    for x in xs:
        blocks = [pooled[x, 128:256, (first + y) * 128 : (first + y + 1) * 128] for y in range(count)]
        both = dot(jnp.concatenate(blocks, axis=0), shifts).astype(BF16)
        for y in range(count):
            lanes = slice((first + y) * 128, (first + y + 1) * 128)
            rows = slice(y * 128, (y + 1) * 128)
            pooled[x, 0:128, lanes] = both[rows, :128]
            pooled[x, 256:384, lanes] = both[rows, 128:]


def transpose_deep_weights(wd, wdt):
    eye = selector(128, 128, lambda r, c: r == c)

    def body(i, carry):
        for ae in range(3):
            for f in range(3):
                rows = slice(f * 128, (f + 1) * 128)
                wdt[3 * i + ae, rows, :] = dot_nt(eye, wd[9 * i + 3 * ae + f]).astype(BF16)
        return carry

    lax.fori_loop(0, 3, body, 0)


def deep_terms(pooled, wd, X, h, shifts):
    total = None
    for a in shifts:
        for e in range(3):
            weights = jnp.concatenate([wd[9 * a + 3 * e + f] for f in range(3)], axis=1)
            term = dot(weights, pooled[X + a, :, h * 256 + e * 128 : h * 256 + e * 128 + 256])
            total = term if total is None else total + term
    return total


def deep_inner(pooled, wd, pre_deep):
    for h in range(2):
        for X, shifts in ((0, (1, 2)), (1, (0, 1))):
            pre_deep[X, :, h * 256 : (h + 1) * 256] = deep_terms(pooled, wd, X, h, shifts)


def deep_outer(pooled, wd, ct, pre_deep, act, deep_in):
    for X, a in ((0, 0), (1, 2)):
        for h in range(2):
            pre = pre_deep[X, :, h * 256 : (h + 1) * 256] + deep_terms(pooled, wd, X, h, (a,))
            s = sigmoid(pre)
            value = (pre * s).astype(BF16)
            slope = s * (1.0 + pre * (1.0 - s))
            for k in range(2):
                Y, part = 2 * h + k, slice(k * 128, (k + 1) * 128)
                act[Y, X] = value[:, part]
                deep_in[X, :, (Y + 2) * 128 : (Y + 3) * 128] = (ct[Y, X].astype(F32) * slope[:, part]).astype(BF16)


def pooled_terms(deep_in, wdt, pairs, first):
    column = lax.broadcasted_iota(jnp.int32, (128, 128), 1)
    total = None
    for X, a in pairs:
        for e in range(3):
            lanes = slice((first + 2 - e) * 128, (first + 4 - e) * 128)
            term = dot(wdt[3 * a + e], deep_in[X, :, lanes])
            total = term if total is None else total + term
    parts = []
    for k in range(2):
        part = total[:, k * 128 : (k + 1) * 128]
        grad = part[128:256]
        grad += jnp.where(column < 127, pltpu.roll(part[0:128], 127, 1), 0.0)
        grad += jnp.where(column > 0, pltpu.roll(part[256:384], 1, 1), 0.0)
        parts.append(grad)
    return jnp.concatenate(parts, axis=1)


def pooled_outer(deep_in, wdt, send_x):
    for n, pairs in enumerate((((0, 0),), ((1, 2),))):
        for first in (0, 2, 4):
            send_x[n, :, first * 128 : (first + 2) * 128] = pooled_terms(deep_in, wdt, pairs, first).astype(BF16)


def pooled_inner(deep_in, wdt, pooled_grad):
    for X, pairs in enumerate((((0, 1), (1, 0)), ((0, 2), (1, 1)))):
        for first in (0, 2, 4):
            pooled_grad[X, :, first * 128 : (first + 2) * 128] = pooled_terms(deep_in, wdt, pairs, first)


def early_cotangent(pooled_grad, got_x, got_y, got_xy, slopes, early_in):
    for X in range(2):
        grad = pooled_grad[X, :, 128:640] + got_x[X].astype(F32)
        for Y in range(4):
            here = grad[:, Y * 128 : (Y + 1) * 128]
            if Y in (0, 3):
                here += got_y[Y // 3, X].astype(F32) + got_xy[X, Y // 3].astype(F32)
            here *= 0.125
            for x in (2 * X, 2 * X + 1):
                for y in (2 * Y, 2 * Y + 1):
                    lanes = slice(y * 128, (y + 1) * 128)
                    for p in range(2):
                        rows = slice(p * 128, (p + 1) * 128)
                        early_in[x, rows, lanes] = (here * slopes[x, rows, lanes]).astype(BF16)


def deep_gradient(deep_in, pooled, out):
    def body(i, carry):
        a, e = i // 3, i % 3
        lanes = pl.ds(pl.multiple_of(e * 128, 128), 512)
        total = None
        for X in range(2):
            term = dot_nt(deep_in[X, :, 256:768], pooled[X + a, :, lanes])
            total = term if total is None else total + term
        for f in range(3):
            tap = total[:, f * 128 : (f + 1) * 128].astype(BF16).reshape(4, 2, 32, 128)
            for h in range(2):
                out[h, 3 * i + f] = tap[:, h]
        return carry

    lax.fori_loop(0, 9, body, 0)


def early_gradient(early_in, taps_in, out, first, last):
    def body(i, carry):
        a, e = i // 3, i % 3
        lanes = pl.ds(pl.multiple_of(e * 128, 128), 1024)
        total = None
        for x in range(4):
            term = dot_nt(taps_in[x + a, :, lanes], early_in[x])
            total = term if total is None else total + term
        total = (total[:192, :128] + total[64:, 128:]).astype(BF16)
        for f in range(3):
            for h in range(2):
                out[h, 3 * i + f] = total[f * 64 + h * 32 : f * 64 + h * 32 + 32]
        return carry

    lax.fori_loop(first, last, body, 0)


def add_taps(count, out, terms):
    def body(t, carry):
        total = None
        for term in terms:
            value = term(t).astype(F32)
            total = value if total is None else total + value
        out(t, total.astype(BF16))
        return carry

    lax.fori_loop(0, count, body, 0)


def kernel(
    samples, ef, wd_own, ct_own,
    act_out, full,
    sample_ext, taps_in, w9, spread, slopes, pool_sum, pooled, wd, wdt, ct, pre_deep, act, deep_in,
    pooled_grad, send_x, send_y, got_x, got_y, got_xy, early_in,
    dg, dg_pair, dg_sum, dg_chan, eg, eg_pair, part, part_in, eg_chan,
    halo_send, halo_recv, chan_send, chan_recv, pair_send, pair_recv, plane_send, plane_recv,
):
    dp, space, chan = lax.axis_index("dp"), lax.axis_index("space"), lax.axis_index("chan")
    core, column = space % 2, space // 2
    rank = column * 2 + dp

    def side_device(dx, dy):
        return {"dp": dp, "space": (space + dx + 16) % 16, "chan": (chan + dy + 4) % 4}

    def chan_device(j):
        return {"dp": dp, "space": space, "chan": (chan + j) % 4}

    def plane_device(j):
        r = (rank + j) % 16
        return {"dp": r % 2, "space": (r // 2) * 2 + core, "chan": chan}

    sibling = {"dp": dp, "space": column * 2 + 1 - core, "chan": chan}

    barrier = pltpu.get_barrier_semaphore()
    peers = [side_device(dx, dy) for dx, dy in SIDES]
    peers += [chan_device(2), sibling] + [plane_device(j) for j in range(1, 16)]
    for peer in peers:
        pl.semaphore_signal(barrier, inc=1, device_id=peer, device_id_type=MESH)

    build_early_weights(ef, w9)
    spread[...] = selector(256, 512, lambda r, c: r == 2 * (c % 128) + c // 128 - 1)
    part[:, 27:, :, :] = jnp.zeros((2, 5, 32, 128), BF16)
    for X in range(2):
        for lanes in (slice(0, 256), slice(768, 1024)):
            deep_in[X, :, lanes] = jnp.zeros((256, 256), BF16)

    pl.semaphore_wait(barrier, len(peers))

    sends = []

    def describe(src, dst, send_sem, recv_sem, device):
        return pltpu.make_async_remote_copy(
            src_ref=src, dst_ref=dst, send_sem=send_sem, recv_sem=recv_sem, device_id=device, device_id_type=MESH
        )

    def remote(*args):
        copy = describe(*args)
        copy.start()
        sends.append(copy)
        return copy

    def landed(copies):
        for copy in copies:
            copy.wait_recv()

    def over_chan(n, src, dst):
        return [
            remote(src((chan + j) % 4), dst(j), chan_send.at[n, j], chan_recv.at[n, j], chan_device(j)) for j in (1, 2, 3)
        ]

    def pair(n, src, dst):
        return remote(src, dst, pair_send.at[n], pair_recv.at[n], sibling)

    def halo(n, view):
        copies = {}
        for k, (dx, dy) in enumerate(SIDES):
            src, dst = view(dx, dy)
            copies[dx, dy] = remote(src, dst, halo_send.at[n, k], halo_recv.at[n, k], side_device(dx, dy))
        return [copies[0, -1], copies[0, 1]], [copy for (dx, _), copy in copies.items() if dx != 0]

    def sample_view(dx, dy):
        (sx, nx), (tx, _) = sent_and_landed(dx, 4)
        (sy, ny), (ty, _) = sent_and_landed(dy, 8)
        src = samples.at[pl.ds(sx - 1, nx), pl.ds(sy - 1, ny)]
        return src, sample_ext.at[pl.ds(tx, nx), pl.ds(ty, ny)]

    def field_view(ref, first, rows):
        def view(dx, dy):
            (sx, nx), (tx, _) = sent_and_landed(dx, 2)
            (sy, ny), (ty, _) = sent_and_landed(dy, 4)
            block = pl.ds(first, rows)
            src = ref.at[pl.ds(sx, nx), block, pl.ds(sy * 128, ny * 128)]
            return src, ref.at[pl.ds(tx, nx), block, pl.ds(ty * 128, ny * 128)]

        return view

    def clear_y(ref, xs, rows, lanes):
        width = ref.shape[2]
        for at, span in ((0, slice(0, lanes)), (3, slice(width - lanes, width))):

            @pl.when(chan == at)
            def _():
                for x in xs:
                    ref[x, rows, span] = jnp.zeros((rows.stop - rows.start, lanes), BF16)

    def clear_x(ref, rows):
        width = ref.shape[2]
        for at, x in ((0, 0), (15, ref.shape[0] - 1)):

            @pl.when(space == at)
            def _():
                ref[x, rows, :] = jnp.zeros((rows.stop - rows.start, width), BF16)

    sample_y, sample_x = halo(0, sample_view)
    for x in range(4):
        place_taps(samples[x].reshape(512, 256), spread, taps_in, x + 1, 1, 8)
    mine = pl.ds(pl.multiple_of(chan * 64, 64), 64)
    wd[:, mine, :] = wd_own[...]
    ct[:, :, mine, :] = ct_own[pl.ds(pl.multiple_of(chan * 4, 4), 4)]
    landed(sample_y)

    half = pl.ds(pl.multiple_of(core * 32, 32), 32)

    def half_of(c):
        return wd.at[:, pl.ds(pl.multiple_of(c * 64 + core * 32, 32), 32), :]

    wd_copies = over_chan(0, lambda c: wd_own.at[:, half, :], lambda j: half_of(chan))
    for y in (0, 9):
        for x in range(1, 5):
            place_taps(sample_ext[x, y], spread, taps_in, x, y, 1)
    clear_y(taps_in, range(1, 5), slice(0, 256), 128)
    early_inner(taps_in, w9, slopes, pool_sum)
    ct_copies = over_chan(
        1, lambda c: ct_own.at[pl.ds(pl.multiple_of(c * 4, 4), 4)], lambda j: ct.at[:, :, mine, :]
    )
    landed(sample_x)
    for x in (0, 5):
        place_taps(sample_ext[x].reshape(640, 256), spread, taps_in, x, 0, 10)
    clear_y(taps_in, (0, 5), slice(0, 256), 128)
    clear_x(taps_in, slice(0, 256))
    early_outer(taps_in, w9, slopes, pool_sum, pooled)

    pooled_y, pooled_x = halo(1, field_view(pooled, 128, 128))
    shift_pooled(pooled, (1, 2), 1, 4)
    wd_halves = []
    for j, copy in zip((1, 2, 3), wd_copies):
        landed([copy])
        block = half_of((chan - j + 4) % 4)
        wd_halves.append(remote(block, block, chan_send.at[2, j], chan_recv.at[2, j], sibling))
    landed(pooled_y)
    clear_y(pooled, (1, 2), slice(128, 256), 128)
    shift_pooled(pooled, (1, 2), 0, 1)
    shift_pooled(pooled, (1, 2), 5, 1)
    for j in (1, 2, 3):
        theirs = pl.ds(pl.multiple_of((chan - j + 4) % 4 * 64 + (1 - core) * 32, 32), 32)
        block = wd.at[:, theirs, :]
        describe(block, block, chan_send.at[2, j], chan_recv.at[2, j], sibling).wait_recv()
    deep_inner(pooled, wd, pre_deep)
    landed(pooled_x)
    clear_y(pooled, (0, 3), slice(128, 256), 128)
    clear_x(pooled, slice(128, 256))
    shift_pooled(pooled, (0, 3), 0, 6)
    transpose_deep_weights(wd, wdt)
    landed(ct_copies)
    deep_outer(pooled, wd, ct, pre_deep, act, deep_in)

    pooled_outer(deep_in, wdt, send_x)
    grad_copies = []
    for n, dx in enumerate((-1, 1)):
        for dy in (-1, 0, 1):
            at, count = {-1: (0, 1), 0: (1, 4), 1: (5, 1)}[dy]
            src = send_x.at[n, :, pl.ds(at * 128, count * 128)]
            dst = got_x.at[1 - n] if dy == 0 else got_xy.at[1 - n, 0 if dy > 0 else 1]
            k = SIDES.index((dx, dy))
            grad_copies.append(remote(src, dst, halo_send.at[2, k], halo_recv.at[2, k], side_device(dx, dy)))
    pooled_inner(deep_in, wdt, pooled_grad)
    for n, (dy, at) in enumerate(((-1, 0), (1, 5))):
        for X in range(2):
            send_y[n, X] = pooled_grad[X, :, at * 128 : (at + 1) * 128].astype(BF16)
        k = SIDES.index((0, dy))
        grad_copies.append(
            remote(send_y.at[n], got_y.at[1 - n], halo_send.at[2, k], halo_recv.at[2, k], side_device(0, dy))
        )

    deep_gradient(deep_in, pooled, dg)
    dg_pair_copy = pair(0, dg.at[1 - core], dg_pair)
    landed(grad_copies)
    for at, n in ((0, 0), (15, 1)):

        @pl.when(space == at)
        def _():
            got_x[n] = jnp.zeros((128, 512), BF16)
            got_xy[n] = jnp.zeros((2, 128, 128), BF16)

    for at, n in ((0, 0), (3, 1)):

        @pl.when(chan == at)
        def _():
            got_y[n] = jnp.zeros((2, 128, 128), BF16)
            for m in range(2):
                got_xy[m, n] = jnp.zeros((128, 128), BF16)

    early_cotangent(pooled_grad, got_x, got_y, got_xy, slopes, early_in)
    early_gradient(early_in, taps_in, eg, 0, 2)
    landed([dg_pair_copy])

    def put_sum(t, value):
        dg_sum[:, t] = value

    add_taps(27, put_sum, [lambda t: dg[core, t], lambda t: dg_pair[t]])
    dg_copies = over_chan(3, lambda c: dg_sum.at[c], lambda j: dg_chan.at[j])
    early_gradient(early_in, taps_in, eg, 2, 9)
    eg_pair_copy = pair(1, eg.at[1 - core], eg_pair)

    def put_part(n):
        def put(t, value):
            part[n, t] = value

        return put

    def taps_of(r):
        return pl.ds(r * 2, 2)

    own = taps_of(rank)

    def plane_scatter(n):
        copies = []
        for j in range(1, 16):
            src = part.at[n, taps_of((rank + j) % 16)]
            copies.append(remote(src, part_in.at[n, j], plane_send.at[n, j], plane_recv.at[n, j], plane_device(j)))
        return copies

    def plane_sum(n):
        summed = part[n, own].astype(F32)
        for j in range(1, 16):
            summed += part_in[n, j].astype(F32)
        return summed

    def plane_gather(n):
        block = full.at[n, own, half, :]
        for j in range(1, 16):
            remote(block, block, plane_send.at[2 + n, j], plane_recv.at[2 + n, j], plane_device(j))

    def plane_gathered(n):
        for j in range(1, 16):
            theirs = full.at[n, taps_of((rank - j + 16) % 16), half, :]
            describe(theirs, theirs, plane_send.at[2 + n, j], plane_recv.at[2 + n, j], plane_device(j)).wait_recv()

    def halves(n):
        block = full.at[n, pl.ds(0, 27), half, :]
        pair(2 + n, block, block)

    def halves_landed(n):
        block = full.at[n, pl.ds(0, 27), pl.ds(pl.multiple_of(32 - core * 32, 32), 32), :]
        describe(block, block, pair_send.at[2 + n], pair_recv.at[2 + n], sibling).wait_recv()

    landed([eg_pair_copy])
    add_taps(27, put_part(1), [lambda t: eg[core, t], lambda t: eg_pair[t]])
    eg_copies = plane_scatter(1)
    landed(dg_copies)
    add_taps(27, put_part(0), [lambda t: dg_sum[chan, t]] + [lambda t, j=j: dg_chan[j, t] for j in (1, 2, 3)])
    dg_plane = plane_scatter(0)
    here = pl.ds(pl.multiple_of(chan * 4, 4), 4)
    act_copies = over_chan(
        4, lambda c: act.at[:, :, pl.ds(pl.multiple_of(c * 64, 64), 64), :], lambda j: act_out.at[here]
    )
    act_out[here] = act[:, :, mine, :]
    landed(eg_copies)
    eg_chan[chan] = plane_sum(1)
    over_chan(5, lambda c: eg_chan.at[chan], lambda j: eg_chan.at[chan])
    landed(dg_plane)
    full[0, own, half, :] = plane_sum(0).astype(BF16)
    plane_gather(0)
    for j in (1, 2, 3):
        block = eg_chan.at[(chan - j + 4) % 4]
        describe(block, block, chan_send.at[5, j], chan_recv.at[5, j], chan_device(j)).wait_recv()
    full[1, own, half, :] = ((eg_chan[0] + eg_chan[1]) + (eg_chan[2] + eg_chan[3])).astype(BF16)
    plane_gather(1)
    plane_gathered(0)
    halves(0)
    plane_gathered(1)
    halves(1)
    halves_landed(0)
    halves_landed(1)

    landed(act_copies)
    for copy in sends:
        copy.wait_send()


def on_device(samples, early_filters, deep_filters, deep_cotangent):
    samples = samples[0].transpose(1, 2, 0, 3)
    early_filters = early_filters.transpose(0, 2, 1)
    deep_cotangent = deep_cotangent[0].transpose(2, 1, 0, 3)
    act, grads = pl.pallas_call(
        kernel,
        out_shape=(
            jax.ShapeDtypeStruct((16, 2, 64, 128), BF16),
            jax.ShapeDtypeStruct((2, 32, 64, 128), BF16),
        ),
        in_specs=[pl.BlockSpec(memory_space=pltpu.VMEM)] * 4,
        out_specs=[pl.BlockSpec(memory_space=pltpu.VMEM)] * 2,
        scratch_shapes=[
            pltpu.VMEM((6, 10, 64, 256), BF16),
            pltpu.VMEM((6, 256, 1280), BF16),
            pltpu.VMEM((9, 256, 256), BF16),
            pltpu.VMEM((256, 512), BF16),
            pltpu.VMEM((4, 256, 1024), F32),
            pltpu.VMEM((2, 128, 512), F32),
            pltpu.VMEM((4, 384, 768), BF16),
            pltpu.VMEM((27, 256, 128), BF16),
            pltpu.VMEM((9, 384, 256), BF16),
            pltpu.VMEM((4, 2, 256, 128), BF16),
            pltpu.VMEM((2, 256, 512), F32),
            pltpu.VMEM((4, 2, 256, 128), BF16),
            pltpu.VMEM((2, 256, 1024), BF16),
            pltpu.VMEM((2, 128, 768), F32),
            pltpu.VMEM((2, 128, 768), BF16),
            pltpu.VMEM((2, 2, 128, 128), BF16),
            pltpu.VMEM((2, 128, 512), BF16),
            pltpu.VMEM((2, 2, 128, 128), BF16),
            pltpu.VMEM((2, 2, 128, 128), BF16),
            pltpu.VMEM((4, 256, 1024), BF16),
            pltpu.VMEM((2, 27, 4, 32, 128), BF16),
            pltpu.VMEM((27, 4, 32, 128), BF16),
            pltpu.VMEM((4, 27, 32, 128), BF16),
            pltpu.VMEM((4, 27, 32, 128), BF16),
            pltpu.VMEM((2, 27, 32, 128), BF16),
            pltpu.VMEM((27, 32, 128), BF16),
            pltpu.VMEM((2, 32, 32, 128), BF16),
            pltpu.VMEM((2, 16, 2, 32, 128), BF16),
            pltpu.VMEM((4, 2, 32, 128), F32),
            pltpu.SemaphoreType.DMA((3, 8)),
            pltpu.SemaphoreType.DMA((3, 8)),
            pltpu.SemaphoreType.DMA((6, 4)),
            pltpu.SemaphoreType.DMA((6, 4)),
            pltpu.SemaphoreType.DMA((4,)),
            pltpu.SemaphoreType.DMA((4,)),
            pltpu.SemaphoreType.DMA((4, 16)),
            pltpu.SemaphoreType.DMA((4, 16)),
        ],
        compiler_params=pltpu.CompilerParams(
            collective_id=0, has_side_effects=True, vmem_limit_bytes=56 * 1024 * 1024
        ),
        name="conv_step",
    )(samples, early_filters, deep_filters, deep_cotangent)
    grads = grads[:, :27].astype(F32)
    return act.transpose(2, 1, 0, 3)[None], grads[0], grads[1].transpose(0, 2, 1)


def solution(mesh):
    placed = (
        P("dp", None, "space", "chan", None),
        P(),
        P(None, "chan", None),
        P("dp", "chan", "space", None, None),
    )
    return jax.shard_map(
        on_device,
        mesh=mesh,
        in_specs=placed,
        out_specs=(P("dp", "chan", "space", None, None), P(None, "chan", None), P()),
        check_vma=False,
    )
```

```python
import jax
import jax.numpy as jnp
from jax import lax
from jax.experimental import pallas as pl
from jax.experimental.pallas import tpu as pltpu
from jax.sharding import PartitionSpec as P

BF16 = jnp.bfloat16
F32 = jnp.float32
MESH = pl.DeviceIdType.MESH

SIDES = [(dx, dy) for dx in (-1, 0, 1) for dy in (-1, 0, 1) if (dx, dy) != (0, 0)]


def dot(a, b):
    return lax.dot_general(a, b, (((1,), (0,)), ((), ())), preferred_element_type=F32)


def dot_nt(a, b):
    return lax.dot_general(a, b, (((1,), (1,)), ((), ())), preferred_element_type=F32)


def selector(rows, cols, hit):
    row = lax.broadcasted_iota(jnp.int32, (rows, cols), 0)
    col = lax.broadcasted_iota(jnp.int32, (rows, cols), 1)
    return jnp.where(hit(row, col), 1.0, 0.0).astype(BF16)


def sigmoid(u):
    return 0.5 + 0.5 * jnp.tanh(0.5 * u)


def sent_and_landed(side, length):
    if side == 0:
        return (1, length), (1, length)
    if side == 1:
        return (length, 1), (0, 1)
    return (1, 1), (length + 1, 1)


def build_early_weights(ef, w9):
    eye = selector(128, 128, lambda r, c: r == c)
    none = jnp.zeros((64, 128), BF16)

    def body(i, carry):
        for ae in range(3):
            taps = [ef[9 * i + 3 * ae + f] for f in range(3)]
            for p in range(2):
                slots = [none] + taps if p else taps + [none]
                rows = slice(p * 128, (p + 1) * 128)
                w9[3 * i + ae, rows, :] = dot_nt(eye, jnp.concatenate(slots, axis=0)).astype(BF16)
        return carry

    lax.fori_loop(0, 3, body, 0)


def cells_first(samples_raw, samples):
    swap = selector(256, 256, lambda r, c: c == (r % 32) * 8 + r // 32)

    def body(x, carry):
        for n in range(2):
            block = samples_raw[n * 32 : (n + 1) * 32, x].astype(F32).reshape(256, 256).astype(BF16)
            block = dot(swap, block).astype(BF16)
            for y in range(8):
                samples[x, y, n * 32 : (n + 1) * 32, :] = block[y * 32 : (y + 1) * 32]
        return carry

    lax.fori_loop(0, 4, body, 0)


def row_swap():
    return selector(256, 256, lambda r, c: c == (r % 16) * 16 + r // 16)


def deep_cells_first(raw, out):
    swap = row_swap()
    for n in range(4):
        rows = slice(n * 16, (n + 1) * 16)
        block = jnp.concatenate([raw[rows, X].reshape(256, 128) for X in range(2)], axis=1)
        block = dot(swap, block).astype(BF16)
        for Y in range(16):
            for X in range(2):
                out[Y, X, rows, :] = block[Y * 16 : (Y + 1) * 16, X * 128 : (X + 1) * 128]


def deep_channels_first(raw, out):
    swap = row_swap()
    for n in range(4):
        rows = slice(n * 16, (n + 1) * 16)
        block = [jnp.concatenate([raw[Y, X, rows, :] for Y in range(16)], axis=0) for X in range(2)]
        block = dot(swap, jnp.concatenate(block, axis=1)).astype(BF16)
        for X in range(2):
            out[rows, X] = block[:, X * 128 : (X + 1) * 128].reshape(16, 16, 128)


def place_taps(block, spread, taps_in, x, first_y, count):
    wide = dot(block, spread[...]).astype(BF16)
    for y in range(count):
        for s in range(4):
            taps_in[x, s * 64 : (s + 1) * 64, pl.ds((first_y + y) * 128, 128)] = wide[
                y * 64 : (y + 1) * 64, s * 128 : (s + 1) * 128
            ]


def early_terms(taps_in, w9, x, Y, shifts):
    total = None
    for a in shifts:
        for e in range(3):
            lanes = pl.ds(pl.multiple_of((2 * Y + e) * 128, 128), 256)
            term = dot(w9[3 * a + e], taps_in[x + a, :, lanes])
            total = term if total is None else total + term
    return total


def early_activation(pre, slopes, x, Y):
    s = sigmoid(pre)
    slopes[x, :, pl.ds(pl.multiple_of(Y * 256, 256), 256)] = s * (1.0 + pre * (1.0 - s))
    act = pre * s
    act = act[:128] + act[128:]
    return act[:, :128] + act[:, 128:]


def early_inner(taps_in, w9, slopes, pool_sum, first, last):
    def body(Y, carry):
        own = pl.ds(pl.multiple_of(Y * 256, 256), 256)
        for x, shifts in ((0, (1, 2)), (3, (0, 1))):
            slopes[x, :, own] = early_terms(taps_in, w9, x, Y, shifts)
        for X, x in enumerate((1, 2)):
            pre = early_terms(taps_in, w9, x, Y, (0, 1, 2))
            pool_sum[X, :, pl.ds(pl.multiple_of(Y * 128, 128), 128)] = early_activation(pre, slopes, x, Y)
        return carry

    lax.fori_loop(first, last, body, 0)


def early_outer(taps_in, w9, slopes, pool_sum, pooled):
    for Y in range(4):
        for X, x, a in ((0, 0, 0), (1, 3, 2)):
            pre = slopes[x, :, Y * 256 : (Y + 1) * 256] + early_terms(taps_in, w9, x, Y, (a,))
            total = pool_sum[X, :, Y * 128 : (Y + 1) * 128] + early_activation(pre, slopes, x, Y)
            pooled[X + 1, 128:256, (Y + 1) * 128 : (Y + 2) * 128] = (total * 0.125).astype(BF16)


def shift_pooled(pooled, xs, first, count):
    shifts = selector(128, 256, lambda r, c: r == jnp.where(c < 128, c - 1, c - 127))
    for x in xs:
        blocks = [pooled[x, 128:256, (first + y) * 128 : (first + y + 1) * 128] for y in range(count)]
        both = dot(jnp.concatenate(blocks, axis=0), shifts).astype(BF16)
        for y in range(count):
            lanes = slice((first + y) * 128, (first + y + 1) * 128)
            rows = slice(y * 128, (y + 1) * 128)
            pooled[x, 0:128, lanes] = both[rows, :128]
            pooled[x, 256:384, lanes] = both[rows, 128:]


def transpose_deep_weights(wd, wdt):
    eye = selector(128, 128, lambda r, c: r == c)

    def body(i, carry):
        for ae in range(3):
            for f in range(3):
                rows = slice(f * 128, (f + 1) * 128)
                wdt[3 * i + ae, rows, :] = dot_nt(eye, wd[9 * i + 3 * ae + f]).astype(BF16)
        return carry

    lax.fori_loop(0, 3, body, 0)


def deep_terms(pooled, wd, X, h, shifts):
    total = None
    for a in shifts:
        for e in range(3):
            weights = jnp.concatenate([wd[9 * a + 3 * e + f] for f in range(3)], axis=1)
            term = dot(weights, pooled[X + a, :, h * 256 + e * 128 : h * 256 + e * 128 + 256])
            total = term if total is None else total + term
    return total


def deep_inner(pooled, wd, pre_deep):
    for h in range(2):
        for X, shifts in ((0, (1, 2)), (1, (0, 1))):
            pre_deep[X, :, h * 256 : (h + 1) * 256] = deep_terms(pooled, wd, X, h, shifts)


def deep_outer(pooled, wd, ct, pre_deep, act, deep_in):
    for X, a in ((0, 0), (1, 2)):
        for h in range(2):
            pre = pre_deep[X, :, h * 256 : (h + 1) * 256] + deep_terms(pooled, wd, X, h, (a,))
            s = sigmoid(pre)
            value = (pre * s).astype(BF16)
            slope = s * (1.0 + pre * (1.0 - s))
            for k in range(2):
                Y, part = 2 * h + k, slice(k * 128, (k + 1) * 128)
                act[Y, X] = value[:, part]
                deep_in[X, :, (Y + 2) * 128 : (Y + 3) * 128] = (ct[Y, X].astype(F32) * slope[:, part]).astype(BF16)


def pooled_terms(deep_in, wdt, pairs, first):
    column = lax.broadcasted_iota(jnp.int32, (128, 128), 1)
    total = None
    for X, a in pairs:
        for e in range(3):
            lanes = slice((first + 2 - e) * 128, (first + 4 - e) * 128)
            term = dot(wdt[3 * a + e], deep_in[X, :, lanes])
            total = term if total is None else total + term
    parts = []
    for k in range(2):
        part = total[:, k * 128 : (k + 1) * 128]
        grad = part[128:256]
        grad += jnp.where(column < 127, pltpu.roll(part[0:128], 127, 1), 0.0)
        grad += jnp.where(column > 0, pltpu.roll(part[256:384], 1, 1), 0.0)
        parts.append(grad)
    return jnp.concatenate(parts, axis=1)


def pooled_outer(deep_in, wdt, send_x):
    for n, pairs in enumerate((((0, 0),), ((1, 2),))):
        for first in (0, 2, 4):
            send_x[n, :, first * 128 : (first + 2) * 128] = pooled_terms(deep_in, wdt, pairs, first).astype(BF16)


def pooled_inner(deep_in, wdt, pooled_grad, firsts):
    for X, pairs in enumerate((((0, 1), (1, 0)), ((0, 2), (1, 1)))):
        for first in firsts:
            pooled_grad[X, :, first * 128 : (first + 2) * 128] = pooled_terms(deep_in, wdt, pairs, first)


def early_cotangent(pooled_grad, got_x, got_y, got_xy, slopes, early_in):
    for X in range(2):
        grad = pooled_grad[X, :, 128:640] + got_x[X].astype(F32)
        for Y in range(4):
            here = grad[:, Y * 128 : (Y + 1) * 128]
            if Y in (0, 3):
                here += got_y[Y // 3, X].astype(F32) + got_xy[X, Y // 3].astype(F32)
            here *= 0.125
            for x in (2 * X, 2 * X + 1):
                for y in (2 * Y, 2 * Y + 1):
                    lanes = slice(y * 128, (y + 1) * 128)
                    for p in range(2):
                        rows = slice(p * 128, (p + 1) * 128)
                        early_in[x, rows, lanes] = (here * slopes[x, rows, lanes]).astype(BF16)


def deep_gradient(deep_in, pooled, out):
    def body(i, carry):
        a, e = i // 3, i % 3
        lanes = pl.ds(pl.multiple_of(e * 128, 128), 512)
        total = None
        for X in range(2):
            term = dot_nt(deep_in[X, :, 256:768], pooled[X + a, :, lanes])
            total = term if total is None else total + term
        for f in range(3):
            tap = total[:, f * 128 : (f + 1) * 128].astype(BF16).reshape(4, 2, 32, 128)
            for h in range(2):
                out[h, 3 * i + f] = tap[:, h]
        return carry

    lax.fori_loop(0, 9, body, 0)


def early_gradient(early_in, taps_in, out):
    def body(i, carry):
        a, e = i // 3, i % 3
        lanes = pl.ds(pl.multiple_of(e * 128, 128), 1024)
        total = None
        for x in range(4):
            term = dot_nt(taps_in[x + a, :, lanes], early_in[x])
            total = term if total is None else total + term
        total = (total[:192, :128] + total[64:, 128:]).astype(BF16)
        for f in range(3):
            for h in range(2):
                out[h, 3 * i + f] = total[f * 64 + h * 32 : f * 64 + h * 32 + 32]
        return carry

    lax.fori_loop(0, 9, body, 0)


def add_taps(count, out, terms):
    def body(t, carry):
        total = None
        for term in terms:
            value = term(t).astype(F32)
            total = value if total is None else total + value
        out(t, total.astype(BF16))
        return carry

    lax.fori_loop(0, count, body, 0)


def kernel(
    samples_raw, ef, wd_own, ct_raw,
    act_out, dg_out, eg_out,
    samples, ct_own, act_in, full, sample_ext, taps_in, w9, spread, slopes, pool_sum, pooled, wd, wdt, ct, pre_deep, act, deep_in,
    pooled_grad, send_x, send_y, got_x, got_y, got_xy, early_in,
    dg, dg_pair, dg_sum, dg_chan, eg, eg_pair, part, part_in, eg_chan,
    halo_send, halo_recv, x_send, x_recv, chan_send, chan_recv, pair_send, pair_recv, plane_send, plane_recv,
):
    dp, space, chan = lax.axis_index("dp"), lax.axis_index("space"), lax.axis_index("chan")
    core, column = space % 2, space // 2
    rank = column * 2 + dp

    def side_device(dx, dy):
        return {"dp": dp, "space": (space + dx + 16) % 16, "chan": (chan + dy + 4) % 4}

    def chan_device(j):
        return {"dp": dp, "space": space, "chan": (chan + j) % 4}

    def x_device(j):
        return {"dp": dp, "space": (space + 4 * j) % 16, "chan": chan}

    def plane_device(j):
        r = (rank + j) % 16
        return {"dp": r % 2, "space": (r // 2) * 2 + core, "chan": chan}

    sibling = {"dp": dp, "space": column * 2 + 1 - core, "chan": chan}

    barrier = pltpu.get_barrier_semaphore()
    peers = [side_device(dx, dy) for dx, dy in SIDES]
    peers += [chan_device(2), sibling] + [plane_device(j) for j in range(1, 16)]
    for peer in peers:
        pl.semaphore_signal(barrier, inc=1, device_id=peer, device_id_type=MESH)

    cells_first(samples_raw, samples)
    build_early_weights(ef, w9)
    spread[...] = selector(256, 512, lambda r, c: r == 2 * (c % 128) + c // 128 - 1)
    pl.semaphore_wait(barrier, len(peers))

    sends = []

    def describe(src, dst, send_sem, recv_sem, device):
        return pltpu.make_async_remote_copy(
            src_ref=src, dst_ref=dst, send_sem=send_sem, recv_sem=recv_sem, device_id=device, device_id_type=MESH
        )

    def remote(*args):
        copy = describe(*args)
        copy.start()
        sends.append(copy)
        return copy

    def landed(copies):
        for copy in copies:
            copy.wait_recv()

    def over_chan(n, src, dst):
        return [
            remote(src((chan + j) % 4), dst(j), chan_send.at[n, j], chan_recv.at[n, j], chan_device(j)) for j in (1, 2, 3)
        ]

    def pair(n, src, dst):
        return remote(src, dst, pair_send.at[n], pair_recv.at[n], sibling)

    def halo(n, view):
        copies = {}
        for k, (dx, dy) in enumerate(SIDES):
            src, dst = view(dx, dy)
            copies[dx, dy] = remote(src, dst, halo_send.at[n, k], halo_recv.at[n, k], side_device(dx, dy))
        return [copies[0, -1], copies[0, 1]], [copy for (dx, _), copy in copies.items() if dx != 0]

    def sample_view(dx, dy):
        (sx, nx), (tx, _) = sent_and_landed(dx, 4)
        (sy, ny), (ty, _) = sent_and_landed(dy, 8)
        src = samples.at[pl.ds(sx - 1, nx), pl.ds(sy - 1, ny)]
        return src, sample_ext.at[pl.ds(tx, nx), pl.ds(ty, ny)]

    def field_view(ref, first, rows):
        def view(dx, dy):
            (sx, nx), (tx, _) = sent_and_landed(dx, 2)
            (sy, ny), (ty, _) = sent_and_landed(dy, 4)
            block = pl.ds(first, rows)
            src = ref.at[pl.ds(sx, nx), block, pl.ds(sy * 128, ny * 128)]
            return src, ref.at[pl.ds(tx, nx), block, pl.ds(ty * 128, ny * 128)]

        return view

    def clear_y(ref, xs, rows, lanes):
        width = ref.shape[2]
        for at, span in ((0, slice(0, lanes)), (3, slice(width - lanes, width))):

            @pl.when(chan == at)
            def _():
                for x in xs:
                    ref[x, rows, span] = jnp.zeros((rows.stop - rows.start, lanes), BF16)

    def clear_x(ref, rows):
        width = ref.shape[2]
        for at, x in ((0, 0), (15, ref.shape[0] - 1)):

            @pl.when(space == at)
            def _():
                ref[x, rows, :] = jnp.zeros((rows.stop - rows.start, width), BF16)

    sample_y, sample_x = halo(0, sample_view)
    mine = pl.ds(pl.multiple_of(chan * 64, 64), 64)
    half = pl.ds(pl.multiple_of(core * 32, 32), 32)
    wd[0:27, mine, :] = wd_own[...]
    wd[27, mine, :] = jnp.zeros((64, 128), BF16)
    for x in range(4):
        place_taps(samples[x].reshape(512, 256), spread, taps_in, x + 1, 1, 8)
    deep_cells_first(ct_raw, ct_own)
    ct[:, :, mine, :] = ct_own[pl.ds(pl.multiple_of(chan * 4, 4), 4)]
    part[:, 27:, :, :] = jnp.zeros((2, 5, 32, 128), BF16)
    for X in range(2):
        for lanes in (slice(0, 256), slice(768, 1024)):
            deep_in[X, :, lanes] = jnp.zeros((256, 256), BF16)

    landed(sample_y)

    def some_of(c, taps, of_core):
        return wd.at[taps, pl.ds(pl.multiple_of(c * 64 + of_core * 32, 32), 32), :]

    my_taps = pl.ds(space // 4 * 7, 7)
    wd_copies = over_chan(0, lambda c: some_of(chan, my_taps, core), lambda j: some_of(chan, my_taps, core))
    ct_copies = over_chan(
        1, lambda c: ct_own.at[pl.ds(pl.multiple_of(c * 4, 4), 4)], lambda j: ct.at[:, :, mine, :]
    )
    for y in (0, 9):
        for x in range(1, 5):
            place_taps(sample_ext[x, y], spread, taps_in, x, y, 1)
    clear_y(taps_in, range(1, 5), slice(0, 256), 128)
    early_inner(taps_in, w9, slopes, pool_sum, 0, 1)
    for j, copy in zip((1, 2, 3), wd_copies):
        landed([copy])
        block = some_of((chan - j + 4) % 4, my_taps, core)
        for i in (1, 2, 3):
            remote(block, block, x_send.at[j, i], x_recv.at[j, i], x_device(i))
    early_inner(taps_in, w9, slopes, pool_sum, 1, 4)
    landed(sample_x)
    for x in (0, 5):
        place_taps(sample_ext[x].reshape(640, 256), spread, taps_in, x, 0, 10)
    clear_y(taps_in, (0, 5), slice(0, 256), 128)
    clear_x(taps_in, slice(0, 256))
    early_outer(taps_in, w9, slopes, pool_sum, pooled)

    pooled_y, pooled_x = halo(1, field_view(pooled, 128, 128))
    shift_pooled(pooled, (1, 2), 1, 4)
    for j in (1, 2, 3):
        for i in (1, 2, 3):
            block = some_of((chan - j + 4) % 4, pl.ds((space // 4 - i + 4) % 4 * 7, 7), core)
            describe(block, block, x_send.at[j, i], x_recv.at[j, i], x_device(i)).wait_recv()
        block = some_of((chan - j + 4) % 4, pl.ds(0, 27), core)
        remote(block, block, chan_send.at[2, j], chan_recv.at[2, j], sibling)
    landed(pooled_y)
    clear_y(pooled, (1, 2), slice(128, 256), 128)
    shift_pooled(pooled, (1, 2), 0, 1)
    shift_pooled(pooled, (1, 2), 5, 1)
    for j in (1, 2, 3):
        block = some_of((chan - j + 4) % 4, pl.ds(0, 27), 1 - core)
        describe(block, block, chan_send.at[2, j], chan_recv.at[2, j], sibling).wait_recv()
    deep_inner(pooled, wd, pre_deep)
    transpose_deep_weights(wd, wdt)
    landed(pooled_x)
    clear_y(pooled, (0, 3), slice(128, 256), 128)
    clear_x(pooled, slice(128, 256))
    shift_pooled(pooled, (0, 3), 0, 6)
    landed(ct_copies)
    deep_outer(pooled, wd, ct, pre_deep, act, deep_in)

    pooled_outer(deep_in, wdt, send_x)
    grad_copies = []
    for n, dx in enumerate((-1, 1)):
        for dy in (-1, 0, 1):
            at, count = {-1: (0, 1), 0: (1, 4), 1: (5, 1)}[dy]
            src = send_x.at[n, :, pl.ds(at * 128, count * 128)]
            dst = got_x.at[1 - n] if dy == 0 else got_xy.at[1 - n, 0 if dy > 0 else 1]
            k = SIDES.index((dx, dy))
            grad_copies.append(remote(src, dst, halo_send.at[2, k], halo_recv.at[2, k], side_device(dx, dy)))
    pooled_inner(deep_in, wdt, pooled_grad, (0, 4))
    for n, (dy, at) in enumerate(((-1, 0), (1, 5))):
        for X in range(2):
            send_y[n, X] = pooled_grad[X, :, at * 128 : (at + 1) * 128].astype(BF16)
        k = SIDES.index((0, dy))
        grad_copies.append(
            remote(send_y.at[n], got_y.at[1 - n], halo_send.at[2, k], halo_recv.at[2, k], side_device(0, dy))
        )

    deep_gradient(deep_in, pooled, dg)
    dg_pair_copy = pair(0, dg.at[1 - core], dg_pair)
    pooled_inner(deep_in, wdt, pooled_grad, (2,))

    def put_sum(t, value):
        dg_sum[:, t] = value

    landed([dg_pair_copy])
    add_taps(27, put_sum, [lambda t: dg[core, t], lambda t: dg_pair[t]])
    dg_copies = over_chan(3, lambda c: dg_sum.at[c], lambda j: dg_chan.at[j])
    landed(grad_copies)
    for at, n in ((0, 0), (15, 1)):

        @pl.when(space == at)
        def _():
            got_x[n] = jnp.zeros((128, 512), BF16)
            got_xy[n] = jnp.zeros((2, 128, 128), BF16)

    for at, n in ((0, 0), (3, 1)):

        @pl.when(chan == at)
        def _():
            got_y[n] = jnp.zeros((2, 128, 128), BF16)
            for m in range(2):
                got_xy[m, n] = jnp.zeros((128, 128), BF16)

    early_cotangent(pooled_grad, got_x, got_y, got_xy, slopes, early_in)
    early_gradient(early_in, taps_in, eg)
    eg_pair_copy = pair(1, eg.at[1 - core], eg_pair)

    def put_part(n):
        def put(t, value):
            part[n, t] = value

        return put

    def taps_of(r):
        return pl.ds(r * 2, 2)

    own = taps_of(rank)

    def plane_scatter(n):
        copies = []
        for j in range(1, 16):
            src = part.at[n, taps_of((rank + j) % 16)]
            copies.append(remote(src, part_in.at[n, j], plane_send.at[n, j], plane_recv.at[n, j], plane_device(j)))
        return copies

    def plane_sum(n):
        summed = part[n, own].astype(F32)
        for j in range(1, 16):
            summed += part_in[n, j].astype(F32)
        return summed

    def plane_gather(n):
        block = full.at[n, own, half, :]
        for j in range(1, 16):
            remote(block, block, plane_send.at[2 + n, j], plane_recv.at[2 + n, j], plane_device(j))

    def plane_gathered(n):
        for j in range(1, 16):
            theirs = full.at[n, taps_of((rank - j + 16) % 16), half, :]
            describe(theirs, theirs, plane_send.at[2 + n, j], plane_recv.at[2 + n, j], plane_device(j)).wait_recv()

    def halves(n):
        block = full.at[n, pl.ds(0, 27), half, :]
        pair(2 + n, block, block)

    def halves_landed(n):
        block = full.at[n, pl.ds(0, 27), pl.ds(pl.multiple_of(32 - core * 32, 32), 32), :]
        describe(block, block, pair_send.at[2 + n], pair_recv.at[2 + n], sibling).wait_recv()

    landed([eg_pair_copy])
    add_taps(27, put_part(1), [lambda t: eg[core, t], lambda t: eg_pair[t]])
    eg_copies = plane_scatter(1)
    landed(dg_copies)
    add_taps(27, put_part(0), [lambda t: dg_sum[chan, t]] + [lambda t, j=j: dg_chan[j, t] for j in (1, 2, 3)])
    dg_plane = plane_scatter(0)
    here = pl.ds(pl.multiple_of(chan * 4, 4), 4)
    act_copies = over_chan(
        4, lambda c: act.at[:, :, pl.ds(pl.multiple_of(c * 64, 64), 64), :], lambda j: act_in.at[here]
    )
    act_in[here] = act[:, :, mine, :]
    landed(eg_copies)
    eg_chan[chan] = plane_sum(1)
    over_chan(5, lambda c: eg_chan.at[chan], lambda j: eg_chan.at[chan])
    landed(dg_plane)
    full[0, own, half, :] = plane_sum(0).astype(BF16)
    plane_gather(0)
    for j in (1, 2, 3):
        block = eg_chan.at[(chan - j + 4) % 4]
        describe(block, block, chan_send.at[5, j], chan_recv.at[5, j], chan_device(j)).wait_recv()
    full[1, own, half, :] = ((eg_chan[0] + eg_chan[1]) + (eg_chan[2] + eg_chan[3])).astype(BF16)
    plane_gather(1)
    plane_gathered(0)
    halves(0)
    landed(act_copies)
    deep_channels_first(act_in, act_out)
    plane_gathered(1)
    halves(1)
    halves_landed(0)
    for t in range(27):
        dg_out[t] = full[0, t].astype(F32)
    halves_landed(1)
    for t in range(27):
        eg_out[t] = full[1, t].astype(F32)

    for copy in sends:
        copy.wait_send()


def on_device(samples, early_filters, deep_filters, deep_cotangent):
    act, deep_grad, early_grad = pl.pallas_call(
        kernel,
        out_shape=(
            jax.ShapeDtypeStruct((64, 2, 16, 128), BF16),
            jax.ShapeDtypeStruct((27, 64, 128), F32),
            jax.ShapeDtypeStruct((27, 64, 128), F32),
        ),
        in_specs=[pl.BlockSpec(memory_space=pltpu.VMEM)] * 4,
        out_specs=[pl.BlockSpec(memory_space=pltpu.VMEM)] * 3,
        scratch_shapes=[
            pltpu.VMEM((4, 8, 64, 256), BF16),
            pltpu.VMEM((16, 2, 64, 128), BF16),
            pltpu.VMEM((16, 2, 64, 128), BF16),
            pltpu.VMEM((2, 32, 64, 128), BF16),
            pltpu.VMEM((6, 10, 64, 256), BF16),
            pltpu.VMEM((6, 256, 1280), BF16),
            pltpu.VMEM((9, 256, 256), BF16),
            pltpu.VMEM((256, 512), BF16),
            pltpu.VMEM((4, 256, 1024), F32),
            pltpu.VMEM((2, 128, 512), F32),
            pltpu.VMEM((4, 384, 768), BF16),
            pltpu.VMEM((28, 256, 128), BF16),
            pltpu.VMEM((9, 384, 256), BF16),
            pltpu.VMEM((4, 2, 256, 128), BF16),
            pltpu.VMEM((2, 256, 512), F32),
            pltpu.VMEM((4, 2, 256, 128), BF16),
            pltpu.VMEM((2, 256, 1024), BF16),
            pltpu.VMEM((2, 128, 768), F32),
            pltpu.VMEM((2, 128, 768), BF16),
            pltpu.VMEM((2, 2, 128, 128), BF16),
            pltpu.VMEM((2, 128, 512), BF16),
            pltpu.VMEM((2, 2, 128, 128), BF16),
            pltpu.VMEM((2, 2, 128, 128), BF16),
            pltpu.VMEM((4, 256, 1024), BF16),
            pltpu.VMEM((2, 27, 4, 32, 128), BF16),
            pltpu.VMEM((27, 4, 32, 128), BF16),
            pltpu.VMEM((4, 27, 32, 128), BF16),
            pltpu.VMEM((4, 27, 32, 128), BF16),
            pltpu.VMEM((2, 27, 32, 128), BF16),
            pltpu.VMEM((27, 32, 128), BF16),
            pltpu.VMEM((2, 32, 32, 128), BF16),
            pltpu.VMEM((2, 16, 2, 32, 128), BF16),
            pltpu.VMEM((4, 2, 32, 128), F32),
            pltpu.SemaphoreType.DMA((3, 8)),
            pltpu.SemaphoreType.DMA((3, 8)),
            pltpu.SemaphoreType.DMA((4, 4)),
            pltpu.SemaphoreType.DMA((4, 4)),
            pltpu.SemaphoreType.DMA((6, 4)),
            pltpu.SemaphoreType.DMA((6, 4)),
            pltpu.SemaphoreType.DMA((4,)),
            pltpu.SemaphoreType.DMA((4,)),
            pltpu.SemaphoreType.DMA((4, 16)),
            pltpu.SemaphoreType.DMA((4, 16)),
        ],
        compiler_params=pltpu.CompilerParams(
            collective_id=0, has_side_effects=True, vmem_limit_bytes=56 * 1024 * 1024
        ),
        name="conv_step",
    )(samples[0], early_filters.transpose(0, 2, 1), deep_filters, deep_cotangent[0])
    return act[None], deep_grad, early_grad.transpose(0, 2, 1)


def solution(mesh):
    placed = (
        P("dp", None, "space", "chan", None),
        P(),
        P(None, "chan", None),
        P("dp", "chan", "space", None, None),
    )
    return jax.shard_map(
        on_device,
        mesh=mesh,
        in_specs=placed,
        out_specs=(P("dp", "chan", "space", None, None), P(None, "chan", None), P()),
        check_vma=False,
    )
```

```python
import jax
import jax.numpy as jnp
from jax import lax
from jax.experimental import pallas as pl
from jax.experimental.pallas import tpu as pltpu
from jax.sharding import PartitionSpec as P

BF16 = jnp.bfloat16
F32 = jnp.float32
MESH = pl.DeviceIdType.MESH

SIDES = [(dx, dy) for dx in (-1, 0, 1) for dy in (-1, 0, 1) if (dx, dy) != (0, 0)]


def dot(a, b):
    return lax.dot_general(a, b, (((1,), (0,)), ((), ())), preferred_element_type=F32)


def dot_nt(a, b):
    return lax.dot_general(a, b, (((1,), (1,)), ((), ())), preferred_element_type=F32)


def selector(rows, cols, hit):
    row = lax.broadcasted_iota(jnp.int32, (rows, cols), 0)
    col = lax.broadcasted_iota(jnp.int32, (rows, cols), 1)
    return jnp.where(hit(row, col), 1.0, 0.0).astype(BF16)


def sigmoid(u):
    return 0.5 + 0.5 * jnp.tanh(0.5 * u)


def sent_and_landed(side, length):
    if side == 0:
        return (1, length), (1, length)
    if side == 1:
        return (length, 1), (0, 1)
    return (1, 1), (length + 1, 1)


def build_early_weights(ef, w9):
    eye = selector(128, 128, lambda r, c: r == c)
    none = jnp.zeros((64, 128), BF16)

    def body(i, carry):
        for ae in range(3):
            taps = [ef[9 * i + 3 * ae + f] for f in range(3)]
            for p in range(2):
                slots = [none] + taps if p else taps + [none]
                rows = slice(p * 128, (p + 1) * 128)
                w9[3 * i + ae, rows, :] = dot_nt(eye, jnp.concatenate(slots, axis=0)).astype(BF16)
        return carry

    lax.fori_loop(0, 3, body, 0)


def cells_first(samples_raw, samples):
    swap = selector(256, 256, lambda r, c: c == (r % 32) * 8 + r // 32)

    def body(x, carry):
        for n in range(2):
            block = samples_raw[n * 32 : (n + 1) * 32, x].astype(F32).reshape(256, 256).astype(BF16)
            block = dot(swap, block).astype(BF16)
            for y in range(8):
                samples[x, y, n * 32 : (n + 1) * 32, :] = block[y * 32 : (y + 1) * 32]
        return carry

    lax.fori_loop(0, 4, body, 0)


def row_swap():
    return selector(256, 256, lambda r, c: c == (r % 16) * 16 + r // 16)


def deep_cells_first(raw, out):
    swap = row_swap()
    for n in range(4):
        rows = slice(n * 16, (n + 1) * 16)
        block = jnp.concatenate([raw[rows, X].reshape(256, 128) for X in range(2)], axis=1)
        block = dot(swap, block).astype(BF16)
        for Y in range(16):
            for X in range(2):
                out[Y, X, rows, :] = block[Y * 16 : (Y + 1) * 16, X * 128 : (X + 1) * 128]


def deep_channels_first(raw, out):
    swap = row_swap()
    for n in range(4):
        rows = slice(n * 16, (n + 1) * 16)
        block = [jnp.concatenate([raw[Y, X, rows, :] for Y in range(16)], axis=0) for X in range(2)]
        block = dot(swap, jnp.concatenate(block, axis=1)).astype(BF16)
        for X in range(2):
            out[rows, X] = block[:, X * 128 : (X + 1) * 128].reshape(16, 16, 128)


def place_taps(block, spread, taps_in, x, first_y, count):
    wide = dot(block, spread[...]).astype(BF16)
    for y in range(count):
        for s in range(4):
            taps_in[x, s * 64 : (s + 1) * 64, pl.ds((first_y + y) * 128, 128)] = wide[
                y * 64 : (y + 1) * 64, s * 128 : (s + 1) * 128
            ]


def early_terms(taps_in, w9, x, Y, shifts):
    total = None
    for a in shifts:
        for e in range(3):
            term = dot(w9[3 * a + e], taps_in[x + a, :, (2 * Y + e) * 128 : (2 * Y + e + 2) * 128])
            total = term if total is None else total + term
    return total


def early_activation(pre, slopes, x, Y):
    s = sigmoid(pre)
    slopes[x, :, Y * 256 : (Y + 1) * 256] = s * (1.0 + pre * (1.0 - s))
    act = pre * s
    act = act[:128] + act[128:]
    return act[:, :128] + act[:, 128:]


def early_inner(taps_in, w9, slopes, pool_sum, Ys):
    for Y in Ys:
        for x, shifts in ((0, (1, 2)), (3, (0, 1))):
            slopes[x, :, Y * 256 : (Y + 1) * 256] = early_terms(taps_in, w9, x, Y, shifts)
        for X, x in enumerate((1, 2)):
            pre = early_terms(taps_in, w9, x, Y, (0, 1, 2))
            pool_sum[X, :, Y * 128 : (Y + 1) * 128] = early_activation(pre, slopes, x, Y)


def early_outer(taps_in, w9, slopes, pool_sum, pooled):
    for Y in range(4):
        for X, x, a in ((0, 0, 0), (1, 3, 2)):
            pre = slopes[x, :, Y * 256 : (Y + 1) * 256] + early_terms(taps_in, w9, x, Y, (a,))
            total = pool_sum[X, :, Y * 128 : (Y + 1) * 128] + early_activation(pre, slopes, x, Y)
            pooled[X + 1, 128:256, (Y + 1) * 128 : (Y + 2) * 128] = (total * 0.125).astype(BF16)


def shift_pooled(pooled, xs, first, count):
    shifts = selector(128, 256, lambda r, c: r == jnp.where(c < 128, c - 1, c - 127))
    for x in xs:
        blocks = [pooled[x, 128:256, (first + y) * 128 : (first + y + 1) * 128] for y in range(count)]
        both = dot(jnp.concatenate(blocks, axis=0), shifts).astype(BF16)
        for y in range(count):
            lanes = slice((first + y) * 128, (first + y + 1) * 128)
            rows = slice(y * 128, (y + 1) * 128)
            pooled[x, 0:128, lanes] = both[rows, :128]
            pooled[x, 256:384, lanes] = both[rows, 128:]


def transpose_deep_weights(wd, wdt):
    eye = selector(128, 128, lambda r, c: r == c)

    def body(i, carry):
        for ae in range(3):
            for f in range(3):
                rows = slice(f * 128, (f + 1) * 128)
                wdt[3 * i + ae, rows, :] = dot_nt(eye, wd[9 * i + 3 * ae + f]).astype(BF16)
        return carry

    lax.fori_loop(0, 3, body, 0)


def deep_terms(pooled, wd, X, h, shifts):
    total = None
    for a in shifts:
        for e in range(3):
            weights = jnp.concatenate([wd[9 * a + 3 * e + f] for f in range(3)], axis=1)
            term = dot(weights, pooled[X + a, :, h * 256 + e * 128 : h * 256 + e * 128 + 256])
            total = term if total is None else total + term
    return total


def deep_inner(pooled, wd, pre_deep):
    for h in range(2):
        for X, shifts in ((0, (1, 2)), (1, (0, 1))):
            pre_deep[X, :, h * 256 : (h + 1) * 256] = deep_terms(pooled, wd, X, h, shifts)


def deep_outer(pooled, wd, ct, pre_deep, act, deep_in):
    for X, a in ((0, 0), (1, 2)):
        for h in range(2):
            pre = pre_deep[X, :, h * 256 : (h + 1) * 256] + deep_terms(pooled, wd, X, h, (a,))
            s = sigmoid(pre)
            value = (pre * s).astype(BF16)
            slope = s * (1.0 + pre * (1.0 - s))
            for k in range(2):
                Y, part = 2 * h + k, slice(k * 128, (k + 1) * 128)
                act[Y, X] = value[:, part]
                deep_in[X, :, (Y + 2) * 128 : (Y + 3) * 128] = (ct[Y, X].astype(F32) * slope[:, part]).astype(BF16)


def pooled_terms(deep_in, wdt, pairs, first):
    column = lax.broadcasted_iota(jnp.int32, (128, 128), 1)
    total = None
    for X, a in pairs:
        for e in range(3):
            lanes = slice((first + 2 - e) * 128, (first + 4 - e) * 128)
            term = dot(wdt[3 * a + e], deep_in[X, :, lanes])
            total = term if total is None else total + term
    parts = []
    for k in range(2):
        part = total[:, k * 128 : (k + 1) * 128]
        grad = part[128:256]
        grad += jnp.where(column < 127, pltpu.roll(part[0:128], 127, 1), 0.0)
        grad += jnp.where(column > 0, pltpu.roll(part[256:384], 1, 1), 0.0)
        parts.append(grad)
    return jnp.concatenate(parts, axis=1)


def pooled_outer(deep_in, wdt, send_x):
    for n, pairs in enumerate((((0, 0),), ((1, 2),))):
        for first in (0, 2, 4):
            send_x[n, :, first * 128 : (first + 2) * 128] = pooled_terms(deep_in, wdt, pairs, first).astype(BF16)


def pooled_inner(deep_in, wdt, pooled_grad, firsts):
    for X, pairs in enumerate((((0, 1), (1, 0)), ((0, 2), (1, 1)))):
        for first in firsts:
            pooled_grad[X, :, first * 128 : (first + 2) * 128] = pooled_terms(deep_in, wdt, pairs, first)


def early_cotangent(pooled_grad, got_x, got_y, got_xy, slopes, early_in):
    for X in range(2):
        grad = pooled_grad[X, :, 128:640] + got_x[X].astype(F32)
        for Y in range(4):
            here = grad[:, Y * 128 : (Y + 1) * 128]
            if Y in (0, 3):
                here += got_y[Y // 3, X].astype(F32) + got_xy[X, Y // 3].astype(F32)
            here *= 0.125
            for x in (2 * X, 2 * X + 1):
                for y in (2 * Y, 2 * Y + 1):
                    lanes = slice(y * 128, (y + 1) * 128)
                    for p in range(2):
                        rows = slice(p * 128, (p + 1) * 128)
                        early_in[x, rows, lanes] = (here * slopes[x, rows, lanes]).astype(BF16)


def slot(ae, f):
    return 3 * ae + f + ae // 5


def deep_gradient(deep_in, pooled, out):
    for ae in range(9):
        a, e = ae // 3, ae % 3
        total = None
        for X in range(2):
            term = dot_nt(deep_in[X, :, 256:768], pooled[X + a, :, e * 128 : e * 128 + 512])
            total = term if total is None else total + term
        for f in range(3):
            tap = total[:, f * 128 : (f + 1) * 128].astype(BF16).reshape(4, 2, 32, 128)
            for h in range(2):
                out[h, slot(ae, f)] = tap[:, h]


def early_gradient(early_in, taps_in, out, first, last):
    for ae in range(first, last):
        a, e = ae // 3, ae % 3
        total = None
        for x in range(4):
            term = dot_nt(taps_in[x + a, :, e * 128 : e * 128 + 1024], early_in[x])
            total = term if total is None else total + term
        total = (total[:192, :128] + total[64:, 128:]).astype(BF16)
        for f in range(3):
            for h in range(2):
                out[h, slot(ae, f)] = total[f * 64 + h * 32 : f * 64 + h * 32 + 32]


def add_taps(first, last, out, terms):
    def body(t, carry):
        total = None
        for term in terms:
            value = term(t).astype(F32)
            total = value if total is None else total + value
        out(t, total.astype(BF16))
        return carry

    lax.fori_loop(first, last, body, 0)


def total_of(own, others):
    total = own.astype(F32)
    for other in others:
        total += other.astype(F32)
    return total


def kernel(
    samples_raw, ef_hbm, wd_hbm, ct_hbm,
    act_in, full,
    samples, ef, ct_raw, ct_own, sample_ext, taps_in, w9, spread, slopes, pool_sum, pooled, wd, wdt, ct, pre_deep, act, deep_in,
    pooled_grad, send_x, send_y, got_x, got_y, got_xy, early_in,
    dg, dg_pair, dg_b, dg_b_in, dg_b_sum, dg_b_chan, dg_a, dg_a_in, dg_a_sum, dg_a_plane,
    eg, eg_pair, eg_sum, eg_plane, eg_chan,
    halo_send, halo_recv, x_send, x_recv, chan_send, chan_recv, pair_send, pair_recv, plane_send, plane_recv, both_send, both_recv, load_sem,
):
    dp, space, chan = lax.axis_index("dp"), lax.axis_index("space"), lax.axis_index("chan")
    core, column = space % 2, space // 2
    rank = column * 2 + dp

    def side_device(dx, dy):
        return {"dp": dp, "space": (space + dx + 16) % 16, "chan": (chan + dy + 4) % 4}

    def chan_device(j):
        return {"dp": dp, "space": space, "chan": (chan + j) % 4}

    def x_device(j):
        return {"dp": dp, "space": (space + 4 * j) % 16, "chan": chan}

    def plane_device(j):
        r = (rank + j) % 16
        return {"dp": r % 2, "space": (r // 2) * 2 + core, "chan": chan}

    sibling = {"dp": dp, "space": column * 2 + 1 - core, "chan": chan}

    barrier = pltpu.get_barrier_semaphore()
    peers = [side_device(dx, dy) for dx, dy in SIDES]
    peers += [chan_device(2), sibling] + [plane_device(j) for j in range(1, 16)]
    for peer in peers:
        pl.semaphore_signal(barrier, inc=1, device_id=peer, device_id_type=MESH)

    mine = pl.ds(pl.multiple_of(chan * 64, 64), 64)
    half = pl.ds(pl.multiple_of(core * 32, 32), 32)
    loads = [
        pltpu.make_async_copy(src, dst, load_sem.at[n])
        for n, (src, dst) in enumerate(((ef_hbm, ef), (ct_hbm, ct_raw), (wd_hbm, wd.at[pl.ds(0, 27), mine, :])))
    ]
    for load in loads:
        load.start()
    cells_first(samples_raw, samples)
    loads[0].wait()
    build_early_weights(ef, w9)
    spread[...] = selector(256, 512, lambda r, c: r == 2 * (c % 128) + c // 128 - 1)
    loads[1].wait()
    deep_cells_first(ct_raw, ct_own)
    ct[:, :, mine, :] = ct_own[pl.ds(pl.multiple_of(chan * 4, 4), 4)]
    loads[2].wait()
    wd[27, mine, :] = jnp.zeros((64, 128), BF16)

    pl.semaphore_wait(barrier, len(peers))

    sends = []

    def describe(src, dst, send_sem, recv_sem, device):
        return pltpu.make_async_remote_copy(
            src_ref=src, dst_ref=dst, send_sem=send_sem, recv_sem=recv_sem, device_id=device, device_id_type=MESH
        )

    def remote(*args):
        copy = describe(*args)
        copy.start()
        sends.append(copy)
        return copy

    def landed(copies):
        for copy in copies:
            copy.wait_recv()

    def over_chan(n, src, dst):
        return [
            remote(src((chan + j) % 4), dst(j), chan_send.at[n, j], chan_recv.at[n, j], chan_device(j)) for j in (1, 2, 3)
        ]

    def pair(n, src, dst):
        return remote(src, dst, pair_send.at[n], pair_recv.at[n], sibling)

    def halo(n, view):
        copies = {}
        for k, (dx, dy) in enumerate(SIDES):
            src, dst = view(dx, dy)
            copies[dx, dy] = remote(src, dst, halo_send.at[n, k], halo_recv.at[n, k], side_device(dx, dy))
        return [copies[0, -1], copies[0, 1]], [copy for (dx, _), copy in copies.items() if dx != 0]

    def sample_view(dx, dy):
        (sx, nx), (tx, _) = sent_and_landed(dx, 4)
        (sy, ny), (ty, _) = sent_and_landed(dy, 8)
        src = samples.at[pl.ds(sx - 1, nx), pl.ds(sy - 1, ny)]
        return src, sample_ext.at[pl.ds(tx, nx), pl.ds(ty, ny)]

    def field_view(ref, first, rows):
        def view(dx, dy):
            (sx, nx), (tx, _) = sent_and_landed(dx, 2)
            (sy, ny), (ty, _) = sent_and_landed(dy, 4)
            block = pl.ds(first, rows)
            src = ref.at[pl.ds(sx, nx), block, pl.ds(sy * 128, ny * 128)]
            return src, ref.at[pl.ds(tx, nx), block, pl.ds(ty * 128, ny * 128)]

        return view

    def clear_y(ref, xs, rows, lanes):
        width = ref.shape[2]
        for at, span in ((0, slice(0, lanes)), (3, slice(width - lanes, width))):

            @pl.when(chan == at)
            def _():
                for x in xs:
                    ref[x, rows, span] = jnp.zeros((rows.stop - rows.start, lanes), BF16)

    def clear_x(ref, rows):
        width = ref.shape[2]
        for at, x in ((0, 0), (15, ref.shape[0] - 1)):

            @pl.when(space == at)
            def _():
                ref[x, rows, :] = jnp.zeros((rows.stop - rows.start, width), BF16)

    sample_y, sample_x = halo(0, sample_view)

    def some_of(c, taps, of_core):
        return wd.at[taps, pl.ds(pl.multiple_of(c * 64 + of_core * 32, 32), 32), :]

    my_taps = pl.ds(space // 4 * 7, 7)
    wd_copies = over_chan(0, lambda c: some_of(chan, my_taps, core), lambda j: some_of(chan, my_taps, core))
    for x in range(4):
        place_taps(samples[x].reshape(512, 256), spread, taps_in, x + 1, 1, 8)
    for h in range(2):
        dg[h, 15] = jnp.zeros((4, 32, 128), BF16)
        eg[h, 15] = jnp.zeros((32, 128), BF16)
    dg_a_sum[12:16] = jnp.zeros((4, 32, 128), BF16)
    eg_sum[28:32] = jnp.zeros((4, 32, 128), BF16)
    for X in range(2):
        for lanes in (slice(0, 256), slice(768, 1024)):
            deep_in[X, :, lanes] = jnp.zeros((256, 256), BF16)

    early_inner(taps_in, w9, slopes, pool_sum, (1, 2))
    landed(sample_y)
    for y in (0, 9):
        for x in range(1, 5):
            place_taps(sample_ext[x, y], spread, taps_in, x, y, 1)
    clear_y(taps_in, range(1, 5), slice(0, 256), 128)
    for j, copy in zip((1, 2, 3), wd_copies):
        landed([copy])
        block = some_of((chan - j + 4) % 4, my_taps, core)
        for i in (1, 2, 3):
            remote(block, block, x_send.at[j, i], x_recv.at[j, i], x_device(i))
    ct_copies = over_chan(
        1, lambda c: ct_own.at[pl.ds(pl.multiple_of(c * 4, 4), 4)], lambda j: ct.at[:, :, mine, :]
    )
    early_inner(taps_in, w9, slopes, pool_sum, (0, 3))
    landed(sample_x)
    for x in (0, 5):
        place_taps(sample_ext[x].reshape(640, 256), spread, taps_in, x, 0, 10)
    clear_y(taps_in, (0, 5), slice(0, 256), 128)
    clear_x(taps_in, slice(0, 256))
    early_outer(taps_in, w9, slopes, pool_sum, pooled)

    pooled_y, pooled_x = halo(1, field_view(pooled, 128, 128))
    shift_pooled(pooled, (1, 2), 1, 4)
    for j in (1, 2, 3):
        for i in (1, 2, 3):
            block = some_of((chan - j + 4) % 4, pl.ds((space // 4 - i + 4) % 4 * 7, 7), core)
            describe(block, block, x_send.at[j, i], x_recv.at[j, i], x_device(i)).wait_recv()
        block = some_of((chan - j + 4) % 4, pl.ds(0, 27), core)
        remote(block, block, chan_send.at[2, j], chan_recv.at[2, j], sibling)
    landed(pooled_y)
    clear_y(pooled, (1, 2), slice(128, 256), 128)
    shift_pooled(pooled, (1, 2), 0, 1)
    shift_pooled(pooled, (1, 2), 5, 1)
    for j in (1, 2, 3):
        block = some_of((chan - j + 4) % 4, pl.ds(0, 27), 1 - core)
        describe(block, block, chan_send.at[2, j], chan_recv.at[2, j], sibling).wait_recv()
    deep_inner(pooled, wd, pre_deep)
    transpose_deep_weights(wd, wdt)
    landed(pooled_x)
    clear_y(pooled, (0, 3), slice(128, 256), 128)
    clear_x(pooled, slice(128, 256))
    shift_pooled(pooled, (0, 3), 0, 6)
    landed(ct_copies)
    deep_outer(pooled, wd, ct, pre_deep, act, deep_in)

    pooled_outer(deep_in, wdt, send_x)
    grad_copies = []
    for n, dx in enumerate((-1, 1)):
        for dy in (-1, 0, 1):
            at, count = {-1: (0, 1), 0: (1, 4), 1: (5, 1)}[dy]
            src = send_x.at[n, :, pl.ds(at * 128, count * 128)]
            dst = got_x.at[1 - n] if dy == 0 else got_xy.at[1 - n, 0 if dy > 0 else 1]
            k = SIDES.index((dx, dy))
            grad_copies.append(remote(src, dst, halo_send.at[2, k], halo_recv.at[2, k], side_device(dx, dy)))
    pooled_inner(deep_in, wdt, pooled_grad, (0, 4))
    for n, (dy, at) in enumerate(((-1, 0), (1, 5))):
        for X in range(2):
            send_y[n, X] = pooled_grad[X, :, at * 128 : (at + 1) * 128].astype(BF16)
        k = SIDES.index((0, dy))
        grad_copies.append(
            remote(send_y.at[n], got_y.at[1 - n], halo_send.at[2, k], halo_recv.at[2, k], side_device(0, dy))
        )

    here = pl.ds(pl.multiple_of(chan * 4, 4), 4)
    act_copies = over_chan(
        4, lambda c: act.at[:, :, pl.ds(pl.multiple_of(c * 64, 64), 64), :], lambda j: act_in.at[here]
    )
    act_in[here] = act[:, :, mine, :]

    def over_plane(n, src, dst):
        return [
            remote(src((rank + j) % 16), dst(j), plane_send.at[n, j], plane_recv.at[n, j], plane_device(j))
            for j in range(1, 16)
        ]

    deep_gradient(deep_in, pooled, dg)
    dg_pair_copy = pair(0, dg.at[1 - core, pl.ds(0, 28)], dg_pair)
    pooled_inner(deep_in, wdt, pooled_grad, (2,))
    landed(grad_copies)
    for at, n in ((0, 0), (15, 1)):

        @pl.when(space == at)
        def _():
            got_x[n] = jnp.zeros((128, 512), BF16)
            got_xy[n] = jnp.zeros((2, 128, 128), BF16)

    for at, n in ((0, 0), (3, 1)):

        @pl.when(chan == at)
        def _():
            got_y[n] = jnp.zeros((2, 128, 128), BF16)
            for m in range(2):
                got_xy[m, n] = jnp.zeros((128, 128), BF16)

    early_cotangent(pooled_grad, got_x, got_y, got_xy, slopes, early_in)
    landed([dg_pair_copy])

    def put_b(t, value):
        dg_b[t] = value

    def put_a(t, value):
        dg_a[:, t - 16] = value

    add_taps(16, 28, put_a, [lambda t: dg[core, t], lambda t: dg_pair[t]])
    dg_a_copies = over_chan(3, lambda c: dg_a.at[c], lambda j: dg_a_in.at[j])
    add_taps(0, 16, put_b, [lambda t: dg[core, t], lambda t: dg_pair[t]])
    dg_b_copies = over_plane(0, lambda r: dg_b.at[r], lambda j: dg_b_in.at[j])
    early_gradient(early_in, taps_in, eg, 0, 5)
    eg_pair_0 = pair(1, eg.at[1 - core, pl.ds(0, 16)], eg_pair.at[pl.ds(0, 16)])
    early_gradient(early_in, taps_in, eg, 5, 7)

    def put_eg(t, value):
        eg_sum[t] = value

    landed([eg_pair_0])
    add_taps(0, 16, put_eg, [lambda t: eg[core, t], lambda t: eg_pair[t]])
    eg_copies = over_plane(2, lambda r: eg_sum.at[r], lambda j: eg_plane.at[0, j])
    early_gradient(early_in, taps_in, eg, 7, 9)
    eg_pair_1 = pair(2, eg.at[1 - core, pl.ds(16, 12)], eg_pair.at[pl.ds(16, 12)])

    def put_a_sum(t, value):
        dg_a_sum[t] = value

    landed(dg_a_copies)
    add_taps(0, 12, put_a_sum, [lambda t: dg_a[chan, t]] + [lambda t, j=j: dg_a_in[j, t] for j in (1, 2, 3)])
    landed([eg_pair_1])
    add_taps(16, 28, put_eg, [lambda t: eg[core, t], lambda t: eg_pair[t]])
    eg_copies += over_plane(3, lambda r: eg_sum.at[16 + r], lambda j: eg_plane.at[1, j])
    dg_a_copies = over_plane(1, lambda r: dg_a_sum.at[r], lambda j: dg_a_plane.at[j])
    landed(dg_b_copies)
    dg_b_sum[...] = total_of(dg_b[rank], [dg_b_in[j] for j in range(1, 16)])
    dg_b_copies = over_chan(6, lambda c: dg_b_sum.at[c], lambda j: dg_b_chan.at[j])

    def both(n, j, block):
        remote(block, block, both_send.at[n, j], both_recv.at[n, j], sibling)

    def gather(n):
        block = full.at[n, :, rank, half, :]
        for j in range(1, 16):
            remote(block, block, plane_send.at[4 + n, j], plane_recv.at[4 + n, j], plane_device(j))
        both(n, 0, block)

    def gathered(n):
        for j in range(1, 16):
            theirs = full.at[n, :, (rank - j + 16) % 16, half, :]
            describe(theirs, theirs, plane_send.at[4 + n, j], plane_recv.at[4 + n, j], plane_device(j)).wait_recv()
            both(n, j, theirs)

    def halves_landed(n):
        other = pl.ds(pl.multiple_of(32 - core * 32, 32), 32)
        for j in range(16):
            theirs = full.at[n, :, (rank - j + 16) % 16, other, :]
            describe(theirs, theirs, both_send.at[n, j], both_recv.at[n, j], sibling).wait_recv()

    landed(eg_copies)
    for n in range(2):
        eg_chan[chan, n] = total_of(eg_sum[16 * n + rank], [eg_plane[n, j] for j in range(1, 16)])
    over_chan(5, lambda c: eg_chan.at[chan], lambda j: eg_chan.at[chan])
    landed(dg_a_copies)
    landed(dg_b_copies)
    full[0, 0, rank, half, :] = total_of(dg_b_sum[chan], [dg_b_chan[j] for j in (1, 2, 3)]).astype(BF16)
    full[0, 1, rank, half, :] = total_of(dg_a_sum[rank], [dg_a_plane[j] for j in range(1, 16)]).astype(BF16)
    for j in (1, 2, 3):
        block = eg_chan.at[(chan - j + 4) % 4]
        describe(block, block, chan_send.at[5, j], chan_recv.at[5, j], chan_device(j)).wait_recv()
    for n in range(2):
        total = (eg_chan[0, n] + eg_chan[1, n]) + (eg_chan[2, n] + eg_chan[3, n])
        full[1, n, rank, half, :] = total.astype(BF16)
    gather(1)
    gather(0)
    gathered(1)
    gathered(0)
    halves_landed(1)
    halves_landed(0)

    landed(act_copies)
    for copy in sends:
        copy.wait_send()


def finish(act_hbm, grads_hbm, act_out, dg_out, eg_out, act_in, grads, sem):
    copies = [
        pltpu.make_async_copy(grads_hbm.at[0], grads.at[0], sem.at[0]),
        pltpu.make_async_copy(grads_hbm.at[1], grads.at[1], sem.at[1]),
        pltpu.make_async_copy(act_hbm, act_in, sem.at[2]),
    ]
    for copy in copies:
        copy.start()
    for n, out in enumerate((dg_out, eg_out)):
        copies[n].wait()
        for t in range(27):
            out[t] = grads[n, t // 15, t % 15].astype(F32)
    copies[2].wait()
    deep_channels_first(act_in, act_out)


def on_device(samples, early_filters, deep_filters, deep_cotangent):
    act, grads = pl.pallas_call(
        kernel,
        out_shape=(
            jax.ShapeDtypeStruct((16, 2, 64, 128), BF16),
            jax.ShapeDtypeStruct((2, 2, 16, 64, 128), BF16),
        ),
        in_specs=[pl.BlockSpec(memory_space=pltpu.VMEM)] + [pl.BlockSpec(memory_space=pl.ANY)] * 3,
        out_specs=[pl.BlockSpec(memory_space=pltpu.VMEM)] * 2,
        scratch_shapes=[
            pltpu.VMEM((4, 8, 64, 256), BF16),
            pltpu.VMEM((27, 64, 128), BF16),
            pltpu.VMEM((64, 2, 16, 128), BF16),
            pltpu.VMEM((16, 2, 64, 128), BF16),
            pltpu.VMEM((6, 10, 64, 256), BF16),
            pltpu.VMEM((6, 256, 1280), BF16),
            pltpu.VMEM((9, 256, 256), BF16),
            pltpu.VMEM((256, 512), BF16),
            pltpu.VMEM((4, 256, 1024), F32),
            pltpu.VMEM((2, 128, 512), F32),
            pltpu.VMEM((4, 384, 768), BF16),
            pltpu.VMEM((28, 256, 128), BF16),
            pltpu.VMEM((9, 384, 256), BF16),
            pltpu.VMEM((4, 2, 256, 128), BF16),
            pltpu.VMEM((2, 256, 512), F32),
            pltpu.VMEM((4, 2, 256, 128), BF16),
            pltpu.VMEM((2, 256, 1024), BF16),
            pltpu.VMEM((2, 128, 768), F32),
            pltpu.VMEM((2, 128, 768), BF16),
            pltpu.VMEM((2, 2, 128, 128), BF16),
            pltpu.VMEM((2, 128, 512), BF16),
            pltpu.VMEM((2, 2, 128, 128), BF16),
            pltpu.VMEM((2, 2, 128, 128), BF16),
            pltpu.VMEM((4, 256, 1024), BF16),
            pltpu.VMEM((2, 28, 4, 32, 128), BF16),
            pltpu.VMEM((28, 4, 32, 128), BF16),
            pltpu.VMEM((16, 4, 32, 128), BF16),
            pltpu.VMEM((16, 4, 32, 128), BF16),
            pltpu.VMEM((4, 32, 128), F32),
            pltpu.VMEM((4, 32, 128), F32),
            pltpu.VMEM((4, 12, 32, 128), BF16),
            pltpu.VMEM((4, 12, 32, 128), BF16),
            pltpu.VMEM((16, 32, 128), BF16),
            pltpu.VMEM((16, 32, 128), BF16),
            pltpu.VMEM((2, 28, 32, 128), BF16),
            pltpu.VMEM((28, 32, 128), BF16),
            pltpu.VMEM((32, 32, 128), BF16),
            pltpu.VMEM((2, 16, 32, 128), BF16),
            pltpu.VMEM((4, 2, 32, 128), F32),
            pltpu.SemaphoreType.DMA((3, 8)),
            pltpu.SemaphoreType.DMA((3, 8)),
            pltpu.SemaphoreType.DMA((4, 4)),
            pltpu.SemaphoreType.DMA((4, 4)),
            pltpu.SemaphoreType.DMA((7, 4)),
            pltpu.SemaphoreType.DMA((7, 4)),
            pltpu.SemaphoreType.DMA((3,)),
            pltpu.SemaphoreType.DMA((3,)),
            pltpu.SemaphoreType.DMA((6, 16)),
            pltpu.SemaphoreType.DMA((6, 16)),
            pltpu.SemaphoreType.DMA((2, 16)),
            pltpu.SemaphoreType.DMA((2, 16)),
            pltpu.SemaphoreType.DMA((3,)),
        ],
        compiler_params=pltpu.CompilerParams(
            collective_id=0, has_side_effects=True, vmem_limit_bytes=56 * 1024 * 1024
        ),
        name="conv_step",
    )(samples[0], early_filters.transpose(0, 2, 1), deep_filters, deep_cotangent[0])
    act, deep_grad, early_grad = pl.pallas_call(
        finish,
        out_shape=(
            jax.ShapeDtypeStruct((64, 2, 16, 128), BF16),
            jax.ShapeDtypeStruct((27, 64, 128), F32),
            jax.ShapeDtypeStruct((27, 64, 128), F32),
        ),
        in_specs=[pl.BlockSpec(memory_space=pl.ANY)] * 2,
        out_specs=[pl.BlockSpec(memory_space=pltpu.VMEM)] * 3,
        scratch_shapes=[
            pltpu.VMEM((16, 2, 64, 128), BF16),
            pltpu.VMEM((2, 2, 16, 64, 128), BF16),
            pltpu.SemaphoreType.DMA((3,)),
        ],
        compiler_params=pltpu.CompilerParams(vmem_limit_bytes=56 * 1024 * 1024),
        name="finish",
    )(act, grads)
    return act[None], deep_grad, early_grad.transpose(0, 2, 1)


def solution(mesh):
    placed = (
        P("dp", None, "space", "chan", None),
        P(),
        P(None, "chan", None),
        P("dp", "chan", "space", None, None),
    )
    return jax.shard_map(
        on_device,
        mesh=mesh,
        in_specs=placed,
        out_specs=(P("dp", "chan", "space", None, None), P(None, "chan", None), P()),
        check_vma=False,
    )
```

```python
import jax
import jax.numpy as jnp
from jax import lax
from jax.experimental import pallas as pl
from jax.experimental.pallas import tpu as pltpu
from jax.sharding import PartitionSpec as P

BF16 = jnp.bfloat16
F32 = jnp.float32
MESH = pl.DeviceIdType.MESH

SIDES = [(dx, dy) for dx in (-1, 0, 1) for dy in (-1, 0, 1) if (dx, dy) != (0, 0)]


def dot(a, b):
    return lax.dot_general(a, b, (((1,), (0,)), ((), ())), preferred_element_type=F32)


def dot_nt(a, b):
    return lax.dot_general(a, b, (((1,), (1,)), ((), ())), preferred_element_type=F32)


def selector(rows, cols, hit):
    row = lax.broadcasted_iota(jnp.int32, (rows, cols), 0)
    col = lax.broadcasted_iota(jnp.int32, (rows, cols), 1)
    return jnp.where(hit(row, col), 1.0, 0.0).astype(BF16)


def sigmoid(u):
    return 0.5 + 0.5 * jnp.tanh(0.5 * u)


def sent_and_landed(side, length):
    if side == 0:
        return (1, length), (1, length)
    if side == 1:
        return (length, 1), (0, 1)
    return (1, 1), (length + 1, 1)


def build_early_weights(ef, w9):
    eye = selector(128, 128, lambda r, c: r == c)
    none = jnp.zeros((64, 128), BF16)

    def body(i, carry):
        for ae in range(3):
            taps = [ef[9 * i + 3 * ae + f] for f in range(3)]
            for p in range(2):
                slots = [none] + taps if p else taps + [none]
                rows = slice(p * 128, (p + 1) * 128)
                w9[3 * i + ae, rows, :] = dot_nt(eye, jnp.concatenate(slots, axis=0)).astype(BF16)
        return carry

    lax.fori_loop(0, 3, body, 0)


def cells_first(samples_raw, samples):
    swap = selector(256, 256, lambda r, c: c == (r % 32) * 8 + r // 32)

    def body(x, carry):
        for n in range(2):
            block = samples_raw[n * 32 : (n + 1) * 32, x].astype(F32).reshape(256, 256).astype(BF16)
            block = dot(swap, block).astype(BF16)
            for y in range(8):
                samples[x, y, n * 32 : (n + 1) * 32, :] = block[y * 32 : (y + 1) * 32]
        return carry

    lax.fori_loop(0, 4, body, 0)


def row_swap():
    return selector(256, 256, lambda r, c: c == (r % 16) * 16 + r // 16)


def deep_cells_first(raw, out):
    swap = row_swap()
    for n in range(4):
        rows = slice(n * 16, (n + 1) * 16)
        block = jnp.concatenate([raw[rows, X].reshape(256, 128) for X in range(2)], axis=1)
        block = dot(swap, block).astype(BF16)
        for Y in range(16):
            for X in range(2):
                out[Y, X, rows, :] = block[Y * 16 : (Y + 1) * 16, X * 128 : (X + 1) * 128]


def deep_channels_first(raw, out):
    swap = row_swap()
    for n in range(4):
        rows = slice(n * 16, (n + 1) * 16)
        block = [jnp.concatenate([raw[Y, X, rows, :] for Y in range(16)], axis=0) for X in range(2)]
        block = dot(swap, jnp.concatenate(block, axis=1)).astype(BF16)
        for X in range(2):
            out[rows, X] = block[:, X * 128 : (X + 1) * 128].reshape(16, 16, 128)


def place_taps(block, spread, taps_in, x, first_y, count):
    wide = dot(block, spread[...]).astype(BF16)
    for y in range(count):
        for s in range(4):
            taps_in[x, s * 64 : (s + 1) * 64, pl.ds((first_y + y) * 128, 128)] = wide[
                y * 64 : (y + 1) * 64, s * 128 : (s + 1) * 128
            ]


def early_terms(taps_in, w9, x, Y, shifts):
    total = None
    for a in shifts:
        for e in range(3):
            term = dot(w9[3 * a + e], taps_in[x + a, :, (2 * Y + e) * 128 : (2 * Y + e + 2) * 128])
            total = term if total is None else total + term
    return total


def early_activation(pre, slopes, x, Y):
    s = sigmoid(pre)
    slopes[x, :, Y * 256 : (Y + 1) * 256] = s * (1.0 + pre * (1.0 - s))
    act = pre * s
    act = act[:128] + act[128:]
    return act[:, :128] + act[:, 128:]


def early_inner(taps_in, w9, slopes, pool_sum, Ys):
    for Y in Ys:
        for x, shifts in ((0, (1, 2)), (3, (0, 1))):
            slopes[x, :, Y * 256 : (Y + 1) * 256] = early_terms(taps_in, w9, x, Y, shifts)
        for X, x in enumerate((1, 2)):
            pre = early_terms(taps_in, w9, x, Y, (0, 1, 2))
            pool_sum[X, :, Y * 128 : (Y + 1) * 128] = early_activation(pre, slopes, x, Y)


def early_outer(taps_in, w9, slopes, pool_sum, pooled, X):
    x, a = ((0, 0), (3, 2))[X]
    for Y in range(4):
        pre = slopes[x, :, Y * 256 : (Y + 1) * 256] + early_terms(taps_in, w9, x, Y, (a,))
        total = pool_sum[X, :, Y * 128 : (Y + 1) * 128] + early_activation(pre, slopes, x, Y)
        pooled[X + 1, 128:256, (Y + 1) * 128 : (Y + 2) * 128] = (total * 0.125).astype(BF16)


def shift_pooled(pooled, xs, first, count):
    shifts = selector(128, 256, lambda r, c: r == jnp.where(c < 128, c - 1, c - 127))
    for x in xs:
        blocks = [pooled[x, 128:256, (first + y) * 128 : (first + y + 1) * 128] for y in range(count)]
        both = dot(jnp.concatenate(blocks, axis=0), shifts).astype(BF16)
        for y in range(count):
            lanes = slice((first + y) * 128, (first + y + 1) * 128)
            rows = slice(y * 128, (y + 1) * 128)
            pooled[x, 0:128, lanes] = both[rows, :128]
            pooled[x, 256:384, lanes] = both[rows, 128:]


def transpose_deep_weights(wd, wdt):
    eye = selector(128, 128, lambda r, c: r == c)

    def body(i, carry):
        for ae in range(3):
            for f in range(3):
                rows = slice(f * 128, (f + 1) * 128)
                wdt[3 * i + ae, rows, :] = dot_nt(eye, wd[9 * i + 3 * ae + f]).astype(BF16)
        return carry

    lax.fori_loop(0, 3, body, 0)


def deep_terms(pooled, wd, X, h, shifts):
    total = None
    for a in shifts:
        for e in range(3):
            weights = jnp.concatenate([wd[9 * a + 3 * e + f] for f in range(3)], axis=1)
            term = dot(weights, pooled[X + a, :, h * 256 + e * 128 : h * 256 + e * 128 + 256])
            total = term if total is None else total + term
    return total


def deep_inner(pooled, wd, pre_deep):
    for h in range(2):
        for X, shifts in ((0, (1, 2)), (1, (0, 1))):
            pre_deep[X, :, h * 256 : (h + 1) * 256] = deep_terms(pooled, wd, X, h, shifts)


def deep_outer(pooled, wd, ct, pre_deep, act, deep_in):
    for X, a in ((0, 0), (1, 2)):
        for h in range(2):
            pre = pre_deep[X, :, h * 256 : (h + 1) * 256] + deep_terms(pooled, wd, X, h, (a,))
            s = sigmoid(pre)
            value = (pre * s).astype(BF16)
            slope = s * (1.0 + pre * (1.0 - s))
            for k in range(2):
                Y, part = 2 * h + k, slice(k * 128, (k + 1) * 128)
                act[Y, X] = value[:, part]
                deep_in[X, :, (Y + 2) * 128 : (Y + 3) * 128] = (ct[Y, X].astype(F32) * slope[:, part]).astype(BF16)


def pooled_terms(deep_in, wdt, pairs, first):
    column = lax.broadcasted_iota(jnp.int32, (128, 128), 1)
    total = None
    for X, a in pairs:
        for e in range(3):
            lanes = slice((first + 2 - e) * 128, (first + 4 - e) * 128)
            term = dot(wdt[3 * a + e], deep_in[X, :, lanes])
            total = term if total is None else total + term
    parts = []
    for k in range(2):
        part = total[:, k * 128 : (k + 1) * 128]
        grad = part[128:256]
        grad += jnp.where(column < 127, pltpu.roll(part[0:128], 127, 1), 0.0)
        grad += jnp.where(column > 0, pltpu.roll(part[256:384], 1, 1), 0.0)
        parts.append(grad)
    return jnp.concatenate(parts, axis=1)


def pooled_outer(deep_in, wdt, send_x, n):
    for first in (0, 2, 4):
        terms = pooled_terms(deep_in, wdt, (((0, 0),), ((1, 2),))[n], first)
        send_x[n, :, first * 128 : (first + 2) * 128] = terms.astype(BF16)


def pooled_inner(deep_in, wdt, pooled_grad, firsts):
    for X, pairs in enumerate((((0, 1), (1, 0)), ((0, 2), (1, 1)))):
        for first in firsts:
            pooled_grad[X, :, first * 128 : (first + 2) * 128] = pooled_terms(deep_in, wdt, pairs, first)


def early_cotangent(pooled_grad, got_x, got_y, got_xy, slopes, early_in):
    for X in range(2):
        grad = pooled_grad[X, :, 128:640] + got_x[X].astype(F32)
        for Y in range(4):
            here = grad[:, Y * 128 : (Y + 1) * 128]
            if Y in (0, 3):
                here += got_y[Y // 3, X].astype(F32) + got_xy[X, Y // 3].astype(F32)
            here *= 0.125
            for x in (2 * X, 2 * X + 1):
                for y in (2 * Y, 2 * Y + 1):
                    lanes = slice(y * 128, (y + 1) * 128)
                    for p in range(2):
                        rows = slice(p * 128, (p + 1) * 128)
                        early_in[x, rows, lanes] = (here * slopes[x, rows, lanes]).astype(BF16)


def slot(ae, f):
    return 3 * ae + f + ae // 5


def deep_gradient(deep_in, pooled, out):
    for ae in range(9):
        a, e = ae // 3, ae % 3
        total = None
        for X in range(2):
            term = dot_nt(deep_in[X, :, 256:768], pooled[X + a, :, e * 128 : e * 128 + 512])
            total = term if total is None else total + term
        for f in range(3):
            tap = total[:, f * 128 : (f + 1) * 128].astype(BF16).reshape(4, 2, 32, 128)
            for h in range(2):
                out[h, slot(ae, f)] = tap[:, h]


def early_gradient(early_in, taps_in, out, first, last):
    for ae in range(first, last):
        a, e = ae // 3, ae % 3
        total = None
        for x in range(4):
            term = dot_nt(taps_in[x + a, :, e * 128 : e * 128 + 1024], early_in[x])
            total = term if total is None else total + term
        total = (total[:192, :128] + total[64:, 128:]).astype(BF16)
        for f in range(3):
            for h in range(2):
                out[h, slot(ae, f)] = total[f * 64 + h * 32 : f * 64 + h * 32 + 32]


def add_taps(first, last, out, terms):
    def body(t, carry):
        total = None
        for term in terms:
            value = term(t).astype(F32)
            total = value if total is None else total + value
        out(t, total.astype(BF16))
        return carry

    lax.fori_loop(first, last, body, 0)


def total_of(own, others):
    total = own.astype(F32)
    for other in others:
        total += other.astype(F32)
    return total


def kernel(
    samples_raw, ef_hbm, wd_hbm, ct_hbm,
    act_in, full,
    samples, ef, ct_raw, ct_own, sample_ext, taps_in, w9, spread, slopes, pool_sum, pooled, wd, wdt, ct, pre_deep, act, deep_in,
    pooled_grad, send_x, send_y, got_x, got_y, got_xy, early_in,
    dg, dg_pair, dg_b, dg_b_in, dg_b_sum, dg_b_chan, dg_a, dg_a_in, dg_a_sum, dg_a_plane,
    eg, eg_pair, eg_sum, eg_plane, eg_chan,
    halo_send, halo_recv, x_send, x_recv, piece_send, piece_recv, chan_send, chan_recv, pair_send, pair_recv, plane_send, plane_recv, both_send, both_recv, load_sem,
):
    dp, space, chan = lax.axis_index("dp"), lax.axis_index("space"), lax.axis_index("chan")
    core, column = space % 2, space // 2
    rank = column * 2 + dp

    def side_device(dx, dy):
        return {"dp": dp, "space": (space + dx + 16) % 16, "chan": (chan + dy + 4) % 4}

    def chan_device(j):
        return {"dp": dp, "space": space, "chan": (chan + j) % 4}

    def x_device(j):
        return {"dp": dp, "space": (space + 4 * j) % 16, "chan": chan}

    def plane_device(j):
        r = (rank + j) % 16
        return {"dp": r % 2, "space": (r // 2) * 2 + core, "chan": chan}

    sibling = {"dp": dp, "space": column * 2 + 1 - core, "chan": chan}

    barrier = pltpu.get_barrier_semaphore()
    peers = [side_device(dx, dy) for dx, dy in SIDES]
    peers += [chan_device(2), sibling] + [plane_device(j) for j in range(1, 16)]
    for peer in peers:
        pl.semaphore_signal(barrier, inc=1, device_id=peer, device_id_type=MESH)

    mine = pl.ds(pl.multiple_of(chan * 64, 64), 64)
    half = pl.ds(pl.multiple_of(core * 32, 32), 32)
    loads = [
        pltpu.make_async_copy(src, dst, load_sem.at[n])
        for n, (src, dst) in enumerate(((ef_hbm, ef), (ct_hbm, ct_raw), (wd_hbm, wd.at[pl.ds(0, 27), mine, :])))
    ]
    for load in loads:
        load.start()
    cells_first(samples_raw, samples)
    loads[0].wait()
    build_early_weights(ef, w9)
    spread[...] = selector(256, 512, lambda r, c: r == 2 * (c % 128) + c // 128 - 1)
    loads[1].wait()
    deep_cells_first(ct_raw, ct_own)
    ct[:, :, mine, :] = ct_own[pl.ds(pl.multiple_of(chan * 4, 4), 4)]
    loads[2].wait()
    wd[27, mine, :] = jnp.zeros((64, 128), BF16)

    pl.semaphore_wait(barrier, len(peers))

    sends = []

    def describe(src, dst, send_sem, recv_sem, device):
        return pltpu.make_async_remote_copy(
            src_ref=src, dst_ref=dst, send_sem=send_sem, recv_sem=recv_sem, device_id=device, device_id_type=MESH
        )

    def remote(*args):
        copy = describe(*args)
        copy.start()
        sends.append(copy)
        return copy

    def landed(copies):
        for copy in copies:
            copy.wait_recv()

    def over_chan(n, src, dst):
        return [
            remote(src((chan + j) % 4), dst(j), chan_send.at[n, j], chan_recv.at[n, j], chan_device(j)) for j in (1, 2, 3)
        ]

    def pair(n, src, dst):
        return remote(src, dst, pair_send.at[n], pair_recv.at[n], sibling)

    def halo(n, view, dxs):
        copies = []
        for dx in dxs:
            for dy in (-1, 0, 1):
                if (dx, dy) != (0, 0):
                    src, dst = view(dx, dy)
                    k = SIDES.index((dx, dy))
                    copies.append(remote(src, dst, halo_send.at[n, k], halo_recv.at[n, k], side_device(dx, dy)))
        return copies

    def sample_view(dx, dy):
        (sx, nx), (tx, _) = sent_and_landed(dx, 4)
        (sy, ny), (ty, _) = sent_and_landed(dy, 8)
        src = samples.at[pl.ds(sx - 1, nx), pl.ds(sy - 1, ny)]
        return src, sample_ext.at[pl.ds(tx, nx), pl.ds(ty, ny)]

    def field_view(ref, first, rows):
        def view(dx, dy):
            (sx, nx), (tx, _) = sent_and_landed(dx, 2)
            (sy, ny), (ty, _) = sent_and_landed(dy, 4)
            block = pl.ds(first, rows)
            src = ref.at[pl.ds(sx, nx), block, pl.ds(sy * 128, ny * 128)]
            return src, ref.at[pl.ds(tx, nx), block, pl.ds(ty * 128, ny * 128)]

        return view

    def clear_y(ref, xs, rows, lanes):
        width = ref.shape[2]
        for at, span in ((0, slice(0, lanes)), (3, slice(width - lanes, width))):

            @pl.when(chan == at)
            def _():
                for x in xs:
                    ref[x, rows, span] = jnp.zeros((rows.stop - rows.start, lanes), BF16)

    def clear_x(ref, rows):
        width = ref.shape[2]
        for at, x in ((0, 0), (15, ref.shape[0] - 1)):

            @pl.when(space == at)
            def _():
                ref[x, rows, :] = jnp.zeros((rows.stop - rows.start, width), BF16)

    sample_y = halo(0, sample_view, (0,))
    sample_x = halo(0, sample_view, (-1, 1))

    def some_of(c, taps, of_core):
        return wd.at[taps, pl.ds(pl.multiple_of(c * 64 + of_core * 32, 32), 32), :]

    my_taps = pl.ds(space // 4 * 7, 7)
    wd_copies = over_chan(0, lambda c: some_of(chan, my_taps, core), lambda j: some_of(chan, my_taps, core))
    for x in range(4):
        place_taps(samples[x].reshape(512, 256), spread, taps_in, x + 1, 1, 8)
    for h in range(2):
        dg[h, 15] = jnp.zeros((4, 32, 128), BF16)
        eg[h, 15] = jnp.zeros((32, 128), BF16)
    dg_a_sum[12:16] = jnp.zeros((4, 32, 128), BF16)
    eg_sum[28:32] = jnp.zeros((4, 32, 128), BF16)
    for X in range(2):
        for lanes in (slice(0, 256), slice(768, 1024)):
            deep_in[X, :, lanes] = jnp.zeros((256, 256), BF16)

    early_inner(taps_in, w9, slopes, pool_sum, (1, 2))
    landed(sample_y)
    for y in (0, 9):
        for x in range(1, 5):
            place_taps(sample_ext[x, y], spread, taps_in, x, y, 1)
    clear_y(taps_in, range(1, 5), slice(0, 256), 128)
    for j, copy in zip((1, 2, 3), wd_copies):
        landed([copy])
        block = some_of((chan - j + 4) % 4, my_taps, core)
        for i in (1, 2, 3):
            remote(block, block, x_send.at[j, i], x_recv.at[j, i], x_device(i))
        remote(block, block, piece_send.at[j, 0], piece_recv.at[j, 0], sibling)
    ct_copies = over_chan(
        1, lambda c: ct_own.at[pl.ds(pl.multiple_of(c * 4, 4), 4)], lambda j: ct.at[:, :, mine, :]
    )
    early_inner(taps_in, w9, slopes, pool_sum, (0, 3))
    landed(sample_x)
    for x in (0, 5):
        place_taps(sample_ext[x].reshape(640, 256), spread, taps_in, x, 0, 10)
    clear_y(taps_in, (0, 5), slice(0, 256), 128)
    clear_x(taps_in, slice(0, 256))
    early_outer(taps_in, w9, slopes, pool_sum, pooled, 0)
    pooled_x = halo(1, field_view(pooled, 128, 128), (-1,))
    early_outer(taps_in, w9, slopes, pool_sum, pooled, 1)
    pooled_x += halo(1, field_view(pooled, 128, 128), (1,))
    pooled_y = halo(1, field_view(pooled, 128, 128), (0,))
    shift_pooled(pooled, (1, 2), 1, 4)
    for j in (1, 2, 3):
        for i in (1, 2, 3):
            block = some_of((chan - j + 4) % 4, pl.ds((space // 4 - i + 4) % 4 * 7, 7), core)
            describe(block, block, x_send.at[j, i], x_recv.at[j, i], x_device(i)).wait_recv()
            remote(block, block, piece_send.at[j, i], piece_recv.at[j, i], sibling)
    landed(pooled_y)
    clear_y(pooled, (1, 2), slice(128, 256), 128)
    shift_pooled(pooled, (1, 2), 0, 1)
    shift_pooled(pooled, (1, 2), 5, 1)
    for j in (1, 2, 3):
        for i in range(4):
            block = some_of((chan - j + 4) % 4, pl.ds((space // 4 - i + 4) % 4 * 7, 7), 1 - core)
            describe(block, block, piece_send.at[j, i], piece_recv.at[j, i], sibling).wait_recv()
    deep_inner(pooled, wd, pre_deep)
    transpose_deep_weights(wd, wdt)
    landed(pooled_x)
    clear_y(pooled, (0, 3), slice(128, 256), 128)
    clear_x(pooled, slice(128, 256))
    shift_pooled(pooled, (0, 3), 0, 6)
    landed(ct_copies)
    deep_outer(pooled, wd, ct, pre_deep, act, deep_in)

    grad_copies = []
    for n, dx in enumerate((-1, 1)):
        pooled_outer(deep_in, wdt, send_x, n)
        for dy in (-1, 0, 1):
            at, count = {-1: (0, 1), 0: (1, 4), 1: (5, 1)}[dy]
            src = send_x.at[n, :, pl.ds(at * 128, count * 128)]
            dst = got_x.at[1 - n] if dy == 0 else got_xy.at[1 - n, 0 if dy > 0 else 1]
            k = SIDES.index((dx, dy))
            grad_copies.append(remote(src, dst, halo_send.at[2, k], halo_recv.at[2, k], side_device(dx, dy)))
    pooled_inner(deep_in, wdt, pooled_grad, (0, 4))
    for n, (dy, at) in enumerate(((-1, 0), (1, 5))):
        for X in range(2):
            send_y[n, X] = pooled_grad[X, :, at * 128 : (at + 1) * 128].astype(BF16)
        k = SIDES.index((0, dy))
        grad_copies.append(
            remote(send_y.at[n], got_y.at[1 - n], halo_send.at[2, k], halo_recv.at[2, k], side_device(0, dy))
        )

    here = pl.ds(pl.multiple_of(chan * 4, 4), 4)
    act_copies = over_chan(
        4, lambda c: act.at[:, :, pl.ds(pl.multiple_of(c * 64, 64), 64), :], lambda j: act_in.at[here]
    )
    act_in[here] = act[:, :, mine, :]

    def over_plane(n, src, dst):
        return [
            remote(src((rank + j) % 16), dst(j), plane_send.at[n, j], plane_recv.at[n, j], plane_device(j))
            for j in range(1, 16)
        ]

    deep_gradient(deep_in, pooled, dg)
    dg_pair_copy = pair(0, dg.at[1 - core, pl.ds(0, 28)], dg_pair)
    pooled_inner(deep_in, wdt, pooled_grad, (2,))
    landed(grad_copies)
    for at, n in ((0, 0), (15, 1)):

        @pl.when(space == at)
        def _():
            got_x[n] = jnp.zeros((128, 512), BF16)
            got_xy[n] = jnp.zeros((2, 128, 128), BF16)

    for at, n in ((0, 0), (3, 1)):

        @pl.when(chan == at)
        def _():
            got_y[n] = jnp.zeros((2, 128, 128), BF16)
            for m in range(2):
                got_xy[m, n] = jnp.zeros((128, 128), BF16)

    early_cotangent(pooled_grad, got_x, got_y, got_xy, slopes, early_in)
    landed([dg_pair_copy])

    def put_b(t, value):
        dg_b[t] = value

    def put_a(t, value):
        dg_a[:, t - 16] = value

    add_taps(16, 28, put_a, [lambda t: dg[core, t], lambda t: dg_pair[t]])
    dg_a_copies = over_chan(3, lambda c: dg_a.at[c], lambda j: dg_a_in.at[j])
    add_taps(0, 16, put_b, [lambda t: dg[core, t], lambda t: dg_pair[t]])
    dg_b_copies = over_plane(0, lambda r: dg_b.at[r], lambda j: dg_b_in.at[j])
    early_gradient(early_in, taps_in, eg, 0, 5)
    eg_pair_0 = pair(1, eg.at[1 - core, pl.ds(0, 16)], eg_pair.at[pl.ds(0, 16)])
    early_gradient(early_in, taps_in, eg, 5, 7)

    def put_eg(t, value):
        eg_sum[t] = value

    landed([eg_pair_0])
    add_taps(0, 16, put_eg, [lambda t: eg[core, t], lambda t: eg_pair[t]])
    eg_copies = [over_plane(2, lambda r: eg_sum.at[r], lambda j: eg_plane.at[0, j])]
    early_gradient(early_in, taps_in, eg, 7, 9)
    eg_pair_1 = pair(2, eg.at[1 - core, pl.ds(16, 12)], eg_pair.at[pl.ds(16, 12)])

    def put_a_sum(t, value):
        dg_a_sum[t] = value

    landed(dg_a_copies)
    add_taps(0, 12, put_a_sum, [lambda t: dg_a[chan, t]] + [lambda t, j=j: dg_a_in[j, t] for j in (1, 2, 3)])
    landed([eg_pair_1])
    add_taps(16, 28, put_eg, [lambda t: eg[core, t], lambda t: eg_pair[t]])
    eg_copies.append(over_plane(3, lambda r: eg_sum.at[16 + r], lambda j: eg_plane.at[1, j]))
    dg_a_copies = over_plane(1, lambda r: dg_a_sum.at[r], lambda j: dg_a_plane.at[j])
    landed(dg_b_copies)
    dg_b_sum[...] = total_of(dg_b[rank], [dg_b_in[j] for j in range(1, 16)])
    dg_b_copies = over_chan(6, lambda c: dg_b_sum.at[c], lambda j: dg_b_chan.at[j])

    def both(n, j, block):
        remote(block, block, both_send.at[n, j], both_recv.at[n, j], sibling)

    def gather(n):
        block = full.at[n, :, rank, half, :]
        for j in range(1, 16):
            remote(block, block, plane_send.at[4 + n, j], plane_recv.at[4 + n, j], plane_device(j))
        both(n, 0, block)

    def gathered(n):
        for j in range(1, 16):
            theirs = full.at[n, :, (rank - j + 16) % 16, half, :]
            describe(theirs, theirs, plane_send.at[4 + n, j], plane_recv.at[4 + n, j], plane_device(j)).wait_recv()
            both(n, j, theirs)

    def halves_landed(n):
        other = pl.ds(pl.multiple_of(32 - core * 32, 32), 32)
        for j in range(16):
            theirs = full.at[n, :, (rank - j + 16) % 16, other, :]
            describe(theirs, theirs, both_send.at[n, j], both_recv.at[n, j], sibling).wait_recv()

    def chan_terms(n):
        landed(eg_copies[n])
        eg_chan[chan, n] = total_of(eg_sum[16 * n + rank], [eg_plane[n, j] for j in range(1, 16)])
        over_chan((5, 2)[n], lambda c: eg_chan.at[chan, n], lambda j: eg_chan.at[chan, n])

    def chan_total(n):
        for j in (1, 2, 3):
            block = eg_chan.at[(chan - j + 4) % 4, n]
            k = (5, 2)[n]
            describe(block, block, chan_send.at[k, j], chan_recv.at[k, j], chan_device(j)).wait_recv()
        total = (eg_chan[0, n] + eg_chan[1, n]) + (eg_chan[2, n] + eg_chan[3, n])
        full[1, n, rank, half, :] = total.astype(BF16)

    chan_terms(0)
    landed(dg_b_copies)
    full[0, 0, rank, half, :] = total_of(dg_b_sum[chan], [dg_b_chan[j] for j in (1, 2, 3)]).astype(BF16)
    landed(dg_a_copies)
    full[0, 1, rank, half, :] = total_of(dg_a_sum[rank], [dg_a_plane[j] for j in range(1, 16)]).astype(BF16)
    gather(0)
    chan_terms(1)
    chan_total(0)
    chan_total(1)
    gather(1)
    gathered(0)
    gathered(1)
    halves_landed(0)
    halves_landed(1)

    landed(act_copies)
    for copy in sends:
        copy.wait_send()


def finish(act_hbm, grads_hbm, act_out, dg_out, eg_out, act_in, grads, sem):
    copies = [
        pltpu.make_async_copy(grads_hbm.at[0], grads.at[0], sem.at[0]),
        pltpu.make_async_copy(grads_hbm.at[1], grads.at[1], sem.at[1]),
        pltpu.make_async_copy(act_hbm, act_in, sem.at[2]),
    ]
    for copy in copies:
        copy.start()
    for n, out in enumerate((dg_out, eg_out)):
        copies[n].wait()
        for t in range(27):
            out[t] = grads[n, t // 15, t % 15].astype(F32)
    copies[2].wait()
    deep_channels_first(act_in, act_out)


def on_device(samples, early_filters, deep_filters, deep_cotangent):
    act, grads = pl.pallas_call(
        kernel,
        out_shape=(
            jax.ShapeDtypeStruct((16, 2, 64, 128), BF16),
            jax.ShapeDtypeStruct((2, 2, 16, 64, 128), BF16),
        ),
        in_specs=[pl.BlockSpec(memory_space=pltpu.VMEM)] + [pl.BlockSpec(memory_space=pl.ANY)] * 3,
        out_specs=[pl.BlockSpec(memory_space=pltpu.VMEM)] * 2,
        scratch_shapes=[
            pltpu.VMEM((4, 8, 64, 256), BF16),
            pltpu.VMEM((27, 64, 128), BF16),
            pltpu.VMEM((64, 2, 16, 128), BF16),
            pltpu.VMEM((16, 2, 64, 128), BF16),
            pltpu.VMEM((6, 10, 64, 256), BF16),
            pltpu.VMEM((6, 256, 1280), BF16),
            pltpu.VMEM((9, 256, 256), BF16),
            pltpu.VMEM((256, 512), BF16),
            pltpu.VMEM((4, 256, 1024), F32),
            pltpu.VMEM((2, 128, 512), F32),
            pltpu.VMEM((4, 384, 768), BF16),
            pltpu.VMEM((28, 256, 128), BF16),
            pltpu.VMEM((9, 384, 256), BF16),
            pltpu.VMEM((4, 2, 256, 128), BF16),
            pltpu.VMEM((2, 256, 512), F32),
            pltpu.VMEM((4, 2, 256, 128), BF16),
            pltpu.VMEM((2, 256, 1024), BF16),
            pltpu.VMEM((2, 128, 768), F32),
            pltpu.VMEM((2, 128, 768), BF16),
            pltpu.VMEM((2, 2, 128, 128), BF16),
            pltpu.VMEM((2, 128, 512), BF16),
            pltpu.VMEM((2, 2, 128, 128), BF16),
            pltpu.VMEM((2, 2, 128, 128), BF16),
            pltpu.VMEM((4, 256, 1024), BF16),
            pltpu.VMEM((2, 28, 4, 32, 128), BF16),
            pltpu.VMEM((28, 4, 32, 128), BF16),
            pltpu.VMEM((16, 4, 32, 128), BF16),
            pltpu.VMEM((16, 4, 32, 128), BF16),
            pltpu.VMEM((4, 32, 128), F32),
            pltpu.VMEM((4, 32, 128), F32),
            pltpu.VMEM((4, 12, 32, 128), BF16),
            pltpu.VMEM((4, 12, 32, 128), BF16),
            pltpu.VMEM((16, 32, 128), BF16),
            pltpu.VMEM((16, 32, 128), BF16),
            pltpu.VMEM((2, 28, 32, 128), BF16),
            pltpu.VMEM((28, 32, 128), BF16),
            pltpu.VMEM((32, 32, 128), BF16),
            pltpu.VMEM((2, 16, 32, 128), BF16),
            pltpu.VMEM((4, 2, 32, 128), F32),
            pltpu.SemaphoreType.DMA((3, 8)),
            pltpu.SemaphoreType.DMA((3, 8)),
            pltpu.SemaphoreType.DMA((4, 4)),
            pltpu.SemaphoreType.DMA((4, 4)),
            pltpu.SemaphoreType.DMA((4, 4)),
            pltpu.SemaphoreType.DMA((4, 4)),
            pltpu.SemaphoreType.DMA((7, 4)),
            pltpu.SemaphoreType.DMA((7, 4)),
            pltpu.SemaphoreType.DMA((3,)),
            pltpu.SemaphoreType.DMA((3,)),
            pltpu.SemaphoreType.DMA((6, 16)),
            pltpu.SemaphoreType.DMA((6, 16)),
            pltpu.SemaphoreType.DMA((2, 16)),
            pltpu.SemaphoreType.DMA((2, 16)),
            pltpu.SemaphoreType.DMA((3,)),
        ],
        compiler_params=pltpu.CompilerParams(
            collective_id=0, has_side_effects=True, vmem_limit_bytes=56 * 1024 * 1024
        ),
        name="conv_step",
    )(samples[0], early_filters.transpose(0, 2, 1), deep_filters, deep_cotangent[0])
    act, deep_grad, early_grad = pl.pallas_call(
        finish,
        out_shape=(
            jax.ShapeDtypeStruct((64, 2, 16, 128), BF16),
            jax.ShapeDtypeStruct((27, 64, 128), F32),
            jax.ShapeDtypeStruct((27, 64, 128), F32),
        ),
        in_specs=[pl.BlockSpec(memory_space=pl.ANY)] * 2,
        out_specs=[pl.BlockSpec(memory_space=pltpu.VMEM)] * 3,
        scratch_shapes=[
            pltpu.VMEM((16, 2, 64, 128), BF16),
            pltpu.VMEM((2, 2, 16, 64, 128), BF16),
            pltpu.SemaphoreType.DMA((3,)),
        ],
        compiler_params=pltpu.CompilerParams(vmem_limit_bytes=56 * 1024 * 1024),
        name="finish",
    )(act, grads)
    return act[None], deep_grad, early_grad.transpose(0, 2, 1)


def solution(mesh):
    placed = (
        P("dp", None, "space", "chan", None),
        P(),
        P(None, "chan", None),
        P("dp", "chan", "space", None, None),
    )
    return jax.shard_map(
        on_device,
        mesh=mesh,
        in_specs=placed,
        out_specs=(P("dp", "chan", "space", None, None), P(None, "chan", None), P()),
        check_vma=False,
    )
```

```python
import jax
import jax.numpy as jnp
from jax import lax
from jax.experimental import pallas as pl
from jax.experimental.pallas import tpu as pltpu
from jax.sharding import PartitionSpec as P

BF16 = jnp.bfloat16
F32 = jnp.float32
MESH = pl.DeviceIdType.MESH

SIDES = [(dx, dy) for dx in (-1, 0, 1) for dy in (-1, 0, 1) if (dx, dy) != (0, 0)]


def dot(a, b):
    return lax.dot_general(a, b, (((1,), (0,)), ((), ())), preferred_element_type=F32)


def dot_nt(a, b):
    return lax.dot_general(a, b, (((1,), (1,)), ((), ())), preferred_element_type=F32)


def selector(rows, cols, hit):
    row = lax.broadcasted_iota(jnp.int32, (rows, cols), 0)
    col = lax.broadcasted_iota(jnp.int32, (rows, cols), 1)
    return jnp.where(hit(row, col), 1.0, 0.0).astype(BF16)


def sigmoid(u):
    return 0.5 + 0.5 * jnp.tanh(0.5 * u)


def sent_and_landed(side, length):
    if side == 0:
        return (1, length), (1, length)
    if side == 1:
        return (length, 1), (0, 1)
    return (1, 1), (length + 1, 1)


def build_early_weights(ef, w9):
    eye = selector(128, 128, lambda r, c: r == c)
    none = jnp.zeros((64, 128), BF16)

    def body(i, carry):
        for ae in range(3):
            taps = [ef[9 * i + 3 * ae + f] for f in range(3)]
            for p in range(2):
                slots = [none] + taps if p else taps + [none]
                rows = slice(p * 128, (p + 1) * 128)
                w9[3 * i + ae, rows, :] = dot_nt(eye, jnp.concatenate(slots, axis=0)).astype(BF16)
        return carry

    lax.fori_loop(0, 3, body, 0)


def cells_first(samples_raw, samples):
    swap = selector(256, 256, lambda r, c: c == (r % 32) * 8 + r // 32)

    def body(x, carry):
        for n in range(2):
            block = samples_raw[n * 32 : (n + 1) * 32, x].astype(F32).reshape(256, 256).astype(BF16)
            block = dot(swap, block).astype(BF16)
            for y in range(8):
                samples[x, y, n * 32 : (n + 1) * 32, :] = block[y * 32 : (y + 1) * 32]
        return carry

    lax.fori_loop(0, 4, body, 0)


def row_swap():
    return selector(256, 256, lambda r, c: c == (r % 16) * 16 + r // 16)


def deep_cells_first(raw, out):
    swap = row_swap()
    for n in range(4):
        rows = slice(n * 16, (n + 1) * 16)
        block = jnp.concatenate([raw[rows, X].reshape(256, 128) for X in range(2)], axis=1)
        block = dot(swap, block).astype(BF16)
        for Y in range(16):
            for X in range(2):
                out[Y, X, rows, :] = block[Y * 16 : (Y + 1) * 16, X * 128 : (X + 1) * 128]


def deep_channels_first(raw, out):
    swap = row_swap()
    for n in range(4):
        rows = slice(n * 16, (n + 1) * 16)
        block = [jnp.concatenate([raw[Y, X, rows, :] for Y in range(16)], axis=0) for X in range(2)]
        block = dot(swap, jnp.concatenate(block, axis=1)).astype(BF16)
        for X in range(2):
            out[rows, X] = block[:, X * 128 : (X + 1) * 128].reshape(16, 16, 128)


def place_taps(block, spread, taps_in, x, first_y, count):
    wide = dot(block, spread[...]).astype(BF16)
    for y in range(count):
        for s in range(4):
            taps_in[x, s * 64 : (s + 1) * 64, pl.ds((first_y + y) * 128, 128)] = wide[
                y * 64 : (y + 1) * 64, s * 128 : (s + 1) * 128
            ]


def early_terms(taps_in, w9, x, Y, shifts):
    total = None
    for a in shifts:
        for e in range(3):
            term = dot(w9[3 * a + e], taps_in[x + a, :, (2 * Y + e) * 128 : (2 * Y + e + 2) * 128])
            total = term if total is None else total + term
    return total


def early_activation(pre, slopes, x, Y):
    s = sigmoid(pre)
    slopes[x, :, Y * 256 : (Y + 1) * 256] = s * (1.0 + pre * (1.0 - s))
    act = pre * s
    act = act[:128] + act[128:]
    return act[:, :128] + act[:, 128:]


def early_inner(taps_in, w9, slopes, pool_sum, Ys):
    for Y in Ys:
        for x, shifts in ((0, (1, 2)), (3, (0, 1))):
            slopes[x, :, Y * 256 : (Y + 1) * 256] = early_terms(taps_in, w9, x, Y, shifts)
        for X, x in enumerate((1, 2)):
            pre = early_terms(taps_in, w9, x, Y, (0, 1, 2))
            pool_sum[X, :, Y * 128 : (Y + 1) * 128] = early_activation(pre, slopes, x, Y)


def early_outer(taps_in, w9, slopes, pool_sum, pooled, X):
    x, a = ((0, 0), (3, 2))[X]
    for Y in range(4):
        pre = slopes[x, :, Y * 256 : (Y + 1) * 256] + early_terms(taps_in, w9, x, Y, (a,))
        total = pool_sum[X, :, Y * 128 : (Y + 1) * 128] + early_activation(pre, slopes, x, Y)
        pooled[X + 1, 128:256, (Y + 1) * 128 : (Y + 2) * 128] = (total * 0.125).astype(BF16)


def shift_pooled(pooled, xs, first, count):
    shifts = selector(128, 256, lambda r, c: r == jnp.where(c < 128, c - 1, c - 127))
    for x in xs:
        blocks = [pooled[x, 128:256, (first + y) * 128 : (first + y + 1) * 128] for y in range(count)]
        both = dot(jnp.concatenate(blocks, axis=0), shifts).astype(BF16)
        for y in range(count):
            lanes = slice((first + y) * 128, (first + y + 1) * 128)
            rows = slice(y * 128, (y + 1) * 128)
            pooled[x, 0:128, lanes] = both[rows, :128]
            pooled[x, 256:384, lanes] = both[rows, 128:]


def transpose_deep_weights(wd, wdt):
    eye = selector(128, 128, lambda r, c: r == c)

    def body(i, carry):
        for ae in range(3):
            for f in range(3):
                rows = slice(f * 128, (f + 1) * 128)
                wdt[3 * i + ae, rows, :] = dot_nt(eye, wd[9 * i + 3 * ae + f]).astype(BF16)
        return carry

    lax.fori_loop(0, 3, body, 0)


def deep_terms(pooled, wd, X, h, shifts):
    total = None
    for a in shifts:
        for e in range(3):
            weights = jnp.concatenate([wd[9 * a + 3 * e + f] for f in range(3)], axis=1)
            term = dot(weights, pooled[X + a, :, h * 256 + e * 128 : h * 256 + e * 128 + 256])
            total = term if total is None else total + term
    return total


def deep_inner(pooled, wd, pre_deep):
    for h in range(2):
        for X, shifts in ((0, (1, 2)), (1, (0, 1))):
            pre_deep[X, :, h * 256 : (h + 1) * 256] = deep_terms(pooled, wd, X, h, shifts)


def deep_outer(pooled, wd, ct, pre_deep, act, deep_in):
    for X, a in ((0, 0), (1, 2)):
        for h in range(2):
            pre = pre_deep[X, :, h * 256 : (h + 1) * 256] + deep_terms(pooled, wd, X, h, (a,))
            s = sigmoid(pre)
            value = (pre * s).astype(BF16)
            slope = s * (1.0 + pre * (1.0 - s))
            for k in range(2):
                Y, part = 2 * h + k, slice(k * 128, (k + 1) * 128)
                act[Y, X] = value[:, part]
                deep_in[X, :, (Y + 2) * 128 : (Y + 3) * 128] = (ct[Y, X].astype(F32) * slope[:, part]).astype(BF16)


def pooled_terms(deep_in, wdt, pairs, first):
    column = lax.broadcasted_iota(jnp.int32, (128, 128), 1)
    total = None
    for X, a in pairs:
        for e in range(3):
            lanes = slice((first + 2 - e) * 128, (first + 4 - e) * 128)
            term = dot(wdt[3 * a + e], deep_in[X, :, lanes])
            total = term if total is None else total + term
    parts = []
    for k in range(2):
        part = total[:, k * 128 : (k + 1) * 128]
        grad = part[128:256]
        grad += jnp.where(column < 127, pltpu.roll(part[0:128], 127, 1), 0.0)
        grad += jnp.where(column > 0, pltpu.roll(part[256:384], 1, 1), 0.0)
        parts.append(grad)
    return jnp.concatenate(parts, axis=1)


def pooled_outer(deep_in, wdt, send_x, n):
    for first in (0, 2, 4):
        terms = pooled_terms(deep_in, wdt, (((0, 0),), ((1, 2),))[n], first)
        send_x[n, :, first * 128 : (first + 2) * 128] = terms.astype(BF16)


def pooled_inner(deep_in, wdt, pooled_grad, firsts):
    for X, pairs in enumerate((((0, 1), (1, 0)), ((0, 2), (1, 1)))):
        for first in firsts:
            pooled_grad[X, :, first * 128 : (first + 2) * 128] = pooled_terms(deep_in, wdt, pairs, first)


def early_cotangent(pooled_grad, got_x, got_y, got_xy, slopes, early_in):
    for X in range(2):
        grad = pooled_grad[X, :, 128:640] + got_x[X].astype(F32)
        for Y in range(4):
            here = grad[:, Y * 128 : (Y + 1) * 128]
            if Y in (0, 3):
                here += got_y[Y // 3, X].astype(F32) + got_xy[X, Y // 3].astype(F32)
            here *= 0.125
            for x in (2 * X, 2 * X + 1):
                for y in (2 * Y, 2 * Y + 1):
                    lanes = slice(y * 128, (y + 1) * 128)
                    for p in range(2):
                        rows = slice(p * 128, (p + 1) * 128)
                        early_in[x, rows, lanes] = (here * slopes[x, rows, lanes]).astype(BF16)


def slot(ae, f):
    return 3 * ae + f + ae // 5


def deep_gradient(deep_in, pooled, out):
    for ae in range(9):
        a, e = ae // 3, ae % 3
        total = None
        for X in range(2):
            term = dot_nt(deep_in[X, :, 256:768], pooled[X + a, :, e * 128 : e * 128 + 512])
            total = term if total is None else total + term
        for f in range(3):
            tap = total[:, f * 128 : (f + 1) * 128].astype(BF16).reshape(4, 2, 32, 128)
            for h in range(2):
                out[h, slot(ae, f)] = tap[:, h]


def early_gradient(early_in, taps_in, out, first, last):
    for ae in range(first, last):
        a, e = ae // 3, ae % 3
        total = None
        for x in range(4):
            term = dot_nt(taps_in[x + a, :, e * 128 : e * 128 + 1024], early_in[x])
            total = term if total is None else total + term
        total = (total[:192, :128] + total[64:, 128:]).astype(BF16)
        for f in range(3):
            for h in range(2):
                out[h, slot(ae, f)] = total[f * 64 + h * 32 : f * 64 + h * 32 + 32]


def add_taps(first, last, out, terms):
    def body(t, carry):
        total = None
        for term in terms:
            value = term(t).astype(F32)
            total = value if total is None else total + value
        out(t, total.astype(BF16))
        return carry

    lax.fori_loop(first, last, body, 0)


def total_of(own, others):
    total = own.astype(F32)
    for other in others:
        total += other.astype(F32)
    return total


def kernel(
    samples_raw, ef_hbm, wd_hbm, ct_hbm,
    act_in, full,
    samples, ef, ct_raw, ct_own, sample_ext, taps_in, w9, spread, slopes, pool_sum, pooled, wd, wdt, ct, pre_deep, act, deep_in,
    pooled_grad, send_x, send_y, got_x, got_y, got_xy, early_in,
    dg, dg_pair, dg_b, dg_b_in, dg_b_sum, dg_b_chan, dg_a, dg_a_in, dg_a_sum, dg_a_plane,
    eg, eg_pair, eg_sum, eg_plane, eg_chan,
    halo_send, halo_recv, x_send, x_recv, piece_send, piece_recv, chan_send, chan_recv, pair_send, pair_recv, plane_send, plane_recv, both_send, both_recv, load_sem,
):
    dp, space, chan = lax.axis_index("dp"), lax.axis_index("space"), lax.axis_index("chan")
    core, column = space % 2, space // 2
    rank = column * 2 + dp

    def side_device(dx, dy):
        return {"dp": dp, "space": (space + dx + 16) % 16, "chan": (chan + dy + 4) % 4}

    def chan_device(j):
        return {"dp": dp, "space": space, "chan": (chan + j) % 4}

    def x_device(j):
        return {"dp": dp, "space": (space + 4 * j) % 16, "chan": chan}

    def plane_device(j):
        r = (rank + j) % 16
        return {"dp": r % 2, "space": (r // 2) * 2 + core, "chan": chan}

    sibling = {"dp": dp, "space": column * 2 + 1 - core, "chan": chan}

    barrier = pltpu.get_barrier_semaphore()
    peers = [side_device(dx, dy) for dx, dy in SIDES]
    peers += [chan_device(2), sibling] + [plane_device(j) for j in range(1, 16)]
    for peer in peers:
        pl.semaphore_signal(barrier, inc=1, device_id=peer, device_id_type=MESH)

    mine = pl.ds(pl.multiple_of(chan * 64, 64), 64)
    half = pl.ds(pl.multiple_of(core * 32, 32), 32)
    loads = [
        pltpu.make_async_copy(src, dst, load_sem.at[n])
        for n, (src, dst) in enumerate(((ef_hbm, ef), (ct_hbm, ct_raw), (wd_hbm, wd.at[pl.ds(0, 27), mine, :])))
    ]
    for load in loads:
        load.start()
    cells_first(samples_raw, samples)
    loads[0].wait()
    build_early_weights(ef, w9)
    spread[...] = selector(256, 512, lambda r, c: r == 2 * (c % 128) + c // 128 - 1)
    loads[1].wait()
    deep_cells_first(ct_raw, ct_own)
    ct[:, :, mine, :] = ct_own[pl.ds(pl.multiple_of(chan * 4, 4), 4)]
    loads[2].wait()
    wd[27, mine, :] = jnp.zeros((64, 128), BF16)

    pl.semaphore_wait(barrier, len(peers))

    sends = []

    def describe(src, dst, send_sem, recv_sem, device):
        return pltpu.make_async_remote_copy(
            src_ref=src, dst_ref=dst, send_sem=send_sem, recv_sem=recv_sem, device_id=device, device_id_type=MESH
        )

    def remote(*args):
        copy = describe(*args)
        copy.start()
        sends.append(copy)
        return copy

    def landed(copies):
        for copy in copies:
            copy.wait_recv()

    def over_chan(n, src, dst):
        return [
            remote(src((chan + j) % 4), dst(j), chan_send.at[n, j], chan_recv.at[n, j], chan_device(j)) for j in (1, 2, 3)
        ]

    def pair(n, src, dst):
        return remote(src, dst, pair_send.at[n], pair_recv.at[n], sibling)

    def halo(n, view, dxs):
        copies = []
        for dx in dxs:
            for dy in (-1, 0, 1):
                if (dx, dy) != (0, 0):
                    src, dst = view(dx, dy)
                    k = SIDES.index((dx, dy))
                    copies.append(remote(src, dst, halo_send.at[n, k], halo_recv.at[n, k], side_device(dx, dy)))
        return copies

    def sample_view(dx, dy):
        (sx, nx), (tx, _) = sent_and_landed(dx, 4)
        (sy, ny), (ty, _) = sent_and_landed(dy, 8)
        src = samples.at[pl.ds(sx - 1, nx), pl.ds(sy - 1, ny)]
        return src, sample_ext.at[pl.ds(tx, nx), pl.ds(ty, ny)]

    def field_view(ref, first, rows):
        def view(dx, dy):
            (sx, nx), (tx, _) = sent_and_landed(dx, 2)
            (sy, ny), (ty, _) = sent_and_landed(dy, 4)
            block = pl.ds(first, rows)
            src = ref.at[pl.ds(sx, nx), block, pl.ds(sy * 128, ny * 128)]
            return src, ref.at[pl.ds(tx, nx), block, pl.ds(ty * 128, ny * 128)]

        return view

    def clear_y(ref, xs, rows, lanes):
        width = ref.shape[2]
        for at, span in ((0, slice(0, lanes)), (3, slice(width - lanes, width))):

            @pl.when(chan == at)
            def _():
                for x in xs:
                    ref[x, rows, span] = jnp.zeros((rows.stop - rows.start, lanes), BF16)

    def clear_x(ref, rows):
        width = ref.shape[2]
        for at, x in ((0, 0), (15, ref.shape[0] - 1)):

            @pl.when(space == at)
            def _():
                ref[x, rows, :] = jnp.zeros((rows.stop - rows.start, width), BF16)

    sample_x = halo(0, sample_view, (-1, 1))

    def some_of(c, taps, of_core):
        return wd.at[taps, pl.ds(pl.multiple_of(c * 64 + of_core * 32, 32), 32), :]

    my_taps = pl.ds(space // 4 * 7, 7)
    wd_copies = over_chan(0, lambda c: some_of(chan, my_taps, core), lambda j: some_of(chan, my_taps, core))
    sample_y = halo(0, sample_view, (0,))
    for x in range(4):
        place_taps(samples[x].reshape(512, 256), spread, taps_in, x + 1, 1, 8)
    for h in range(2):
        dg[h, 15] = jnp.zeros((4, 32, 128), BF16)
        eg[h, 15] = jnp.zeros((32, 128), BF16)
    dg_a_sum[12:16] = jnp.zeros((4, 32, 128), BF16)
    eg_sum[28:32] = jnp.zeros((4, 32, 128), BF16)
    for X in range(2):
        for lanes in (slice(0, 256), slice(768, 1024)):
            deep_in[X, :, lanes] = jnp.zeros((256, 256), BF16)

    early_inner(taps_in, w9, slopes, pool_sum, (1, 2))
    for j, copy in zip((1, 2, 3), wd_copies):
        landed([copy])
        block = some_of((chan - j + 4) % 4, my_taps, core)
        for i in (1, 2, 3):
            remote(block, block, x_send.at[j, i], x_recv.at[j, i], x_device(i))
        remote(block, block, piece_send.at[j, 0], piece_recv.at[j, 0], sibling)
    landed(sample_y)
    for y in (0, 9):
        for x in range(1, 5):
            place_taps(sample_ext[x, y], spread, taps_in, x, y, 1)
    clear_y(taps_in, range(1, 5), slice(0, 256), 128)
    ct_copies = over_chan(
        1, lambda c: ct_own.at[pl.ds(pl.multiple_of(c * 4, 4), 4)], lambda j: ct.at[:, :, mine, :]
    )
    early_inner(taps_in, w9, slopes, pool_sum, (0, 3))
    landed(sample_x)
    for x in (0, 5):
        place_taps(sample_ext[x].reshape(640, 256), spread, taps_in, x, 0, 10)
    clear_y(taps_in, (0, 5), slice(0, 256), 128)
    clear_x(taps_in, slice(0, 256))
    early_outer(taps_in, w9, slopes, pool_sum, pooled, 0)
    pooled_x = halo(1, field_view(pooled, 128, 128), (-1,))
    early_outer(taps_in, w9, slopes, pool_sum, pooled, 1)
    pooled_x += halo(1, field_view(pooled, 128, 128), (1,))
    pooled_y = halo(1, field_view(pooled, 128, 128), (0,))
    shift_pooled(pooled, (1, 2), 1, 4)
    for j in (1, 2, 3):
        for i in (1, 2, 3):
            block = some_of((chan - j + 4) % 4, pl.ds((space // 4 - i + 4) % 4 * 7, 7), core)
            describe(block, block, x_send.at[j, i], x_recv.at[j, i], x_device(i)).wait_recv()
            remote(block, block, piece_send.at[j, i], piece_recv.at[j, i], sibling)
    landed(pooled_y)
    clear_y(pooled, (1, 2), slice(128, 256), 128)
    shift_pooled(pooled, (1, 2), 0, 1)
    shift_pooled(pooled, (1, 2), 5, 1)
    for j in (1, 2, 3):
        for i in range(4):
            block = some_of((chan - j + 4) % 4, pl.ds((space // 4 - i + 4) % 4 * 7, 7), 1 - core)
            describe(block, block, piece_send.at[j, i], piece_recv.at[j, i], sibling).wait_recv()
    deep_inner(pooled, wd, pre_deep)
    transpose_deep_weights(wd, wdt)
    landed(pooled_x)
    clear_y(pooled, (0, 3), slice(128, 256), 128)
    clear_x(pooled, slice(128, 256))
    shift_pooled(pooled, (0, 3), 0, 6)
    landed(ct_copies)
    deep_outer(pooled, wd, ct, pre_deep, act, deep_in)

    grad_copies = []
    for n, dx in enumerate((-1, 1)):
        pooled_outer(deep_in, wdt, send_x, n)
        for dy in (-1, 0, 1):
            at, count = {-1: (0, 1), 0: (1, 4), 1: (5, 1)}[dy]
            src = send_x.at[n, :, pl.ds(at * 128, count * 128)]
            dst = got_x.at[1 - n] if dy == 0 else got_xy.at[1 - n, 0 if dy > 0 else 1]
            k = SIDES.index((dx, dy))
            grad_copies.append(remote(src, dst, halo_send.at[2, k], halo_recv.at[2, k], side_device(dx, dy)))
    pooled_inner(deep_in, wdt, pooled_grad, (0, 4))
    for n, (dy, at) in enumerate(((-1, 0), (1, 5))):
        for X in range(2):
            send_y[n, X] = pooled_grad[X, :, at * 128 : (at + 1) * 128].astype(BF16)
        k = SIDES.index((0, dy))
        grad_copies.append(
            remote(send_y.at[n], got_y.at[1 - n], halo_send.at[2, k], halo_recv.at[2, k], side_device(0, dy))
        )

    here = pl.ds(pl.multiple_of(chan * 4, 4), 4)
    act_copies = over_chan(
        4, lambda c: act.at[:, :, pl.ds(pl.multiple_of(c * 64, 64), 64), :], lambda j: act_in.at[here]
    )
    act_in[here] = act[:, :, mine, :]

    def over_plane(n, src, dst):
        return [
            remote(src((rank + j) % 16), dst(j), plane_send.at[n, j], plane_recv.at[n, j], plane_device(j))
            for j in range(1, 16)
        ]

    deep_gradient(deep_in, pooled, dg)
    dg_pair_copy = pair(0, dg.at[1 - core, pl.ds(0, 28)], dg_pair)
    pooled_inner(deep_in, wdt, pooled_grad, (2,))
    landed(grad_copies)
    for at, n in ((0, 0), (15, 1)):

        @pl.when(space == at)
        def _():
            got_x[n] = jnp.zeros((128, 512), BF16)
            got_xy[n] = jnp.zeros((2, 128, 128), BF16)

    for at, n in ((0, 0), (3, 1)):

        @pl.when(chan == at)
        def _():
            got_y[n] = jnp.zeros((2, 128, 128), BF16)
            for m in range(2):
                got_xy[m, n] = jnp.zeros((128, 128), BF16)

    early_cotangent(pooled_grad, got_x, got_y, got_xy, slopes, early_in)
    landed([dg_pair_copy])

    def put_b(t, value):
        dg_b[t] = value

    def put_a(t, value):
        dg_a[:, t - 16] = value

    add_taps(16, 28, put_a, [lambda t: dg[core, t], lambda t: dg_pair[t]])
    dg_a_copies = over_chan(3, lambda c: dg_a.at[c], lambda j: dg_a_in.at[j])
    add_taps(0, 16, put_b, [lambda t: dg[core, t], lambda t: dg_pair[t]])
    dg_b_copies = over_plane(0, lambda r: dg_b.at[r], lambda j: dg_b_in.at[j])
    early_gradient(early_in, taps_in, eg, 0, 5)
    eg_pair_0 = pair(1, eg.at[1 - core, pl.ds(0, 16)], eg_pair.at[pl.ds(0, 16)])
    early_gradient(early_in, taps_in, eg, 5, 7)

    def put_eg(t, value):
        eg_sum[t] = value

    landed([eg_pair_0])
    add_taps(0, 16, put_eg, [lambda t: eg[core, t], lambda t: eg_pair[t]])
    eg_copies = [over_plane(2, lambda r: eg_sum.at[r], lambda j: eg_plane.at[0, j])]
    early_gradient(early_in, taps_in, eg, 7, 9)
    eg_pair_1 = pair(2, eg.at[1 - core, pl.ds(16, 12)], eg_pair.at[pl.ds(16, 12)])

    def put_a_sum(t, value):
        dg_a_sum[t] = value

    landed(dg_a_copies)
    add_taps(0, 12, put_a_sum, [lambda t: dg_a[chan, t]] + [lambda t, j=j: dg_a_in[j, t] for j in (1, 2, 3)])
    landed([eg_pair_1])
    add_taps(16, 28, put_eg, [lambda t: eg[core, t], lambda t: eg_pair[t]])
    eg_copies.append(over_plane(3, lambda r: eg_sum.at[16 + r], lambda j: eg_plane.at[1, j]))
    dg_a_copies = over_plane(1, lambda r: dg_a_sum.at[r], lambda j: dg_a_plane.at[j])
    landed(dg_b_copies)
    dg_b_sum[...] = total_of(dg_b[rank], [dg_b_in[j] for j in range(1, 16)])
    dg_b_copies = over_chan(6, lambda c: dg_b_sum.at[c], lambda j: dg_b_chan.at[j])

    def both(n, j, block):
        remote(block, block, both_send.at[n, j], both_recv.at[n, j], sibling)

    def gather(n):
        block = full.at[n, :, rank, half, :]
        for j in range(1, 16):
            remote(block, block, plane_send.at[4 + n, j], plane_recv.at[4 + n, j], plane_device(j))
        both(n, 0, block)

    def gathered(n):
        for j in range(1, 16):
            theirs = full.at[n, :, (rank - j + 16) % 16, half, :]
            describe(theirs, theirs, plane_send.at[4 + n, j], plane_recv.at[4 + n, j], plane_device(j)).wait_recv()
            both(n, j, theirs)

    def halves_landed(n):
        other = pl.ds(pl.multiple_of(32 - core * 32, 32), 32)
        for j in range(16):
            theirs = full.at[n, :, (rank - j + 16) % 16, other, :]
            describe(theirs, theirs, both_send.at[n, j], both_recv.at[n, j], sibling).wait_recv()

    def chan_terms(n):
        landed(eg_copies[n])
        eg_chan[chan, n] = total_of(eg_sum[16 * n + rank], [eg_plane[n, j] for j in range(1, 16)])
        over_chan((5, 2)[n], lambda c: eg_chan.at[chan, n], lambda j: eg_chan.at[chan, n])

    def chan_total(n):
        for j in (1, 2, 3):
            block = eg_chan.at[(chan - j + 4) % 4, n]
            k = (5, 2)[n]
            describe(block, block, chan_send.at[k, j], chan_recv.at[k, j], chan_device(j)).wait_recv()
        total = (eg_chan[0, n] + eg_chan[1, n]) + (eg_chan[2, n] + eg_chan[3, n])
        full[1, n, rank, half, :] = total.astype(BF16)

    chan_terms(0)
    landed(dg_b_copies)
    full[0, 0, rank, half, :] = total_of(dg_b_sum[chan], [dg_b_chan[j] for j in (1, 2, 3)]).astype(BF16)
    landed(dg_a_copies)
    full[0, 1, rank, half, :] = total_of(dg_a_sum[rank], [dg_a_plane[j] for j in range(1, 16)]).astype(BF16)
    gather(0)
    chan_terms(1)
    chan_total(0)
    chan_total(1)
    gather(1)
    gathered(0)
    gathered(1)
    halves_landed(0)
    halves_landed(1)

    landed(act_copies)
    for copy in sends:
        copy.wait_send()


def finish(act_hbm, grads_hbm, act_out, dg_out, eg_out, act_in, grads, sem):
    copies = [
        pltpu.make_async_copy(grads_hbm.at[0], grads.at[0], sem.at[0]),
        pltpu.make_async_copy(grads_hbm.at[1], grads.at[1], sem.at[1]),
        pltpu.make_async_copy(act_hbm, act_in, sem.at[2]),
    ]
    for copy in copies:
        copy.start()
    for n, out in enumerate((dg_out, eg_out)):
        copies[n].wait()
        for t in range(27):
            out[t] = grads[n, t // 15, t % 15].astype(F32)
    copies[2].wait()
    deep_channels_first(act_in, act_out)


def on_device(samples, early_filters, deep_filters, deep_cotangent):
    act, grads = pl.pallas_call(
        kernel,
        out_shape=(
            jax.ShapeDtypeStruct((16, 2, 64, 128), BF16),
            jax.ShapeDtypeStruct((2, 2, 16, 64, 128), BF16),
        ),
        in_specs=[pl.BlockSpec(memory_space=pltpu.VMEM)] + [pl.BlockSpec(memory_space=pl.ANY)] * 3,
        out_specs=[pl.BlockSpec(memory_space=pltpu.VMEM)] * 2,
        scratch_shapes=[
            pltpu.VMEM((4, 8, 64, 256), BF16),
            pltpu.VMEM((27, 64, 128), BF16),
            pltpu.VMEM((64, 2, 16, 128), BF16),
            pltpu.VMEM((16, 2, 64, 128), BF16),
            pltpu.VMEM((6, 10, 64, 256), BF16),
            pltpu.VMEM((6, 256, 1280), BF16),
            pltpu.VMEM((9, 256, 256), BF16),
            pltpu.VMEM((256, 512), BF16),
            pltpu.VMEM((4, 256, 1024), F32),
            pltpu.VMEM((2, 128, 512), F32),
            pltpu.VMEM((4, 384, 768), BF16),
            pltpu.VMEM((28, 256, 128), BF16),
            pltpu.VMEM((9, 384, 256), BF16),
            pltpu.VMEM((4, 2, 256, 128), BF16),
            pltpu.VMEM((2, 256, 512), F32),
            pltpu.VMEM((4, 2, 256, 128), BF16),
            pltpu.VMEM((2, 256, 1024), BF16),
            pltpu.VMEM((2, 128, 768), F32),
            pltpu.VMEM((2, 128, 768), BF16),
            pltpu.VMEM((2, 2, 128, 128), BF16),
            pltpu.VMEM((2, 128, 512), BF16),
            pltpu.VMEM((2, 2, 128, 128), BF16),
            pltpu.VMEM((2, 2, 128, 128), BF16),
            pltpu.VMEM((4, 256, 1024), BF16),
            pltpu.VMEM((2, 28, 4, 32, 128), BF16),
            pltpu.VMEM((28, 4, 32, 128), BF16),
            pltpu.VMEM((16, 4, 32, 128), BF16),
            pltpu.VMEM((16, 4, 32, 128), BF16),
            pltpu.VMEM((4, 32, 128), F32),
            pltpu.VMEM((4, 32, 128), F32),
            pltpu.VMEM((4, 12, 32, 128), BF16),
            pltpu.VMEM((4, 12, 32, 128), BF16),
            pltpu.VMEM((16, 32, 128), BF16),
            pltpu.VMEM((16, 32, 128), BF16),
            pltpu.VMEM((2, 28, 32, 128), BF16),
            pltpu.VMEM((28, 32, 128), BF16),
            pltpu.VMEM((32, 32, 128), BF16),
            pltpu.VMEM((2, 16, 32, 128), BF16),
            pltpu.VMEM((4, 2, 32, 128), F32),
            pltpu.SemaphoreType.DMA((3, 8)),
            pltpu.SemaphoreType.DMA((3, 8)),
            pltpu.SemaphoreType.DMA((4, 4)),
            pltpu.SemaphoreType.DMA((4, 4)),
            pltpu.SemaphoreType.DMA((4, 4)),
            pltpu.SemaphoreType.DMA((4, 4)),
            pltpu.SemaphoreType.DMA((7, 4)),
            pltpu.SemaphoreType.DMA((7, 4)),
            pltpu.SemaphoreType.DMA((3,)),
            pltpu.SemaphoreType.DMA((3,)),
            pltpu.SemaphoreType.DMA((6, 16)),
            pltpu.SemaphoreType.DMA((6, 16)),
            pltpu.SemaphoreType.DMA((2, 16)),
            pltpu.SemaphoreType.DMA((2, 16)),
            pltpu.SemaphoreType.DMA((3,)),
        ],
        compiler_params=pltpu.CompilerParams(
            collective_id=0, has_side_effects=True, vmem_limit_bytes=56 * 1024 * 1024
        ),
        name="conv_step",
    )(samples[0], early_filters.transpose(0, 2, 1), deep_filters, deep_cotangent[0])
    act, deep_grad, early_grad = pl.pallas_call(
        finish,
        out_shape=(
            jax.ShapeDtypeStruct((64, 2, 16, 128), BF16),
            jax.ShapeDtypeStruct((27, 64, 128), F32),
            jax.ShapeDtypeStruct((27, 64, 128), F32),
        ),
        in_specs=[pl.BlockSpec(memory_space=pl.ANY)] * 2,
        out_specs=[pl.BlockSpec(memory_space=pltpu.VMEM)] * 3,
        scratch_shapes=[
            pltpu.VMEM((16, 2, 64, 128), BF16),
            pltpu.VMEM((2, 2, 16, 64, 128), BF16),
            pltpu.SemaphoreType.DMA((3,)),
        ],
        compiler_params=pltpu.CompilerParams(vmem_limit_bytes=56 * 1024 * 1024),
        name="finish",
    )(act, grads)
    return act[None], deep_grad, early_grad.transpose(0, 2, 1)


def solution(mesh):
    placed = (
        P("dp", None, "space", "chan", None),
        P(),
        P(None, "chan", None),
        P("dp", "chan", "space", None, None),
    )
    return jax.shard_map(
        on_device,
        mesh=mesh,
        in_specs=placed,
        out_specs=(P("dp", "chan", "space", None, None), P(None, "chan", None), P()),
        check_vma=False,
    )
```

```python
import jax
import jax.numpy as jnp
from jax import lax
from jax.experimental import pallas as pl
from jax.experimental.pallas import tpu as pltpu
from jax.sharding import PartitionSpec as P

BF16 = jnp.bfloat16
F32 = jnp.float32
MESH = pl.DeviceIdType.MESH

SIDES = [(dx, dy) for dx in (-1, 0, 1) for dy in (-1, 0, 1) if (dx, dy) != (0, 0)]


def dot(a, b):
    return lax.dot_general(a, b, (((1,), (0,)), ((), ())), preferred_element_type=F32)


def dot_nt(a, b):
    return lax.dot_general(a, b, (((1,), (1,)), ((), ())), preferred_element_type=F32)


def selector(rows, cols, hit):
    row = lax.broadcasted_iota(jnp.int32, (rows, cols), 0)
    col = lax.broadcasted_iota(jnp.int32, (rows, cols), 1)
    return jnp.where(hit(row, col), 1.0, 0.0).astype(BF16)


def sigmoid(u):
    return 0.5 + 0.5 * jnp.tanh(0.5 * u)


def sent_and_landed(side, length):
    if side == 0:
        return (1, length), (1, length)
    if side == 1:
        return (length, 1), (0, 1)
    return (1, 1), (length + 1, 1)


def build_early_weights(ef, w9):
    eye = selector(128, 128, lambda r, c: r == c)
    none = jnp.zeros((64, 128), BF16)

    def body(i, carry):
        for ae in range(3):
            taps = [ef[9 * i + 3 * ae + f] for f in range(3)]
            for p in range(2):
                slots = [none] + taps if p else taps + [none]
                rows = slice(p * 128, (p + 1) * 128)
                w9[3 * i + ae, rows, :] = dot_nt(eye, jnp.concatenate(slots, axis=0)).astype(BF16)
        return carry

    lax.fori_loop(0, 3, body, 0)


def cells_first(samples_raw, samples):
    swap = selector(256, 256, lambda r, c: c == (r % 32) * 8 + r // 32)

    def body(x, carry):
        for n in range(2):
            block = samples_raw[n * 32 : (n + 1) * 32, x].astype(F32).reshape(256, 256).astype(BF16)
            block = dot(swap, block).astype(BF16)
            for y in range(8):
                samples[x, y, n * 32 : (n + 1) * 32, :] = block[y * 32 : (y + 1) * 32]
        return carry

    lax.fori_loop(0, 4, body, 0)


def row_swap():
    return selector(256, 256, lambda r, c: c == (r % 16) * 16 + r // 16)


def deep_cells_first(raw, out):
    swap = row_swap()
    for n in range(4):
        rows = slice(n * 16, (n + 1) * 16)
        block = jnp.concatenate([raw[rows, X].reshape(256, 128) for X in range(2)], axis=1)
        block = dot(swap, block).astype(BF16)
        for Y in range(16):
            for X in range(2):
                out[Y, X, rows, :] = block[Y * 16 : (Y + 1) * 16, X * 128 : (X + 1) * 128]


def deep_channels_first(raw, out):
    swap = row_swap()
    for n in range(4):
        rows = slice(n * 16, (n + 1) * 16)
        block = [jnp.concatenate([raw[Y, X, rows, :] for Y in range(16)], axis=0) for X in range(2)]
        block = dot(swap, jnp.concatenate(block, axis=1)).astype(BF16)
        for X in range(2):
            out[rows, X] = block[:, X * 128 : (X + 1) * 128].reshape(16, 16, 128)


def place_taps(block, spread, taps_in, x, first_y, count):
    wide = dot(block, spread[...]).astype(BF16)
    for y in range(count):
        for s in range(4):
            taps_in[x, s * 64 : (s + 1) * 64, pl.ds((first_y + y) * 128, 128)] = wide[
                y * 64 : (y + 1) * 64, s * 128 : (s + 1) * 128
            ]


def early_terms(taps_in, w9, x, Y, shifts):
    total = None
    for a in shifts:
        for e in range(3):
            term = dot(w9[3 * a + e], taps_in[x + a, :, (2 * Y + e) * 128 : (2 * Y + e + 2) * 128])
            total = term if total is None else total + term
    return total


def early_activation(pre, slopes, x, Y):
    s = sigmoid(pre)
    slopes[x, :, Y * 256 : (Y + 1) * 256] = s * (1.0 + pre * (1.0 - s))
    act = pre * s
    act = act[:128] + act[128:]
    return act[:, :128] + act[:, 128:]


def early_inner(taps_in, w9, slopes, pool_sum, Ys):
    for Y in Ys:
        for x, shifts in ((0, (1, 2)), (3, (0, 1))):
            slopes[x, :, Y * 256 : (Y + 1) * 256] = early_terms(taps_in, w9, x, Y, shifts)
        for X, x in enumerate((1, 2)):
            pre = early_terms(taps_in, w9, x, Y, (0, 1, 2))
            pool_sum[X, :, Y * 128 : (Y + 1) * 128] = early_activation(pre, slopes, x, Y)


def early_outer(taps_in, w9, slopes, pool_sum, pooled, X):
    x, a = ((0, 0), (3, 2))[X]
    for Y in range(4):
        pre = slopes[x, :, Y * 256 : (Y + 1) * 256] + early_terms(taps_in, w9, x, Y, (a,))
        total = pool_sum[X, :, Y * 128 : (Y + 1) * 128] + early_activation(pre, slopes, x, Y)
        pooled[X + 1, 128:256, (Y + 1) * 128 : (Y + 2) * 128] = (total * 0.125).astype(BF16)


def shift_pooled(pooled, xs, first, count):
    shifts = selector(128, 256, lambda r, c: r == jnp.where(c < 128, c - 1, c - 127))
    for x in xs:
        blocks = [pooled[x, 128:256, (first + y) * 128 : (first + y + 1) * 128] for y in range(count)]
        both = dot(jnp.concatenate(blocks, axis=0), shifts).astype(BF16)
        for y in range(count):
            lanes = slice((first + y) * 128, (first + y + 1) * 128)
            rows = slice(y * 128, (y + 1) * 128)
            pooled[x, 0:128, lanes] = both[rows, :128]
            pooled[x, 256:384, lanes] = both[rows, 128:]


def transpose_deep_weights(wd, wdt):
    eye = selector(128, 128, lambda r, c: r == c)

    def body(i, carry):
        for ae in range(3):
            for f in range(3):
                rows = slice(f * 128, (f + 1) * 128)
                wdt[3 * i + ae, rows, :] = dot_nt(eye, wd[9 * i + 3 * ae + f]).astype(BF16)
        return carry

    lax.fori_loop(0, 3, body, 0)


def deep_terms(pooled, wd, X, h, shifts):
    total = None
    for a in shifts:
        for e in range(3):
            weights = jnp.concatenate([wd[9 * a + 3 * e + f] for f in range(3)], axis=1)
            term = dot(weights, pooled[X + a, :, h * 256 + e * 128 : h * 256 + e * 128 + 256])
            total = term if total is None else total + term
    return total


def deep_inner(pooled, wd, pre_deep):
    for h in range(2):
        for X, shifts in ((0, (1, 2)), (1, (0, 1))):
            pre_deep[X, :, h * 256 : (h + 1) * 256] = deep_terms(pooled, wd, X, h, shifts)


def deep_outer(pooled, wd, ct, pre_deep, act, deep_in):
    for X, a in ((0, 0), (1, 2)):
        for h in range(2):
            pre = pre_deep[X, :, h * 256 : (h + 1) * 256] + deep_terms(pooled, wd, X, h, (a,))
            s = sigmoid(pre)
            value = (pre * s).astype(BF16)
            slope = s * (1.0 + pre * (1.0 - s))
            for k in range(2):
                Y, part = 2 * h + k, slice(k * 128, (k + 1) * 128)
                act[Y, X] = value[:, part]
                deep_in[X, :, (Y + 2) * 128 : (Y + 3) * 128] = (ct[Y, X].astype(F32) * slope[:, part]).astype(BF16)


def pooled_terms(deep_in, wdt, pairs, first):
    column = lax.broadcasted_iota(jnp.int32, (128, 128), 1)
    total = None
    for X, a in pairs:
        for e in range(3):
            lanes = slice((first + 2 - e) * 128, (first + 4 - e) * 128)
            term = dot(wdt[3 * a + e], deep_in[X, :, lanes])
            total = term if total is None else total + term
    parts = []
    for k in range(2):
        part = total[:, k * 128 : (k + 1) * 128]
        grad = part[128:256]
        grad += jnp.where(column < 127, pltpu.roll(part[0:128], 127, 1), 0.0)
        grad += jnp.where(column > 0, pltpu.roll(part[256:384], 1, 1), 0.0)
        parts.append(grad)
    return jnp.concatenate(parts, axis=1)


def pooled_outer(deep_in, wdt, send_x, n):
    for first in (0, 2, 4):
        terms = pooled_terms(deep_in, wdt, (((0, 0),), ((1, 2),))[n], first)
        send_x[n, :, first * 128 : (first + 2) * 128] = terms.astype(BF16)


def pooled_inner(deep_in, wdt, pooled_grad, firsts):
    for X, pairs in enumerate((((0, 1), (1, 0)), ((0, 2), (1, 1)))):
        for first in firsts:
            pooled_grad[X, :, first * 128 : (first + 2) * 128] = pooled_terms(deep_in, wdt, pairs, first)


def early_cotangent(pooled_grad, got_x, got_y, got_xy, slopes, early_in):
    for X in range(2):
        grad = pooled_grad[X, :, 128:640] + got_x[X].astype(F32)
        for Y in range(4):
            here = grad[:, Y * 128 : (Y + 1) * 128]
            if Y in (0, 3):
                here += got_y[Y // 3, X].astype(F32) + got_xy[X, Y // 3].astype(F32)
            here *= 0.125
            for x in (2 * X, 2 * X + 1):
                for y in (2 * Y, 2 * Y + 1):
                    lanes = slice(y * 128, (y + 1) * 128)
                    for p in range(2):
                        rows = slice(p * 128, (p + 1) * 128)
                        early_in[x, rows, lanes] = (here * slopes[x, rows, lanes]).astype(BF16)


def slot(ae, f):
    return 3 * ae + f + ae // 5


def deep_gradient(deep_in, pooled, out):
    for ae in range(9):
        a, e = ae // 3, ae % 3
        total = None
        for X in range(2):
            term = dot_nt(deep_in[X, :, 256:768], pooled[X + a, :, e * 128 : e * 128 + 512])
            total = term if total is None else total + term
        for f in range(3):
            tap = total[:, f * 128 : (f + 1) * 128].astype(BF16).reshape(4, 2, 32, 128)
            for h in range(2):
                out[h, slot(ae, f)] = tap[:, h]


def early_gradient(early_in, taps_in, out, first, last):
    for ae in range(first, last):
        a, e = ae // 3, ae % 3
        total = None
        for x in range(4):
            term = dot_nt(taps_in[x + a, :, e * 128 : e * 128 + 1024], early_in[x])
            total = term if total is None else total + term
        total = (total[:192, :128] + total[64:, 128:]).astype(BF16)
        for f in range(3):
            for h in range(2):
                out[h, slot(ae, f)] = total[f * 64 + h * 32 : f * 64 + h * 32 + 32]


def add_taps(first, last, out, terms):
    def body(t, carry):
        total = None
        for term in terms:
            value = term(t).astype(F32)
            total = value if total is None else total + value
        out(t, total.astype(BF16))
        return carry

    lax.fori_loop(first, last, body, 0)


def total_of(own, others):
    total = own.astype(F32)
    for other in others:
        total += other.astype(F32)
    return total


def kernel(
    samples_raw, ef_hbm, wd_hbm, ct_hbm,
    act_in, full,
    samples, ef, ct_raw, ct_own, sample_ext, taps_in, w9, spread, slopes, pool_sum, pooled, wd, wdt, ct, pre_deep, act, deep_in,
    pooled_grad, send_x, send_y, got_x, got_y, got_xy, early_in,
    dg, dg_pair, dg_b, dg_b_in, dg_b_sum, dg_b_chan, dg_a, dg_a_in, dg_a_sum, dg_a_plane,
    eg, eg_pair, eg_sum, eg_plane, eg_chan,
    halo_send, halo_recv, x_send, x_recv, piece_send, piece_recv, chan_send, chan_recv, pair_send, pair_recv, plane_send, plane_recv, both_send, both_recv, load_sem,
):
    dp, space, chan = lax.axis_index("dp"), lax.axis_index("space"), lax.axis_index("chan")
    core, column = space % 2, space // 2
    rank = column * 2 + dp

    def side_device(dx, dy):
        return {"dp": dp, "space": (space + dx + 16) % 16, "chan": (chan + dy + 4) % 4}

    def chan_device(j):
        return {"dp": dp, "space": space, "chan": (chan + j) % 4}

    def x_device(j):
        return {"dp": dp, "space": (space + 4 * j) % 16, "chan": chan}

    def plane_device(j):
        r = (rank + j) % 16
        return {"dp": r % 2, "space": (r // 2) * 2 + core, "chan": chan}

    sibling = {"dp": dp, "space": column * 2 + 1 - core, "chan": chan}

    barrier = pltpu.get_barrier_semaphore()
    peers = [side_device(dx, dy) for dx, dy in SIDES]
    peers += [chan_device(2), sibling] + [plane_device(j) for j in range(1, 16)]
    for peer in peers:
        pl.semaphore_signal(barrier, inc=1, device_id=peer, device_id_type=MESH)

    mine = pl.ds(pl.multiple_of(chan * 64, 64), 64)
    half = pl.ds(pl.multiple_of(core * 32, 32), 32)
    loads = [
        pltpu.make_async_copy(src, dst, load_sem.at[n])
        for n, (src, dst) in enumerate(((ef_hbm, ef), (ct_hbm, ct_raw), (wd_hbm, wd.at[pl.ds(0, 27), mine, :])))
    ]
    for load in loads:
        load.start()
    cells_first(samples_raw, samples)
    loads[0].wait()
    build_early_weights(ef, w9)
    spread[...] = selector(256, 512, lambda r, c: r == 2 * (c % 128) + c // 128 - 1)
    loads[1].wait()
    deep_cells_first(ct_raw, ct_own)
    ct[:, :, mine, :] = ct_own[pl.ds(pl.multiple_of(chan * 4, 4), 4)]
    loads[2].wait()
    wd[27, mine, :] = jnp.zeros((64, 128), BF16)

    pl.semaphore_wait(barrier, len(peers))

    sends = []

    def describe(src, dst, send_sem, recv_sem, device):
        return pltpu.make_async_remote_copy(
            src_ref=src, dst_ref=dst, send_sem=send_sem, recv_sem=recv_sem, device_id=device, device_id_type=MESH
        )

    def remote(*args):
        copy = describe(*args)
        copy.start()
        sends.append(copy)
        return copy

    def landed(copies):
        for copy in copies:
            copy.wait_recv()

    def over_chan(n, src, dst):
        return [
            remote(src((chan + j) % 4), dst(j), chan_send.at[n, j], chan_recv.at[n, j], chan_device(j)) for j in (1, 2, 3)
        ]

    def pair(n, src, dst):
        return remote(src, dst, pair_send.at[n], pair_recv.at[n], sibling)

    def halo(n, view, dxs):
        copies = []
        for dx in dxs:
            for dy in (-1, 0, 1):
                if (dx, dy) != (0, 0):
                    src, dst = view(dx, dy)
                    k = SIDES.index((dx, dy))
                    copies.append(remote(src, dst, halo_send.at[n, k], halo_recv.at[n, k], side_device(dx, dy)))
        return copies

    def sample_view(dx, dy):
        (sx, nx), (tx, _) = sent_and_landed(dx, 4)
        (sy, ny), (ty, _) = sent_and_landed(dy, 8)
        src = samples.at[pl.ds(sx - 1, nx), pl.ds(sy - 1, ny)]
        return src, sample_ext.at[pl.ds(tx, nx), pl.ds(ty, ny)]

    def field_view(ref, first, rows):
        def view(dx, dy):
            (sx, nx), (tx, _) = sent_and_landed(dx, 2)
            (sy, ny), (ty, _) = sent_and_landed(dy, 4)
            block = pl.ds(first, rows)
            src = ref.at[pl.ds(sx, nx), block, pl.ds(sy * 128, ny * 128)]
            return src, ref.at[pl.ds(tx, nx), block, pl.ds(ty * 128, ny * 128)]

        return view

    def clear_y(ref, xs, rows, lanes):
        width = ref.shape[2]
        for at, span in ((0, slice(0, lanes)), (3, slice(width - lanes, width))):

            @pl.when(chan == at)
            def _():
                for x in xs:
                    ref[x, rows, span] = jnp.zeros((rows.stop - rows.start, lanes), BF16)

    def clear_x(ref, rows):
        width = ref.shape[2]
        for at, x in ((0, 0), (15, ref.shape[0] - 1)):

            @pl.when(space == at)
            def _():
                ref[x, rows, :] = jnp.zeros((rows.stop - rows.start, width), BF16)

    sample_x = halo(0, sample_view, (-1, 1))

    def some_of(c, taps, of_core):
        return wd.at[taps, pl.ds(pl.multiple_of(c * 64 + of_core * 32, 32), 32), :]

    my_taps = pl.ds(space // 4 * 7, 7)
    wd_copies = over_chan(0, lambda c: some_of(chan, my_taps, core), lambda j: some_of(chan, my_taps, core))
    sample_y = halo(0, sample_view, (0,))
    for x in range(4):
        place_taps(samples[x].reshape(512, 256), spread, taps_in, x + 1, 1, 8)
    for h in range(2):
        dg[h, 15] = jnp.zeros((4, 32, 128), BF16)
        eg[h, 15] = jnp.zeros((32, 128), BF16)
    dg_a_sum[12:16] = jnp.zeros((4, 32, 128), BF16)
    eg_sum[28:32] = jnp.zeros((4, 32, 128), BF16)
    for X in range(2):
        for lanes in (slice(0, 256), slice(768, 1024)):
            deep_in[X, :, lanes] = jnp.zeros((256, 256), BF16)

    early_inner(taps_in, w9, slopes, pool_sum, (1, 2))
    for j, copy in zip((1, 2, 3), wd_copies):
        landed([copy])
        block = some_of((chan - j + 4) % 4, my_taps, core)
        for i in (1, 2, 3):
            remote(block, block, x_send.at[j, i], x_recv.at[j, i], x_device(i))
        remote(block, block, piece_send.at[j, 0], piece_recv.at[j, 0], sibling)
    landed(sample_y)
    for y in (0, 9):
        for x in range(1, 5):
            place_taps(sample_ext[x, y], spread, taps_in, x, y, 1)
    clear_y(taps_in, range(1, 5), slice(0, 256), 128)
    ct_copies = over_chan(
        1, lambda c: ct_own.at[pl.ds(pl.multiple_of(c * 4, 4), 4)], lambda j: ct.at[:, :, mine, :]
    )
    early_inner(taps_in, w9, slopes, pool_sum, (0, 3))
    landed(sample_x)
    for x in (0, 5):
        place_taps(sample_ext[x].reshape(640, 256), spread, taps_in, x, 0, 10)
    clear_y(taps_in, (0, 5), slice(0, 256), 128)
    clear_x(taps_in, slice(0, 256))
    early_outer(taps_in, w9, slopes, pool_sum, pooled, 0)
    pooled_x = halo(1, field_view(pooled, 128, 128), (-1,))
    early_outer(taps_in, w9, slopes, pool_sum, pooled, 1)
    pooled_x += halo(1, field_view(pooled, 128, 128), (1,))
    pooled_y = halo(1, field_view(pooled, 128, 128), (0,))
    shift_pooled(pooled, (1, 2), 1, 4)
    for j in (1, 2, 3):
        for i in (1, 2, 3):
            block = some_of((chan - j + 4) % 4, pl.ds((space // 4 - i + 4) % 4 * 7, 7), core)
            describe(block, block, x_send.at[j, i], x_recv.at[j, i], x_device(i)).wait_recv()
            remote(block, block, piece_send.at[j, i], piece_recv.at[j, i], sibling)
    landed(pooled_y)
    clear_y(pooled, (1, 2), slice(128, 256), 128)
    shift_pooled(pooled, (1, 2), 0, 1)
    shift_pooled(pooled, (1, 2), 5, 1)
    for j in (1, 2, 3):
        for i in range(4):
            block = some_of((chan - j + 4) % 4, pl.ds((space // 4 - i + 4) % 4 * 7, 7), 1 - core)
            describe(block, block, piece_send.at[j, i], piece_recv.at[j, i], sibling).wait_recv()
    deep_inner(pooled, wd, pre_deep)
    transpose_deep_weights(wd, wdt)
    landed(pooled_x)
    clear_y(pooled, (0, 3), slice(128, 256), 128)
    clear_x(pooled, slice(128, 256))
    shift_pooled(pooled, (0, 3), 0, 6)
    landed(ct_copies)
    deep_outer(pooled, wd, ct, pre_deep, act, deep_in)

    grad_copies = []
    for n, dx in enumerate((-1, 1)):
        pooled_outer(deep_in, wdt, send_x, n)
        for dy in (-1, 0, 1):
            at, count = {-1: (0, 1), 0: (1, 4), 1: (5, 1)}[dy]
            src = send_x.at[n, :, pl.ds(at * 128, count * 128)]
            dst = got_x.at[1 - n] if dy == 0 else got_xy.at[1 - n, 0 if dy > 0 else 1]
            k = SIDES.index((dx, dy))
            grad_copies.append(remote(src, dst, halo_send.at[2, k], halo_recv.at[2, k], side_device(dx, dy)))
    pooled_inner(deep_in, wdt, pooled_grad, (0, 4))
    for n, (dy, at) in enumerate(((-1, 0), (1, 5))):
        for X in range(2):
            send_y[n, X] = pooled_grad[X, :, at * 128 : (at + 1) * 128].astype(BF16)
        k = SIDES.index((0, dy))
        grad_copies.append(
            remote(send_y.at[n], got_y.at[1 - n], halo_send.at[2, k], halo_recv.at[2, k], side_device(0, dy))
        )

    def over_plane(n, src, dst):
        return [
            remote(src((rank + j) % 16), dst(j), plane_send.at[n, j], plane_recv.at[n, j], plane_device(j))
            for j in range(1, 16)
        ]

    deep_gradient(deep_in, pooled, dg)
    dg_pair_copy = pair(0, dg.at[1 - core, pl.ds(0, 28)], dg_pair)
    pooled_inner(deep_in, wdt, pooled_grad, (2,))
    landed(grad_copies)
    for at, n in ((0, 0), (15, 1)):

        @pl.when(space == at)
        def _():
            got_x[n] = jnp.zeros((128, 512), BF16)
            got_xy[n] = jnp.zeros((2, 128, 128), BF16)

    for at, n in ((0, 0), (3, 1)):

        @pl.when(chan == at)
        def _():
            got_y[n] = jnp.zeros((2, 128, 128), BF16)
            for m in range(2):
                got_xy[m, n] = jnp.zeros((128, 128), BF16)

    early_cotangent(pooled_grad, got_x, got_y, got_xy, slopes, early_in)
    landed([dg_pair_copy])

    def put_b(t, value):
        dg_b[t] = value

    def put_a(t, value):
        dg_a[:, t - 16] = value

    add_taps(16, 28, put_a, [lambda t: dg[core, t], lambda t: dg_pair[t]])
    dg_a_copies = over_chan(3, lambda c: dg_a.at[c], lambda j: dg_a_in.at[j])
    add_taps(0, 16, put_b, [lambda t: dg[core, t], lambda t: dg_pair[t]])
    dg_b_copies = over_plane(0, lambda r: dg_b.at[r], lambda j: dg_b_in.at[j])
    here = pl.ds(pl.multiple_of(chan * 4, 4), 4)
    act_copies = over_chan(
        4, lambda c: act.at[:, :, pl.ds(pl.multiple_of(c * 64, 64), 64), :], lambda j: act_in.at[here]
    )
    act_in[here] = act[:, :, mine, :]

    early_gradient(early_in, taps_in, eg, 0, 5)
    eg_pair_0 = pair(1, eg.at[1 - core, pl.ds(0, 16)], eg_pair.at[pl.ds(0, 16)])
    early_gradient(early_in, taps_in, eg, 5, 7)

    def put_eg(t, value):
        eg_sum[t] = value

    landed([eg_pair_0])
    add_taps(0, 16, put_eg, [lambda t: eg[core, t], lambda t: eg_pair[t]])
    eg_copies = [over_plane(2, lambda r: eg_sum.at[r], lambda j: eg_plane.at[0, j])]
    early_gradient(early_in, taps_in, eg, 7, 9)
    eg_pair_1 = pair(2, eg.at[1 - core, pl.ds(16, 12)], eg_pair.at[pl.ds(16, 12)])

    def put_a_sum(t, value):
        dg_a_sum[t] = value

    landed(dg_a_copies)
    add_taps(0, 12, put_a_sum, [lambda t: dg_a[chan, t]] + [lambda t, j=j: dg_a_in[j, t] for j in (1, 2, 3)])
    landed([eg_pair_1])
    add_taps(16, 28, put_eg, [lambda t: eg[core, t], lambda t: eg_pair[t]])
    eg_copies.append(over_plane(3, lambda r: eg_sum.at[16 + r], lambda j: eg_plane.at[1, j]))
    dg_a_copies = over_plane(1, lambda r: dg_a_sum.at[r], lambda j: dg_a_plane.at[j])
    landed(dg_b_copies)
    dg_b_sum[...] = total_of(dg_b[rank], [dg_b_in[j] for j in range(1, 16)])
    dg_b_copies = over_chan(6, lambda c: dg_b_sum.at[c], lambda j: dg_b_chan.at[j])

    def both(n, j, block):
        remote(block, block, both_send.at[n, j], both_recv.at[n, j], sibling)

    def gather(n):
        block = full.at[n, :, rank, half, :]
        for j in range(1, 16):
            remote(block, block, plane_send.at[4 + n, j], plane_recv.at[4 + n, j], plane_device(j))
        both(n, 0, block)

    def gathered(n):
        for j in range(1, 16):
            theirs = full.at[n, :, (rank - j + 16) % 16, half, :]
            describe(theirs, theirs, plane_send.at[4 + n, j], plane_recv.at[4 + n, j], plane_device(j)).wait_recv()
            both(n, j, theirs)

    def halves_landed(n):
        other = pl.ds(pl.multiple_of(32 - core * 32, 32), 32)
        for j in range(16):
            theirs = full.at[n, :, (rank - j + 16) % 16, other, :]
            describe(theirs, theirs, both_send.at[n, j], both_recv.at[n, j], sibling).wait_recv()

    def chan_terms(n):
        landed(eg_copies[n])
        eg_chan[chan, n] = total_of(eg_sum[16 * n + rank], [eg_plane[n, j] for j in range(1, 16)])
        over_chan((5, 2)[n], lambda c: eg_chan.at[chan, n], lambda j: eg_chan.at[chan, n])

    def chan_total(n):
        for j in (1, 2, 3):
            block = eg_chan.at[(chan - j + 4) % 4, n]
            k = (5, 2)[n]
            describe(block, block, chan_send.at[k, j], chan_recv.at[k, j], chan_device(j)).wait_recv()
        total = (eg_chan[0, n] + eg_chan[1, n]) + (eg_chan[2, n] + eg_chan[3, n])
        full[1, n, rank, half, :] = total.astype(BF16)

    chan_terms(0)
    landed(dg_b_copies)
    full[0, 0, rank, half, :] = total_of(dg_b_sum[chan], [dg_b_chan[j] for j in (1, 2, 3)]).astype(BF16)
    landed(dg_a_copies)
    full[0, 1, rank, half, :] = total_of(dg_a_sum[rank], [dg_a_plane[j] for j in range(1, 16)]).astype(BF16)
    gather(0)
    chan_terms(1)
    chan_total(0)
    chan_total(1)
    gather(1)
    gathered(0)
    gathered(1)
    halves_landed(0)
    halves_landed(1)

    landed(act_copies)
    for copy in sends:
        copy.wait_send()


def finish(act_hbm, grads_hbm, act_out, dg_out, eg_out, act_in, grads, act, wide, sem):
    loads = [
        pltpu.make_async_copy(grads_hbm.at[0], grads.at[0], sem.at[0]),
        pltpu.make_async_copy(grads_hbm.at[1], grads.at[1], sem.at[1]),
        pltpu.make_async_copy(act_hbm, act_in, sem.at[2]),
    ]
    stores = [
        pltpu.make_async_copy(wide.at[0], dg_out, sem.at[3]),
        pltpu.make_async_copy(wide.at[1], eg_out, sem.at[4]),
        pltpu.make_async_copy(act, act_out, sem.at[5]),
    ]
    for load in loads:
        load.start()
    for n in range(2):
        loads[n].wait()
        for t in range(27):
            wide[n, t] = grads[n, t // 15, t % 15].astype(F32)
        stores[n].start()
    loads[2].wait()
    deep_channels_first(act_in, act)
    stores[2].start()
    for store in stores:
        store.wait()


def on_device(samples, early_filters, deep_filters, deep_cotangent):
    act, grads = pl.pallas_call(
        kernel,
        out_shape=(
            jax.ShapeDtypeStruct((16, 2, 64, 128), BF16),
            jax.ShapeDtypeStruct((2, 2, 16, 64, 128), BF16),
        ),
        in_specs=[pl.BlockSpec(memory_space=pltpu.VMEM)] + [pl.BlockSpec(memory_space=pl.ANY)] * 3,
        out_specs=[pl.BlockSpec(memory_space=pltpu.VMEM)] * 2,
        scratch_shapes=[
            pltpu.VMEM((4, 8, 64, 256), BF16),
            pltpu.VMEM((27, 64, 128), BF16),
            pltpu.VMEM((64, 2, 16, 128), BF16),
            pltpu.VMEM((16, 2, 64, 128), BF16),
            pltpu.VMEM((6, 10, 64, 256), BF16),
            pltpu.VMEM((6, 256, 1280), BF16),
            pltpu.VMEM((9, 256, 256), BF16),
            pltpu.VMEM((256, 512), BF16),
            pltpu.VMEM((4, 256, 1024), F32),
            pltpu.VMEM((2, 128, 512), F32),
            pltpu.VMEM((4, 384, 768), BF16),
            pltpu.VMEM((28, 256, 128), BF16),
            pltpu.VMEM((9, 384, 256), BF16),
            pltpu.VMEM((4, 2, 256, 128), BF16),
            pltpu.VMEM((2, 256, 512), F32),
            pltpu.VMEM((4, 2, 256, 128), BF16),
            pltpu.VMEM((2, 256, 1024), BF16),
            pltpu.VMEM((2, 128, 768), F32),
            pltpu.VMEM((2, 128, 768), BF16),
            pltpu.VMEM((2, 2, 128, 128), BF16),
            pltpu.VMEM((2, 128, 512), BF16),
            pltpu.VMEM((2, 2, 128, 128), BF16),
            pltpu.VMEM((2, 2, 128, 128), BF16),
            pltpu.VMEM((4, 256, 1024), BF16),
            pltpu.VMEM((2, 28, 4, 32, 128), BF16),
            pltpu.VMEM((28, 4, 32, 128), BF16),
            pltpu.VMEM((16, 4, 32, 128), BF16),
            pltpu.VMEM((16, 4, 32, 128), BF16),
            pltpu.VMEM((4, 32, 128), F32),
            pltpu.VMEM((4, 32, 128), F32),
            pltpu.VMEM((4, 12, 32, 128), BF16),
            pltpu.VMEM((4, 12, 32, 128), BF16),
            pltpu.VMEM((16, 32, 128), BF16),
            pltpu.VMEM((16, 32, 128), BF16),
            pltpu.VMEM((2, 28, 32, 128), BF16),
            pltpu.VMEM((28, 32, 128), BF16),
            pltpu.VMEM((32, 32, 128), BF16),
            pltpu.VMEM((2, 16, 32, 128), BF16),
            pltpu.VMEM((4, 2, 32, 128), F32),
            pltpu.SemaphoreType.DMA((3, 8)),
            pltpu.SemaphoreType.DMA((3, 8)),
            pltpu.SemaphoreType.DMA((4, 4)),
            pltpu.SemaphoreType.DMA((4, 4)),
            pltpu.SemaphoreType.DMA((4, 4)),
            pltpu.SemaphoreType.DMA((4, 4)),
            pltpu.SemaphoreType.DMA((7, 4)),
            pltpu.SemaphoreType.DMA((7, 4)),
            pltpu.SemaphoreType.DMA((3,)),
            pltpu.SemaphoreType.DMA((3,)),
            pltpu.SemaphoreType.DMA((6, 16)),
            pltpu.SemaphoreType.DMA((6, 16)),
            pltpu.SemaphoreType.DMA((2, 16)),
            pltpu.SemaphoreType.DMA((2, 16)),
            pltpu.SemaphoreType.DMA((3,)),
        ],
        compiler_params=pltpu.CompilerParams(
            collective_id=0, has_side_effects=True, vmem_limit_bytes=56 * 1024 * 1024
        ),
        name="conv_step",
    )(samples[0], early_filters.transpose(0, 2, 1), deep_filters, deep_cotangent[0])
    act, deep_grad, early_grad = pl.pallas_call(
        finish,
        out_shape=(
            jax.ShapeDtypeStruct((64, 2, 16, 128), BF16),
            jax.ShapeDtypeStruct((27, 64, 128), F32),
            jax.ShapeDtypeStruct((27, 64, 128), F32),
        ),
        in_specs=[pl.BlockSpec(memory_space=pl.ANY)] * 2,
        out_specs=[pl.BlockSpec(memory_space=pl.ANY)] * 3,
        scratch_shapes=[
            pltpu.VMEM((16, 2, 64, 128), BF16),
            pltpu.VMEM((2, 2, 16, 64, 128), BF16),
            pltpu.VMEM((64, 2, 16, 128), BF16),
            pltpu.VMEM((2, 27, 64, 128), F32),
            pltpu.SemaphoreType.DMA((6,)),
        ],
        compiler_params=pltpu.CompilerParams(vmem_limit_bytes=56 * 1024 * 1024),
        name="finish",
    )(act, grads)
    return act[None], deep_grad, early_grad.transpose(0, 2, 1)


def solution(mesh):
    placed = (
        P("dp", None, "space", "chan", None),
        P(),
        P(None, "chan", None),
        P("dp", "chan", "space", None, None),
    )
    return jax.shard_map(
        on_device,
        mesh=mesh,
        in_specs=placed,
        out_specs=(P("dp", "chan", "space", None, None), P(None, "chan", None), P()),
        check_vma=False,
    )
```
